512 devices in a mesh: row: 32 (over y, z_hi, core), col: 16 (over z_lo, x).
Axes of the slice: x: 4, y: 4, z: 16 (z_hi: 4, z_lo: 4; z = z_hi * 4 + z_lo), core: 2. Of those that a mesh axis runs over, the one named last changes fastest.
Arguments:
- atoms: bfloat16 [4, 65536, 128], P(None, ('row', 'col')), may hold values from -6 to 6
- cotangent: bfloat16 [4, 65536, 128], P(None, ('row', 'col')), may hold values from -6 to 6
- project: bfloat16 [128, 512], replicated, may hold values from -0.5 to 0.5
- combine: bfloat16 [128, 128], replicated, may hold values from -0.5 to 0.5
- atom_gain: float32 [128], replicated, may hold values from 0.5 to 1.5
- pair_band: bfloat16 [8192, 48, 128], P('row', 'col'), may hold values from -6 to 6
- pair_gain: float32 [128], replicated, may hold values from 0.5 to 1.5
- pair_weight: bfloat16 [128, 4], replicated, may hold values from -1.06066017 to 1.06066017
- atom_token: int32 [65536], P(('row', 'col')), may hold values from 0 to 8191, as said below
- key_range: int32 [2048, 2], P(('row', 'col')), may hold values from 0 to 65536, as said below
Outputs:
- atoms_grad: bfloat16 [4, 65536, 128], P(None, ('row', 'col'))
- project_grad: bfloat16 [128, 512], replicated
- combine_grad: bfloat16 [128, 128], replicated
- scale_grad: float32 [128], replicated
- band_grad: bfloat16 [8192, 48, 128], P('row', 'col')
- weight_grad: bfloat16 [128, 4], replicated
- gain_grad: float32 [128], replicated
The draws below stay inside these ranges and needn't reach their ends.
Inputs may be any that keep to these rules, and one draw needn't show every extreme that they name: `atom_token`: Nondecreasing; the atoms d * 128 to (d + 1) * 128 - 1 name exactly the tokens d * 16 to (d + 1) * 16 - 1, each at least once. For window w: max(0, w * 32 - 48) <= key_range[w, 0] <= w * 32 and w * 32 + 32 <= key_range[w, 1] <= min(65536, w * 32 + 80); both outer limits are taken by some windows.
All inputs are finite; a program needn't handle non-finite values.
Results may differ from the reference program's by a relative error of at most 0.013.
The reference program's roundings to bfloat16 on the way count: a program that leaves them out, or rounds other values in their place, can miss the bound.
Values may be sent and summed in bfloat16 or wider, within the bound.
No kernel may reach another device: no remote copies, remote signals or barrier semaphores. Data moves between devices by JAX's collectives and lax.ppermute only.
A program may use at most 64 MiB of HBM per device.

```python
import math
import jax
import jax.numpy as jnp
from jax import lax

CA = 128
C = 128
H = 4
QW = 32
KW = 128
S = 4
ATOM_DEV = 128
TB = 16
HD = 128
RIM = 48
NATOM = 65536
NTOK = 8192
NWIN = 2048


def draw_pair_weight(key, part):
    key = jax.random.fold_in(key, 5)
    values = jnp.clip(jax.random.normal(key, (C, H), jnp.float32), -4.0, 4.0)
    return (values * C ** (-0.5)).astype(jnp.bfloat16)


def draw_atom_token(key, part):
    key = jax.random.fold_in(key, 7)
    blocks = NATOM // ATOM_DEV
    block_keys = jax.random.split(key, blocks)
    positions = jnp.arange(ATOM_DEV, dtype=jnp.int32)

    def one_block(block_key, block_id):
        shuffled = jax.random.permutation(block_key, ATOM_DEV - 1)
        cuts = shuffled[:TB - 1] + 1
        local = jnp.sum((cuts[None, :] <= positions[:, None]).astype(jnp.int32), axis=1)
        return block_id * TB + local
    tokens = jax.vmap(one_block)(block_keys, jnp.arange(blocks, dtype=jnp.int32))
    return tokens.reshape(NATOM).astype(jnp.int32)


def draw_key_range(key, part):
    key = jax.random.fold_in(key, 11)
    window_ids = jnp.arange(NWIN, dtype=jnp.int32)
    starts = window_ids * QW
    low_key, high_key = jax.random.split(key)
    low_cut = jax.random.randint(low_key, (NWIN,), 0, RIM + 1)
    high_cut = jax.random.randint(high_key, (NWIN,), 0, RIM + 1)
    full_span = window_ids % 4 == 1
    low_cut = jnp.where(full_span, 0, low_cut)
    high_cut = jnp.where(full_span, 0, high_cut)
    lower = jnp.maximum(starts - RIM + low_cut, 0)
    upper = jnp.minimum(starts + QW + RIM - high_cut, NATOM)
    return jnp.stack([lower, upper], axis=1).astype(jnp.int32)


def shard_levels(rng, dims, shards, least, largest):
    factor_of = 1.0
    for position, parts in shards:
        heights = jax.random.uniform(jax.random.fold_in(jax.random.fold_in(rng, 6), position), (parts,), jnp.float32, least / len(shards), largest / len(shards))
        factor_of = factor_of * jnp.repeat(jnp.exp(heights), dims[position] // parts).reshape((-1,) + (1,) * (len(dims) - 1 - position))
    return factor_of


def normal_values(own_key, shape, deviation, limit, cuts=(), kind=jnp.bfloat16):
    level = shard_levels(own_key, shape, cuts, -0.22, 0.18) if cuts else 1.0
    result = jax.random.normal(own_key, shape, jnp.float32) * deviation * level
    return jnp.minimum(jnp.maximum(result, -limit), limit).astype(kind)


def setup_inputs(seed: int = 0) -> dict:
    key_of = jax.random.split(jax.random.key(seed), 11)
    return {
        "atoms": normal_values(key_of[0], (S, NATOM, CA), 1.0, 6.0, ((1, 512),)),
        "cotangent": normal_values(key_of[1], (S, NATOM, CA), 1.0, 6.0, ((1, 512),)),
        "project": normal_values(key_of[2], (CA, 4 * HD), CA ** -0.5, 0.5),
        "combine": normal_values(key_of[3], (HD, CA), HD ** -0.5, 0.5),
        "atom_gain": jnp.clip(1.0 + 0.1 * jax.random.normal(key_of[4], (CA,), jnp.float32), 0.5, 1.5),
        "pair_band": normal_values(key_of[5], (NTOK, 3 * TB, C), 1.0, 6.0, ((0, 32), (1, 16))),
        "pair_gain": jnp.clip(1.0 + 0.1 * jax.random.normal(key_of[6], (C,), jnp.float32), 0.5, 1.5),
        "pair_weight": draw_pair_weight(jax.random.fold_in(key_of[10], 71), 0),
        "atom_token": draw_atom_token(jax.random.fold_in(key_of[10], 71), 0),
        "key_range": draw_key_range(jax.random.fold_in(key_of[10], 71), 0),
    }


EPSILON = 1e-05
NEG_FILL = -1e+30
FINEST = lax.Precision.HIGHEST

def layer_stats(values):
    mean_value = lax.optimization_barrier(jnp.mean(values, axis=-1, keepdims=True))
    centred = values - mean_value
    inv_std = lax.rsqrt(lax.optimization_barrier(jnp.mean(centred * centred, axis=-1, keepdims=True)) + EPSILON)
    return (centred * inv_std, inv_std)

def layer_back(grad_hat, normal, inv_std):
    first_mean = lax.optimization_barrier(jnp.mean(grad_hat, axis=-1, keepdims=True))
    second_mean = lax.optimization_barrier(jnp.mean(grad_hat * normal, axis=-1, keepdims=True))
    return inv_std * (grad_hat - first_mean - normal * second_mean)

def one_hot(indices, columns):
    return (indices[:, None] == jnp.arange(columns, dtype=jnp.int32)[None, :]).astype(jnp.float32)

def key_windows(padded, windows):
    span_count = KW // QW
    blocked = padded.reshape(padded.shape[0], windows + span_count - 1, QW, padded.shape[-1])
    return jnp.concatenate([blocked[:, offset:offset + windows] for offset in range(span_count)], axis=2)

def from_windows(grad_win, windows):
    span_count = KW // QW
    lead = grad_win.shape[0]
    pieces = grad_win.reshape(lead, windows, span_count, QW, grad_win.shape[-1])
    summed = jnp.zeros((lead, windows + span_count - 1, QW, grad_win.shape[-1]), jnp.float32)
    for offset in range(span_count):
        summed = summed.at[:, offset:offset + windows].add(pieces[:, :, offset])
    return summed.reshape(lead, (windows + span_count - 1) * QW, grad_win.shape[-1])

def window_bias(table, query_hot, key_hot, windows):
    query_sel = query_hot.reshape(windows, QW, query_hot.shape[-1])
    key_sel = key_windows(key_hot[None], windows)[0]
    row_terms = jnp.einsum('wit,htu->whiu', query_sel, table, precision=FINEST)
    return (jnp.einsum('whiu,wju->whij', row_terms, key_sel, precision=FINEST), query_sel, key_sel)

def table_back(bias_grad, query_sel, key_sel):
    col_terms = jnp.einsum('whij,wju->whiu', bias_grad, key_sel, precision=FINEST)
    return jnp.einsum('wit,whiu->htu', query_sel, col_terms, precision=FINEST)

def window_mask(ranges, first_atom, windows):
    key_pos = first_atom - RIM + QW * jnp.arange(windows, dtype=jnp.int32)[:, None] + jnp.arange(KW, dtype=jnp.int32)[None, :]
    return (key_pos >= ranges[:, 0:1]) & (key_pos < ranges[:, 1:2])

def pair_front(tiles, pair_gain, pair_weight):
    z_hat, inv_std = layer_stats(tiles.astype(jnp.float32))
    pair_norm = (z_hat * pair_gain).astype(jnp.bfloat16)
    bias_rows = jnp.dot(pair_norm.reshape(-1, tiles.shape[-1]), pair_weight, preferred_element_type=jnp.float32)
    table = jnp.transpose(bias_rows.reshape(tiles.shape[0], tiles.shape[1], pair_weight.shape[1]), (2, 0, 1))
    return (table, pair_norm, z_hat, inv_std)

def pair_back(pair_norm, z_hat, inv_std, grad_rows, pair_gain, pair_weight):
    channels = pair_norm.shape[-1]
    weight_part = jnp.dot(pair_norm.reshape(-1, channels).T, grad_rows, preferred_element_type=jnp.float32)
    norm_grad = jnp.dot(grad_rows, pair_weight.T, preferred_element_type=jnp.float32).astype(jnp.bfloat16)
    norm_wide = norm_grad.astype(jnp.float32).reshape(z_hat.shape)
    gain_part = lax.optimization_barrier(jnp.sum(norm_wide * z_hat, axis=(0, 1)))
    band_part = layer_back(norm_wide * pair_gain, z_hat, inv_std).astype(jnp.bfloat16)
    return (band_part, weight_part, gain_part)

def attend(query, gate, padded_kv, bias, allowed, cotangent, combine):
    samples, atom_count, inner_width = query.shape
    head_count = bias.shape[1]
    head_dim = inner_width // head_count
    windows = atom_count // QW
    score_scale = 1.0 / math.sqrt(head_dim)
    kv_win = key_windows(padded_kv, windows).astype(jnp.float32)
    key_win = kv_win[..., :inner_width].reshape(samples, windows, KW, head_count, head_dim)
    value_win = kv_win[..., inner_width:].reshape(samples, windows, KW, head_count, head_dim)
    query_win = query.astype(jnp.float32).reshape(samples, windows, QW, head_count, head_dim)
    scores = jnp.einsum('swihd,swjhd->swhij', query_win, key_win, precision=FINEST) * score_scale + bias[None]
    scores = jnp.where(allowed[None, :, None, None, :], scores, NEG_FILL)
    exp_scores = jnp.exp(scores - lax.optimization_barrier(jnp.max(scores, axis=-1, keepdims=True)))
    weights = exp_scores / lax.optimization_barrier(jnp.sum(exp_scores, axis=-1, keepdims=True))
    weights_low = lax.optimization_barrier(weights.astype(jnp.bfloat16)).astype(jnp.float32)
    mixture = jnp.einsum('swhij,swjhd->swihd', weights_low, value_win, precision=FINEST).reshape(samples, atom_count, inner_width)
    sigmoid = jax.nn.sigmoid(gate.astype(jnp.float32))
    gated_out = (mixture * sigmoid).astype(jnp.bfloat16)
    out_rows = cotangent.reshape(-1, cotangent.shape[-1])
    gated_grad = jnp.dot(out_rows, combine.T, preferred_element_type=jnp.float32).astype(jnp.bfloat16)
    combine_part = jnp.dot(gated_out.reshape(-1, inner_width).T, out_rows, preferred_element_type=jnp.float32)
    gated_wide = gated_grad.astype(jnp.float32).reshape(samples, atom_count, inner_width)
    mixture_grad = (gated_wide * sigmoid).astype(jnp.bfloat16)
    gate_grad = (gated_wide * mixture * sigmoid * (1.0 - sigmoid)).astype(jnp.bfloat16)
    mixture_win = mixture_grad.astype(jnp.float32).reshape(samples, windows, QW, head_count, head_dim)
    weights_grad = jnp.einsum('swihd,swjhd->swhij', mixture_win, value_win, precision=FINEST)
    weights_grad = lax.optimization_barrier(weights_grad.astype(jnp.bfloat16)).astype(jnp.float32)
    value_grad = jnp.einsum('swhij,swihd->swjhd', weights_low, mixture_win, precision=FINEST)
    row_dot = lax.optimization_barrier(jnp.sum(weights * weights_grad, axis=-1, keepdims=True))
    score_grad = weights * (weights_grad - row_dot)
    bias_grad = lax.optimization_barrier(jnp.sum(score_grad, axis=0))
    score_low = lax.optimization_barrier((score_grad * score_scale).astype(jnp.bfloat16)).astype(jnp.float32)
    query_grad = jnp.einsum('swhij,swjhd->swihd', score_low, key_win, precision=FINEST).reshape(samples, atom_count, inner_width).astype(jnp.bfloat16)
    key_grad = jnp.einsum('swhij,swihd->swjhd', score_low, query_win, precision=FINEST)
    kv_grad = jnp.concatenate([key_grad.reshape(samples, windows, KW, inner_width), value_grad.reshape(samples, windows, KW, inner_width)], axis=-1)
    return (query_grad, gate_grad, from_windows(kv_grad, windows), bias_grad, combine_part)

def reference(atoms, cotangent, project, combine, atom_gain, pair_band, pair_gain, pair_weight, atom_token, key_range):
    samples, atom_total, channels = atoms.shape
    blocks = atom_total // ATOM_DEV
    inner_width = combine.shape[0]
    head_count = pair_weight.shape[1]
    band_width = pair_band.shape[1]
    windows = ATOM_DEV // QW
    extent = ATOM_DEV + 2 * RIM
    band_blocks = pair_band.reshape(blocks, TB, band_width, pair_band.shape[2])

    def table_of(tiles):
        return pair_front(tiles, pair_gain, pair_weight)[0]
    tables = lax.map(table_of, band_blocks)
    atoms_pad = jnp.pad(atoms, ((0, 0), (RIM, RIM), (0, 0)))
    tokens_pad = jnp.pad(atom_token, (RIM, RIM))
    out_blocks = jnp.transpose(cotangent.reshape(samples, blocks, ATOM_DEV, channels), (1, 0, 2, 3))
    range_blocks = key_range.reshape(blocks, windows, 2)
    block_ids = jnp.arange(blocks, dtype=jnp.int32)

    def first_pass(packed):
        block_id, table, out_block, ranges = packed
        first_atom = block_id * ATOM_DEV
        extended = lax.dynamic_slice_in_dim(atoms_pad, first_atom, extent, 1)
        tokens_ext = lax.dynamic_slice_in_dim(tokens_pad, first_atom, extent, 0)
        x_hat, inv_std = layer_stats(extended.astype(jnp.float32))
        normed = (x_hat * atom_gain).astype(jnp.bfloat16)
        projected = jnp.dot(normed.reshape(-1, channels), project, preferred_element_type=jnp.float32).astype(jnp.bfloat16).reshape(samples, extent, 4 * inner_width)
        query = projected[:, RIM:RIM + ATOM_DEV, :inner_width]
        gate = projected[:, RIM:RIM + ATOM_DEV, 3 * inner_width:]
        padded_kv = projected[:, :, inner_width:3 * inner_width]
        token_base = block_id * TB
        query_hot = one_hot(tokens_ext[RIM:RIM + ATOM_DEV] - token_base, TB)
        key_hot = one_hot(tokens_ext - token_base + TB, band_width)
        bias, query_sel, key_sel = window_bias(table, query_hot, key_hot, windows)
        allowed = window_mask(ranges, first_atom, windows)
        query_grad, gate_grad, pad_grad, bias_grad, combine_part = attend(query, gate, padded_kv, bias, allowed, out_block, combine)
        table_grad = table_back(bias_grad, query_sel, key_sel).astype(jnp.bfloat16)
        return (query_grad, gate_grad, pad_grad, table_grad, combine_part)
    query_grads, gate_grads, pad_grads, table_grads, combine_parts = lax.map(first_pass, (block_ids, tables, out_blocks, range_blocks))
    atom_blocks = jnp.transpose(atoms.reshape(samples, blocks, ATOM_DEV, channels), (1, 0, 2, 3))

    def second_pass(packed):
        block_id, atom_block, out_block, query_grad, gate_grad = packed
        own_part = lax.dynamic_index_in_dim(pad_grads, block_id, 0, keepdims=False)
        before = lax.dynamic_index_in_dim(pad_grads, jnp.maximum(block_id - 1, 0), 0, keepdims=False)
        after = lax.dynamic_index_in_dim(pad_grads, jnp.minimum(block_id + 1, blocks - 1), 0, keepdims=False)
        left_low = lax.optimization_barrier(before[:, RIM + ATOM_DEV:].astype(jnp.bfloat16)).astype(jnp.float32)
        right_low = lax.optimization_barrier(after[:, :RIM].astype(jnp.bfloat16)).astype(jnp.float32)
        from_left = left_low * (block_id > 0).astype(jnp.float32)
        from_right = right_low * (block_id < blocks - 1).astype(jnp.float32)
        kv_total = own_part[:, RIM:RIM + ATOM_DEV] + jnp.pad(from_left, ((0, 0), (0, ATOM_DEV - RIM), (0, 0))) + jnp.pad(from_right, ((0, 0), (ATOM_DEV - RIM, 0), (0, 0)))
        x_hat, inv_std = layer_stats(atom_block.astype(jnp.float32))
        normed = (x_hat * atom_gain).astype(jnp.bfloat16)
        flat_normed = normed.reshape(-1, channels)
        projected_grad = jnp.concatenate([query_grad, kv_total.astype(jnp.bfloat16), gate_grad], axis=-1).reshape(-1, 4 * inner_width)
        project_part = jnp.dot(flat_normed.T, projected_grad, preferred_element_type=jnp.float32)
        normed_grad = jnp.dot(projected_grad, project.T, preferred_element_type=jnp.float32).astype(jnp.bfloat16)
        normed_wide = normed_grad.astype(jnp.float32).reshape(samples, ATOM_DEV, channels)
        scale_part = lax.optimization_barrier(jnp.sum(normed_wide * x_hat, axis=(0, 1)))
        atoms_grad = (out_block.astype(jnp.float32) + layer_back(normed_wide * atom_gain, x_hat, inv_std)).astype(jnp.bfloat16)
        return (atoms_grad, project_part, scale_part)
    atom_grads, project_parts, scale_parts = lax.map(second_pass, (block_ids, atom_blocks, out_blocks, query_grads, gate_grads))
    atoms_grad = jnp.transpose(atom_grads, (1, 0, 2, 3)).reshape(samples, atom_total, channels)

    def pair_pass(packed):
        tiles, table_grad = packed
        table_unused, pair_norm, z_hat, pair_std = pair_front(tiles, pair_gain, pair_weight)
        grad_rows = jnp.transpose(table_grad, (1, 2, 0)).reshape(-1, head_count)
        return pair_back(pair_norm, z_hat, pair_std, grad_rows, pair_gain, pair_weight)
    band_parts, weight_parts, gain_parts = lax.map(pair_pass, (band_blocks, table_grads))
    return (atoms_grad, lax.optimization_barrier(jnp.sum(project_parts, axis=0)).astype(jnp.bfloat16), lax.optimization_barrier(jnp.sum(combine_parts, axis=0)).astype(jnp.bfloat16), lax.optimization_barrier(jnp.sum(scale_parts, axis=0)), band_parts.reshape(pair_band.shape), lax.optimization_barrier(jnp.sum(weight_parts, axis=0)).astype(jnp.bfloat16), lax.optimization_barrier(jnp.sum(gain_parts, axis=0)))
```

```python
import math

import jax
import jax.numpy as jnp
from jax import lax
from jax.experimental import pallas as pl
from jax.experimental.pallas import tpu as pltpu
from jax.sharding import PartitionSpec as P

QW = 32
KW = 128
RIM = 48
EPSILON = 1e-05
NEG_FILL = -1e30
F32 = jnp.float32
BF = jnp.bfloat16


def nn(a, b):
    return lax.dot_general(a, b, (((1,), (0,)), ((), ())), preferred_element_type=F32)


def nt(a, b):
    return lax.dot_general(a, b, (((1,), (1,)), ((), ())), preferred_element_type=F32)


def tn(a, b):
    return lax.dot_general(a, b, (((0,), (0,)), ((), ())), preferred_element_type=F32)


def split2(x):
    high = x.astype(BF)
    return high, (x - high.astype(F32)).astype(BF)


def norm(v):
    mean = jnp.mean(v, axis=-1, keepdims=True)
    centred = v - mean
    inv = lax.rsqrt(jnp.mean(centred * centred, axis=-1, keepdims=True) + EPSILON)
    return centred * inv, inv


def norm_back(g, hat, inv):
    first = jnp.mean(g, axis=-1, keepdims=True)
    second = jnp.mean(g * hat, axis=-1, keepdims=True)
    return inv * (g - first - hat * second)


def iota(shape, dim):
    return lax.broadcasted_iota(jnp.int32, shape, dim)


def attention_kernel(
    ranges,
    atoms,
    cotangent,
    before,
    after,
    project,
    combine,
    atom_gain,
    band,
    pair_gain,
    weight_rows,
    query_tokens,
    key_tokens,
    grads,
    to_before,
    to_after,
    own_grad,
    local_band,
    bias,
    bias_grad,
    kv_grad,
    z_hat,
):
    samples, count, width = atoms.shape
    heads = 4
    windows = count // QW
    entries = band.shape[0]
    slots = entries // 16
    extent = count + 2 * RIM
    scale = 1.0 / math.sqrt(width // heads)
    gain = atom_gain[...]

    hat, pair_inv = norm(band[...].astype(F32))
    z_hat[...] = hat
    pair_norm = (hat * pair_gain[...]).astype(BF)
    bias_rows = nt(weight_rows[...], pair_norm)
    stacked = jnp.concatenate(
        [jnp.broadcast_to(bias_rows[h : h + 1], (16, entries)) for h in range(heads)], axis=0
    )
    own_token = (iota((64, entries), 0) & 15) == (iota((64, entries), 1) & 15)
    high, low = split2(jnp.where(own_token, stacked, 0.0))
    spread = (iota((entries, KW), 0) >> 4) == iota((entries, KW), 1)
    spread = jnp.where(spread, 1.0, 0.0).astype(BF)
    table = nn(jnp.concatenate([high, low], axis=0), spread).astype(BF)
    lane = iota((KW, KW), 1)
    line = iota((KW, KW), 0)

    def query_hot(w):
        tokens = query_tokens[w * QW : (w + 1) * QW, :]
        tokens = jnp.concatenate([tokens] * heads, axis=0)
        hit = (tokens == (lane & 15)) & ((line >> 5) == ((lane >> 4) & 3))
        return jnp.where(hit, 1.0, 0.0).astype(BF)

    def key_hot(w):
        return jnp.where(line == key_tokens[w : w + 1, :], 1.0, 0.0).astype(BF)

    for w in range(windows):
        by_key = nn(table, key_hot(w)).astype(BF)
        values = nn(query_hot(w), by_key)
        allowed = (lane >= ranges[w, 0]) & (lane < ranges[w, 1])
        bias[w] = jnp.where(allowed, values, NEG_FILL)
        bias_grad[w] = jnp.zeros((KW, KW), F32)
    grads[...] = jnp.zeros_like(grads)
    same_head = (line >> 5) == (lane >> 5)
    diag = jnp.where(same_head, 1.0, 0.0).astype(BF)
    head_of = iota((QW, width), 1) >> 5

    def spread_heads(x):
        return jnp.concatenate([x] * heads, axis=0) * diag

    def gather_heads(x):
        total = jnp.where(head_of == 0, x[:QW], 0.0)
        for h in range(1, heads):
            total = total + jnp.where(head_of == h, x[h * QW : (h + 1) * QW], 0.0)
        return total

    def sample(s, carry):
        project_sum, combine_sum, scale_sum = carry
        x = jnp.concatenate([before[s], atoms[s], after[s]], axis=0).astype(F32)
        x_hat, _ = norm(x)
        normed = (x_hat * gain).astype(BF)
        projected = nn(normed, project[...]).astype(BF)
        query = projected[RIM : RIM + count, :width]
        key = projected[:, width : 2 * width]
        value = projected[:, 2 * width : 3 * width]
        gate = projected[RIM : RIM + count, 3 * width :].astype(F32)
        out = cotangent[s]
        sigmoid = jax.nn.sigmoid(gate)
        gated_grad = nt(out, combine[...]).astype(BF).astype(F32)
        mixture_grad = (gated_grad * sigmoid).astype(BF)
        kv_grad[...] = jnp.zeros_like(kv_grad)
        mixtures = []
        query_grads = []
        for w in range(windows):
            own = slice(w * QW, (w + 1) * QW)
            near = slice(w * QW, w * QW + KW)
            q = spread_heads(query[own])
            k = key[near]
            v = value[near]
            scores = nt(q, k) * scale + bias[w]
            scores = jnp.exp(scores - jnp.max(scores, axis=-1, keepdims=True))
            weights = scores * (1.0 / jnp.sum(scores, axis=-1, keepdims=True))
            weights_low = weights.astype(BF)
            mixtures.append(gather_heads(nn(weights_low, v)))
            mg = spread_heads(mixture_grad[own])
            weights_grad = nt(mg, v).astype(BF).astype(F32)
            row_dot = jnp.sum(weights * weights_grad, axis=-1, keepdims=True)
            score_grad = weights * (weights_grad - row_dot)
            bias_grad[w] += score_grad
            score_low = (score_grad * scale).astype(BF)
            query_grads.append(gather_heads(nn(score_low, k)).astype(BF))
            kv_grad[near, :width] += tn(score_low, q)
            kv_grad[near, width:] += tn(weights_low, mg)
        mixture = jnp.concatenate(mixtures, axis=0)
        gated = (mixture * sigmoid).astype(BF)
        combine_sum = combine_sum + tn(gated, out)
        gate_grad = (gated_grad * mixture * sigmoid * (1.0 - sigmoid)).astype(BF)
        rim = jnp.zeros((RIM, width), BF)
        query_cols = jnp.concatenate([rim] + query_grads + [rim], axis=0)
        gate_cols = jnp.concatenate([rim, gate_grad, rim], axis=0)
        grad = jnp.concatenate([query_cols, kv_grad[...].astype(BF), gate_cols], axis=1)
        project_sum = project_sum + tn(normed, grad)
        normed_grad = nt(grad, project[...])
        scale_sum = scale_sum + jnp.sum(normed_grad * x_hat, axis=0, keepdims=True)
        to_before[s] = normed_grad[:RIM].astype(BF)
        to_after[s] = normed_grad[RIM + count :].astype(BF)
        own_grad[s] = normed_grad[RIM : RIM + count]
        return project_sum, combine_sum, scale_sum

    start = (
        jnp.zeros((width, 4 * width), F32),
        jnp.zeros((width, width), F32),
        jnp.zeros((1, width), F32),
    )
    project_sum, combine_sum, scale_sum = lax.fori_loop(0, samples, sample, start)
    for part in range(4):
        grads[part * width : (part + 1) * width, :] = project_sum[
            :, part * width : (part + 1) * width
        ].astype(BF)
    grads[4 * width : 5 * width, :] = combine_sum.astype(BF)

    table_grad = jnp.zeros((64, KW), F32)
    for w in range(windows):
        hot = key_hot(w)
        high, low = split2(bias_grad[w])
        by_slot = nt(high, hot) + nt(low, hot)
        high, low = split2(by_slot)
        rows = query_hot(w)
        table_grad = table_grad + (tn(rows, high) + tn(rows, low))[:64]
    table_grad = table_grad.astype(BF)
    entry_grad = jnp.where(own_token, nt(table_grad, spread), 0.0).astype(BF)
    weight_of = jnp.concatenate(
        [jnp.broadcast_to(weight_rows[h : h + 1, :], (16, width)) for h in range(heads)], axis=0
    )
    hat = z_hat[...]
    pair_norm = (hat * pair_gain[...]).astype(BF)
    norm_grad = tn(entry_grad, weight_of).astype(BF).astype(F32)
    weight_part = nn(entry_grad, pair_norm)
    tail = [
        jnp.sum(weight_part[h * 16 : (h + 1) * 16], axis=0, keepdims=True) for h in range(heads)
    ]
    tail = tail + [scale_sum, jnp.sum(norm_grad * hat, axis=0, keepdims=True)]
    tail = tail + [jnp.zeros((10, width), F32)]
    grads[5 * width : 5 * width + 16, :] = jnp.concatenate(tail, axis=0).astype(BF)
    local_band[...] = norm_back(norm_grad * pair_gain[...], hat, pair_inv).astype(BF)


def finish_kernel(atoms, cotangent, own_grad, from_before, from_after, atom_gain, result):
    samples, count, width = atoms.shape
    gain = atom_gain[...]
    for s in range(samples):
        x_hat, inv = norm(atoms[s].astype(F32))
        rim = jnp.zeros((count - RIM, width), F32)
        total = own_grad[s] + jnp.concatenate([from_before[s].astype(F32), rim], axis=0)
        total = total + jnp.concatenate([rim, from_after[s].astype(F32)], axis=0)
        g = total.astype(BF).astype(F32) * gain
        result[s] = (cotangent[s].astype(F32) + norm_back(g, x_hat, inv)).astype(BF)


def vmem(n):
    return [pl.BlockSpec(memory_space=pltpu.VMEM)] * n


def shards(
    atoms,
    cotangent,
    project,
    combine,
    atom_gain,
    pair_band,
    pair_gain,
    pair_weight,
    atom_token,
    key_range,
):
    samples, count, width = atoms.shape
    heads = pair_weight.shape[1]
    rows, cols = lax.axis_size("row"), lax.axis_size("col")
    peers = rows * cols
    device = lax.axis_index(("row", "col"))
    windows = count // QW
    block = pair_band.shape[0] // cols
    keys = pair_band.shape[1]
    up = [(i, i + 1) for i in range(peers - 1)]
    down = [(i + 1, i) for i in range(peers - 1)]

    tiles = jnp.transpose(pair_band.reshape(cols, block, keys, width), (0, 2, 1, 3))
    tiles = lax.all_to_all(tiles, "col", 0, 0, tiled=True).reshape(cols * keys * block, width)

    local = atom_token - device * block

    def packed(part, tokens):
        line = jnp.pad(tokens.astype(BF), (0, width - RIM))
        return jnp.concatenate([part, jnp.broadcast_to(line, (1, RIM, width))], axis=0)

    before = lax.ppermute(packed(atoms[:, count - RIM :], local[count - RIM :]), ("row", "col"), up)
    after = lax.ppermute(packed(atoms[:, :RIM], local[:RIM]), ("row", "col"), down)
    extended = jnp.concatenate(
        [
            before[samples, 0, :RIM].astype(jnp.int32),
            local + block,
            after[samples, 0, :RIM].astype(jnp.int32) + 2 * block,
        ]
    )
    key_tokens = jnp.stack([extended[w * QW : w * QW + KW] for w in range(windows)])
    key_tokens = jnp.pad(key_tokens, ((0, 8 - windows), (0, 0)))
    query_tokens = jnp.broadcast_to(local[:, None], (count, KW))
    first_slot = device * count - RIM + QW * jnp.arange(windows, dtype=jnp.int32)
    ranges = key_range - first_slot[:, None]
    weight_rows = jnp.pad(pair_weight.T, ((0, 16 - heads), (0, 0)))
    gain = atom_gain.reshape(1, width)
    entries = tiles.shape[0]
    shape = jax.ShapeDtypeStruct
    grads, to_before, to_after, own_grad, local_band = pl.pallas_call(
        attention_kernel,
        out_shape=(
            shape((768, width), BF),
            shape((samples, RIM, width), BF),
            shape((samples, RIM, width), BF),
            shape((samples, count, width), F32),
            shape((entries, width), BF),
        ),
        in_specs=[pl.BlockSpec(memory_space=pltpu.SMEM)] + vmem(12),
        out_specs=tuple(vmem(5)),
        scratch_shapes=[
            pltpu.VMEM((windows, KW, KW), F32),
            pltpu.VMEM((windows, KW, KW), F32),
            pltpu.VMEM((count + 2 * RIM, 2 * width), F32),
            pltpu.VMEM((entries, width), F32),
        ],
        compiler_params=pltpu.CompilerParams(vmem_limit_bytes=32 * 1024 * 1024),
        name="attention",
    )(
        ranges,
        atoms,
        cotangent,
        before,
        after,
        project,
        combine,
        gain,
        tiles,
        pair_gain.reshape(1, width),
        weight_rows,
        query_tokens,
        key_tokens,
    )

    from_before = lax.ppermute(to_after, ("row", "col"), up)
    from_after = lax.ppermute(to_before, ("row", "col"), down)

    chunk = grads.shape[0] // cols
    pair = lax.ppermute(grads, "row", [(i, i ^ 1) for i in range(rows)])
    summed = (grads.astype(F32) + pair.astype(F32)).astype(BF).reshape(cols, chunk, width)
    part = lax.all_to_all(summed, "col", 0, 0, tiled=True)
    part = jnp.sum(part.astype(F32), axis=0).astype(BF)
    groups = [list(range(first, rows, 2)) for first in range(2)]
    part = jnp.broadcast_to(part, (rows // 2, chunk, width))
    part = lax.all_to_all(part, "row", 0, 0, axis_index_groups=groups, tiled=True)
    part = jnp.sum(part.astype(F32), axis=0).astype(BF)
    part = jnp.broadcast_to(part, (cols, chunk, width))
    total = lax.all_to_all(part, "col", 0, 0, tiled=True).reshape(cols * chunk, width)

    band_grad = local_band.reshape(cols, keys, block, width)
    band_grad = lax.all_to_all(band_grad, "col", 0, 0, tiled=True)
    band_grad = jnp.transpose(band_grad, (0, 2, 1, 3)).reshape(pair_band.shape)

    atoms_grad = pl.pallas_call(
        finish_kernel,
        out_shape=shape(atoms.shape, BF),
        in_specs=vmem(6),
        out_specs=pl.BlockSpec(memory_space=pltpu.VMEM),
        name="finish",
    )(atoms, cotangent, own_grad, from_before, from_after, gain)

    project_grad = jnp.transpose(total[: 4 * width].reshape(4, width, width), (1, 0, 2))
    tail = total[5 * width :]
    return (
        atoms_grad,
        project_grad.reshape(width, 4 * width),
        total[4 * width : 5 * width],
        tail[heads].astype(F32),
        band_grad,
        tail[:heads].T,
        tail[heads + 1].astype(F32),
    )


def solution(mesh):
    in_specs = (
        P(None, ("row", "col"), None),
        P(None, ("row", "col"), None),
        P(),
        P(),
        P(),
        P("row", "col", None),
        P(),
        P(),
        P(("row", "col")),
        P(("row", "col"), None),
    )
    out_specs = (P(None, ("row", "col"), None), P(), P(), P(), P("row", "col", None), P(), P())
    return jax.shard_map(shards, mesh=mesh, in_specs=in_specs, out_specs=out_specs, check_vma=False)
```

```python
import math

import jax
import jax.numpy as jnp
from jax import lax
from jax.experimental import pallas as pl
from jax.experimental.pallas import tpu as pltpu
from jax.sharding import PartitionSpec as P

QW = 32
KW = 128
RIM = 48
EPSILON = 1e-05
NEG_FILL = -1e30
F32 = jnp.float32
BF = jnp.bfloat16


def nn(a, b):
    return lax.dot_general(a, b, (((1,), (0,)), ((), ())), preferred_element_type=F32)


def nt(a, b):
    return lax.dot_general(a, b, (((1,), (1,)), ((), ())), preferred_element_type=F32)


def tn(a, b):
    return lax.dot_general(a, b, (((0,), (0,)), ((), ())), preferred_element_type=F32)


def split2(x):
    high = x.astype(BF)
    return high, (x - high.astype(F32)).astype(BF)


def norm(v):
    mean = jnp.mean(v, axis=-1, keepdims=True)
    centred = v - mean
    inv = lax.rsqrt(jnp.mean(centred * centred, axis=-1, keepdims=True) + EPSILON)
    return centred * inv, inv


def norm_back(g, hat, inv):
    first = jnp.mean(g, axis=-1, keepdims=True)
    second = jnp.mean(g * hat, axis=-1, keepdims=True)
    return inv * (g - first - hat * second)


def iota(shape, dim):
    return lax.broadcasted_iota(jnp.int32, shape, dim)


def attention_kernel(
    ranges,
    atoms,
    cotangent,
    before,
    after,
    project,
    combine,
    atom_gain,
    band,
    pair_gain,
    weight_rows,
    query_tokens,
    key_tokens,
    grads,
    to_before,
    to_after,
    own_grad,
    outgoing,
    bias,
    bias_grad,
    kv_grad,
    z_hat,
):
    samples, count, width = atoms.shape
    heads = 4
    windows = count // QW
    entries = band.shape[0]
    slots = entries // 16
    extent = count + 2 * RIM
    scale = 1.0 / math.sqrt(width // heads)
    gain = atom_gain[...]

    hat, pair_inv = norm(band[...].astype(F32))
    z_hat[...] = hat
    pair_norm = (hat * pair_gain[...]).astype(BF)
    bias_rows = nt(weight_rows[...], pair_norm)
    stacked = jnp.concatenate(
        [jnp.broadcast_to(bias_rows[h : h + 1], (16, entries)) for h in range(heads)], axis=0
    )
    own_token = (iota((64, entries), 0) & 15) == (iota((64, entries), 1) & 15)
    high, low = split2(jnp.where(own_token, stacked, 0.0))
    spread = (iota((entries, KW), 0) >> 4) == iota((entries, KW), 1)
    spread = jnp.where(spread, 1.0, 0.0).astype(BF)
    table = nn(jnp.concatenate([high, low], axis=0), spread).astype(BF)
    lane = iota((KW, KW), 1)
    line = iota((KW, KW), 0)

    def query_hot(w):
        tokens = query_tokens[w * QW : (w + 1) * QW, :]
        tokens = jnp.concatenate([tokens] * heads, axis=0)
        hit = (tokens == (lane & 15)) & ((line >> 5) == ((lane >> 4) & 3))
        return jnp.where(hit, 1.0, 0.0).astype(BF)

    def key_hot(w):
        return jnp.where(line == key_tokens[w : w + 1, :], 1.0, 0.0).astype(BF)

    for w in range(windows):
        by_key = nn(table, key_hot(w)).astype(BF)
        values = nn(query_hot(w), by_key)
        allowed = (lane >= ranges[w, 0]) & (lane < ranges[w, 1])
        bias[w] = jnp.where(allowed, values, NEG_FILL)
        bias_grad[w] = jnp.zeros((KW, KW), F32)
    grads[...] = jnp.zeros_like(grads)
    same_head = (line >> 5) == (lane >> 5)
    diag = jnp.where(same_head, 1.0, 0.0).astype(BF)
    head_of = iota((QW, width), 1) >> 5

    def spread_heads(x):
        return jnp.concatenate([x] * heads, axis=0) * diag

    def gather_heads(x):
        total = jnp.where(head_of == 0, x[:QW], 0.0)
        for h in range(1, heads):
            total = total + jnp.where(head_of == h, x[h * QW : (h + 1) * QW], 0.0)
        return total

    def sample(s, carry):
        project_sum, combine_sum, scale_sum = carry
        x = jnp.concatenate([before[s], atoms[s], after[s]], axis=0).astype(F32)
        x_hat, _ = norm(x)
        normed = (x_hat * gain).astype(BF)
        projected = nn(normed, project[...]).astype(BF)
        query = projected[RIM : RIM + count, :width]
        key = projected[:, width : 2 * width]
        value = projected[:, 2 * width : 3 * width]
        gate = projected[RIM : RIM + count, 3 * width :].astype(F32)
        out = cotangent[s]
        sigmoid = jax.nn.sigmoid(gate)
        gated_grad = nt(out, combine[...]).astype(BF).astype(F32)
        mixture_grad = (gated_grad * sigmoid).astype(BF)
        kv_grad[...] = jnp.zeros_like(kv_grad)
        mixtures = []
        query_grads = []
        for w in range(windows):
            own = slice(w * QW, (w + 1) * QW)
            near = slice(w * QW, w * QW + KW)
            q = spread_heads(query[own])
            k = key[near]
            v = value[near]
            scores = nt(q, k) * scale + bias[w]
            scores = jnp.exp(scores - jnp.max(scores, axis=-1, keepdims=True))
            weights = scores * (1.0 / jnp.sum(scores, axis=-1, keepdims=True))
            weights_low = weights.astype(BF)
            mixtures.append(gather_heads(nn(weights_low, v)))
            mg = spread_heads(mixture_grad[own])
            weights_grad = nt(mg, v).astype(BF).astype(F32)
            row_dot = jnp.sum(weights * weights_grad, axis=-1, keepdims=True)
            score_grad = weights * (weights_grad - row_dot)
            bias_grad[w] += score_grad
            score_low = (score_grad * scale).astype(BF)
            query_grads.append(gather_heads(nn(score_low, k)).astype(BF))
            kv_grad[near, :width] += tn(score_low, q)
            kv_grad[near, width:] += tn(weights_low, mg)
        mixture = jnp.concatenate(mixtures, axis=0)
        gated = (mixture * sigmoid).astype(BF)
        combine_sum = combine_sum + tn(gated, out)
        gate_grad = (gated_grad * mixture * sigmoid * (1.0 - sigmoid)).astype(BF)
        rim = jnp.zeros((RIM, width), BF)
        query_cols = jnp.concatenate([rim] + query_grads + [rim], axis=0)
        gate_cols = jnp.concatenate([rim, gate_grad, rim], axis=0)
        grad = jnp.concatenate([query_cols, kv_grad[...].astype(BF), gate_cols], axis=1)
        project_sum = project_sum + tn(normed, grad)
        normed_grad = nt(grad, project[...])
        scale_sum = scale_sum + jnp.sum(normed_grad * x_hat, axis=0, keepdims=True)
        to_before[s] = normed_grad[:RIM].astype(BF)
        to_after[s] = normed_grad[RIM + count :].astype(BF)
        own_grad[s] = normed_grad[RIM : RIM + count]
        return project_sum, combine_sum, scale_sum

    start = (
        jnp.zeros((width, 4 * width), F32),
        jnp.zeros((width, width), F32),
        jnp.zeros((1, width), F32),
    )
    project_sum, combine_sum, scale_sum = lax.fori_loop(0, samples, sample, start)
    for part in range(4):
        grads[part * width : (part + 1) * width, :] = project_sum[
            :, part * width : (part + 1) * width
        ].astype(BF)
    grads[4 * width : 5 * width, :] = combine_sum.astype(BF)

    table_grad = jnp.zeros((64, KW), F32)
    for w in range(windows):
        hot = key_hot(w)
        high, low = split2(bias_grad[w])
        by_slot = nt(high, hot) + nt(low, hot)
        high, low = split2(by_slot)
        rows = query_hot(w)
        table_grad = table_grad + (tn(rows, high) + tn(rows, low))[:64]
    table_grad = table_grad.astype(BF)
    entry_grad = jnp.where(own_token, nt(table_grad, spread), 0.0).astype(BF)
    weight_of = jnp.concatenate(
        [jnp.broadcast_to(weight_rows[h : h + 1, :], (16, width)) for h in range(heads)], axis=0
    )
    hat = z_hat[...]
    pair_norm = (hat * pair_gain[...]).astype(BF)
    norm_grad = tn(entry_grad, weight_of).astype(BF).astype(F32)
    weight_part = nn(entry_grad, pair_norm)
    tail = [
        jnp.sum(weight_part[h * 16 : (h + 1) * 16], axis=0, keepdims=True) for h in range(heads)
    ]
    tail = tail + [scale_sum, jnp.sum(norm_grad * hat, axis=0, keepdims=True)]
    tail = tail + [jnp.zeros((10, width), F32)]
    grads[5 * width : 5 * width + 16, :] = jnp.concatenate(tail, axis=0).astype(BF)
    band_part = norm_back(norm_grad * pair_gain[...], hat, pair_inv).astype(BF)
    for c in range(16):
        outgoing[c, : entries // 16, :] = band_part[c * (entries // 16) : (c + 1) * (entries // 16)]


def finish_kernel(atoms, cotangent, own_grad, from_before, from_after, atom_gain, result):
    samples, count, width = atoms.shape
    gain = atom_gain[...]
    for s in range(samples):
        x_hat, inv = norm(atoms[s].astype(F32))
        rim = jnp.zeros((count - RIM, width), F32)
        total = own_grad[s] + jnp.concatenate([from_before[s].astype(F32), rim], axis=0)
        total = total + jnp.concatenate([rim, from_after[s].astype(F32)], axis=0)
        g = total.astype(BF).astype(F32) * gain
        result[s] = (cotangent[s].astype(F32) + norm_back(g, x_hat, inv)).astype(BF)


def vmem(n):
    return [pl.BlockSpec(memory_space=pltpu.VMEM)] * n


def shards(
    atoms,
    cotangent,
    project,
    combine,
    atom_gain,
    pair_band,
    pair_gain,
    pair_weight,
    atom_token,
    key_range,
):
    samples, count, width = atoms.shape
    heads = pair_weight.shape[1]
    rows, cols = lax.axis_size("row"), lax.axis_size("col")
    peers = rows * cols
    device = lax.axis_index(("row", "col"))
    windows = count // QW
    block = pair_band.shape[0] // cols
    keys = pair_band.shape[1]
    up = [(i, i + 1) for i in range(peers - 1)]
    down = [(i + 1, i) for i in range(peers - 1)]

    tiles = jnp.transpose(pair_band.reshape(cols, block, keys, width), (0, 2, 1, 3))
    tiles = lax.all_to_all(tiles, "col", 0, 0, tiled=True).reshape(cols * keys * block, width)

    local = atom_token - device * block

    def packed(part, tokens):
        line = jnp.pad(tokens.astype(BF), (0, width - RIM))
        return jnp.concatenate([part, jnp.broadcast_to(line, (1, RIM, width))], axis=0)

    before = lax.ppermute(packed(atoms[:, count - RIM :], local[count - RIM :]), ("row", "col"), up)
    after = lax.ppermute(packed(atoms[:, :RIM], local[:RIM]), ("row", "col"), down)
    extended = jnp.concatenate(
        [
            before[samples, 0, :RIM].astype(jnp.int32),
            local + block,
            after[samples, 0, :RIM].astype(jnp.int32) + 2 * block,
        ]
    )
    key_tokens = jnp.stack([extended[w * QW : w * QW + KW] for w in range(windows)])
    key_tokens = jnp.pad(key_tokens, ((0, 8 - windows), (0, 0)))
    query_tokens = jnp.broadcast_to(local[:, None], (count, KW))
    first_slot = device * count - RIM + QW * jnp.arange(windows, dtype=jnp.int32)
    ranges = key_range - first_slot[:, None]
    weight_rows = jnp.pad(pair_weight.T, ((0, 16 - heads), (0, 0)))
    gain = atom_gain.reshape(1, width)
    entries = tiles.shape[0]
    shape = jax.ShapeDtypeStruct
    grads, to_before, to_after, own_grad, outgoing = pl.pallas_call(
        attention_kernel,
        out_shape=(
            shape((768, width), BF),
            shape((samples, RIM, width), BF),
            shape((samples, RIM, width), BF),
            shape((samples, count, width), F32),
            shape((cols, 2 * RIM - 24, width), BF),
        ),
        in_specs=[pl.BlockSpec(memory_space=pltpu.SMEM)] + vmem(12),
        out_specs=tuple(vmem(5)),
        scratch_shapes=[
            pltpu.VMEM((windows, KW, KW), F32),
            pltpu.VMEM((windows, KW, KW), F32),
            pltpu.VMEM((count + 2 * RIM, 2 * width), F32),
            pltpu.VMEM((entries, width), F32),
        ],
        compiler_params=pltpu.CompilerParams(vmem_limit_bytes=32 * 1024 * 1024),
        name="attention",
    )(
        ranges,
        atoms,
        cotangent,
        before,
        after,
        project,
        combine,
        gain,
        tiles,
        pair_gain.reshape(1, width),
        weight_rows,
        query_tokens,
        key_tokens,
    )

    core = lax.axis_index("row") % 2
    swap = [(i, i ^ 1) for i in range(rows)]
    grads = grads.reshape(2, grads.shape[0] // 2, width)
    chunk = grads.shape[1] // cols
    line = keys * block
    theirs = lax.ppermute(lax.dynamic_index_in_dim(grads, 1 - core, 0, False), "row", swap)
    mine = lax.dynamic_index_in_dim(grads, core, 0, False)
    half = (mine.astype(F32) + theirs.astype(F32)).astype(BF).reshape(cols, chunk, width)
    outgoing = lax.dynamic_update_slice(outgoing, half, (0, line, 0))
    scattered = lax.all_to_all(outgoing, "col", 0, 0, tiled=True)
    band_grad = scattered[:, :line].reshape(cols, keys, block, width)
    band_grad = jnp.transpose(band_grad, (0, 2, 1, 3)).reshape(pair_band.shape)
    part = jnp.sum(scattered[:, line:].astype(F32), axis=0).astype(BF)

    part, to_before, to_after = lax.optimization_barrier((part, to_before, to_after))
    groups = [list(range(first, rows, 2)) for first in range(2)]
    part = jnp.broadcast_to(part, (rows // 2, chunk, width))
    part = lax.all_to_all(part, "row", 0, 0, axis_index_groups=groups, tiled=True)
    from_before = lax.ppermute(to_after, ("row", "col"), up)
    from_after = lax.ppermute(to_before, ("row", "col"), down)
    part = jnp.sum(part.astype(F32), axis=0).astype(BF)
    part, from_before, from_after = lax.optimization_barrier((part, from_before, from_after))
    part = jnp.broadcast_to(part, (cols, chunk, width))
    half = lax.all_to_all(part, "col", 0, 0, tiled=True).reshape(cols * chunk, width)
    atoms_grad = pl.pallas_call(
        finish_kernel,
        out_shape=shape(atoms.shape, BF),
        in_specs=vmem(6),
        out_specs=pl.BlockSpec(memory_space=pltpu.VMEM),
        name="finish",
    )(atoms, cotangent, own_grad, from_before, from_after, gain)
    half, atoms_grad, band_grad = lax.optimization_barrier((half, atoms_grad, band_grad))
    other = lax.ppermute(half, "row", swap)
    total = jnp.where(
        core == 0,
        jnp.concatenate([half, other], axis=0),
        jnp.concatenate([other, half], axis=0),
    )

    project_grad = jnp.transpose(total[: 4 * width].reshape(4, width, width), (1, 0, 2))
    tail = total[5 * width :]
    return (
        atoms_grad,
        project_grad.reshape(width, 4 * width),
        total[4 * width : 5 * width],
        tail[heads].astype(F32),
        band_grad,
        tail[:heads].T,
        tail[heads + 1].astype(F32),
    )


def solution(mesh):
    in_specs = (
        P(None, ("row", "col"), None),
        P(None, ("row", "col"), None),
        P(),
        P(),
        P(),
        P("row", "col", None),
        P(),
        P(),
        P(("row", "col")),
        P(("row", "col"), None),
    )
    out_specs = (P(None, ("row", "col"), None), P(), P(), P(), P("row", "col", None), P(), P())
    return jax.shard_map(shards, mesh=mesh, in_specs=in_specs, out_specs=out_specs, check_vma=False)
```

```python
import math

import jax
import jax.numpy as jnp
from jax import lax
from jax.experimental import pallas as pl
from jax.experimental.pallas import tpu as pltpu
from jax.sharding import PartitionSpec as P

QW = 32
KW = 128
RIM = 48
EPSILON = 1e-05
NEG_FILL = -1e30
F32 = jnp.float32
BF = jnp.bfloat16


def nn(a, b):
    return lax.dot_general(a, b, (((1,), (0,)), ((), ())), preferred_element_type=F32)


def nt(a, b):
    return lax.dot_general(a, b, (((1,), (1,)), ((), ())), preferred_element_type=F32)


def tn(a, b):
    return lax.dot_general(a, b, (((0,), (0,)), ((), ())), preferred_element_type=F32)


def split2(x):
    high = x.astype(BF)
    return high, (x - high.astype(F32)).astype(BF)


def norm(v):
    mean = jnp.mean(v, axis=-1, keepdims=True)
    centred = v - mean
    inv = lax.rsqrt(jnp.mean(centred * centred, axis=-1, keepdims=True) + EPSILON)
    return centred * inv, inv


def norm_back(g, hat, inv):
    first = jnp.mean(g, axis=-1, keepdims=True)
    second = jnp.mean(g * hat, axis=-1, keepdims=True)
    return inv * (g - first - hat * second)


def iota(shape, dim):
    return lax.broadcasted_iota(jnp.int32, shape, dim)


def pack_kernel(atoms, tokens, to_before, to_after):
    samples, count, width = atoms.shape
    to_before[:samples] = atoms[:, :RIM]
    to_after[:samples] = atoms[:, count - RIM :]
    line = tokens[...].astype(F32)
    to_before[samples] = jnp.broadcast_to(line, (RIM, width)).astype(BF)
    to_after[samples] = jnp.broadcast_to(line, (RIM, width)).astype(BF)


def pair_kernel(band, pair_gain, weight_rows, table, z_hat, pair_inv):
    heads = 4
    entries = band.shape[0]
    hat, inv = norm(band[...].astype(F32))
    z_hat[...] = hat
    pair_inv[...] = inv
    pair_norm = (hat * pair_gain[...]).astype(BF)
    bias_rows = nt(weight_rows[...], pair_norm)
    stacked = jnp.concatenate(
        [jnp.broadcast_to(bias_rows[h : h + 1], (16, entries)) for h in range(heads)], axis=0
    )
    own_token = (iota((64, entries), 0) & 15) == (iota((64, entries), 1) & 15)
    high, low = split2(jnp.where(own_token, stacked, 0.0))
    spread = (iota((entries, KW), 0) >> 4) == iota((entries, KW), 1)
    spread = jnp.where(spread, 1.0, 0.0).astype(BF)
    table[...] = nn(jnp.concatenate([high, low], axis=0), spread).astype(BF)


def attention_kernel(
    key_range,
    device,
    atoms,
    cotangent,
    before,
    after,
    project,
    combine,
    atom_gain,
    table,
    z_hat,
    pair_inv,
    pair_gain,
    weight_rows,
    tokens,
    outgoing,
    to_before,
    to_after,
    own_grad,
    bias,
    bias_grad,
):
    samples, count, width = atoms.shape
    heads = 4
    windows = count // QW
    entries = z_hat.shape[0]
    scale = 1.0 / math.sqrt(width // heads)
    gain = atom_gain[...]

    lane = iota((KW, KW), 1)
    line = iota((KW, KW), 0)

    own = jnp.broadcast_to(tokens[...].astype(F32), (8, KW))
    left = before[samples][:16].astype(F32)[:8] - 16.0
    right = after[samples][:16].astype(F32)[:8] + 16.0
    row_lane = iota((8, KW), 1)
    turned = [own] + [pltpu.roll(own, h * QW, 1) for h in range(1, heads)]

    def query_row(w):
        row = turned[(-w) % heads]
        for h in range(1, heads):
            row = jnp.where((row_lane >> 5) == h, turned[(h - w) % heads], row)
        return row.astype(jnp.int32)[:1]

    def key_row(w):
        shift = RIM - w * QW
        first, second = (left, own) if shift > 0 else (own, right)
        shift = shift % KW
        row = jnp.where(row_lane < shift, pltpu.roll(first, shift, 1), pltpu.roll(second, shift, 1))
        return row.astype(jnp.int32)[:1] + 16

    def query_hot(w):
        hit = ((line & 15) == query_row(w)) & (((line >> 4) & 3) == (lane >> 5))
        return jnp.where(hit, 1.0, 0.0).astype(BF)

    def key_hot(w):
        return jnp.where(line == key_row(w), 1.0, 0.0).astype(BF)

    for w in range(windows):
        by_key = nn(table[...], key_hot(w)).astype(BF)
        values = tn(by_key, query_hot(w))
        first = device[0] * count - RIM + w * QW
        allowed = (line >= key_range[w, 0] - first) & (line < key_range[w, 1] - first)
        bias[w] = jnp.where(allowed, values, NEG_FILL)
        bias_grad[w] = jnp.zeros((KW, KW), F32)
    diag = jnp.where((line >> 5) == (lane >> 5), 1.0, 0.0).astype(BF)
    head_of = iota((QW, width), 1) >> 5

    def spread_heads(x):
        return jnp.concatenate([x] * heads, axis=0) * diag

    def gather_heads(x):
        total = x[:QW]
        for h in range(1, heads):
            total = jnp.where(head_of == h, x[h * QW : (h + 1) * QW], total)
        return total

    def overlap(parts):
        sums = []
        for m in range(windows + KW // QW - 1):
            total = None
            for w in range(windows):
                if 0 <= m - w < KW // QW:
                    term = parts[w][(m - w) * QW : (m - w + 1) * QW]
                    total = term if total is None else total + term
            sums.append(total)
        return jnp.concatenate(sums, axis=0).astype(BF)

    def sample(s, carry):
        project_sum, combine_sum, scale_sum = carry
        x = jnp.concatenate([before[s], atoms[s], after[s]], axis=0).astype(F32)
        x_hat, _ = norm(x)
        normed = (x_hat * gain).astype(BF)
        projected = nn(normed, project[...]).astype(BF)
        query = projected[RIM : RIM + count, :width]
        key = projected[:, width : 2 * width]
        value = projected[:, 2 * width : 3 * width]
        gate = projected[RIM : RIM + count, 3 * width :].astype(F32)
        out = cotangent[s]
        sigmoid = jax.nn.sigmoid(gate)
        gated_grad = nt(out, combine[...]).astype(BF).astype(F32)
        mixture_grad = (gated_grad * sigmoid).astype(BF)
        span = range(windows)
        q = [spread_heads(query[w * QW : (w + 1) * QW]) for w in span]
        g = [spread_heads(mixture_grad[w * QW : (w + 1) * QW]) for w in span]
        k = [key[w * QW : w * QW + KW] for w in span]
        v = [value[w * QW : w * QW + KW] for w in span]
        scores = [nt(k[w], q[w]) * scale + bias[w] for w in span]
        weights_grad = [nt(v[w], g[w]).astype(BF).astype(F32) for w in span]
        scores = [jnp.exp(x - jnp.max(x, axis=0, keepdims=True)) for x in scores]
        weights = [x * (1.0 / jnp.sum(x, axis=0, keepdims=True)) for x in scores]
        low = [x.astype(BF) for x in weights]
        mixture = jnp.concatenate([gather_heads(tn(low[w], v[w])) for w in span], axis=0)
        row_dot = [jnp.sum(weights[w] * weights_grad[w], axis=0, keepdims=True) for w in span]
        score_grad = [weights[w] * (weights_grad[w] - row_dot[w]) for w in span]
        for w in span:
            bias_grad[w] += score_grad[w]
        score_low = [(x * scale).astype(BF) for x in score_grad]
        query_grads = [gather_heads(tn(score_low[w], k[w])).astype(BF) for w in span]
        key_grad = overlap([nn(score_low[w], q[w]) for w in span])
        value_grad = overlap([nn(low[w], g[w]) for w in span])
        gated = (mixture * sigmoid).astype(BF)
        combine_sum = combine_sum + tn(gated, out)
        gate_grad = (gated_grad * mixture * sigmoid * (1.0 - sigmoid)).astype(BF)
        rim = jnp.zeros((RIM, width), BF)
        query_cols = jnp.concatenate([rim] + query_grads + [rim], axis=0)
        gate_cols = jnp.concatenate([rim, gate_grad, rim], axis=0)
        grad = jnp.concatenate([query_cols, key_grad, value_grad, gate_cols], axis=1)
        project_sum = project_sum + tn(normed, grad)
        normed_grad = nt(grad, project[...])
        scale_sum = scale_sum + jnp.sum(normed_grad * x_hat, axis=0, keepdims=True)
        to_before[s] = normed_grad[:RIM].astype(BF)
        to_after[s] = normed_grad[RIM + count :].astype(BF)
        own_grad[s] = normed_grad[RIM : RIM + count]
        return project_sum, combine_sum, scale_sum

    start = (
        jnp.zeros((width, 4 * width), F32),
        jnp.zeros((width, width), F32),
        jnp.zeros((1, width), F32),
    )
    project_sum, combine_sum, scale_sum = lax.fori_loop(0, samples, sample, start, unroll=True)

    table_grad = jnp.zeros((KW, KW), F32)
    for w in range(windows):
        high, low = split2(bias_grad[w])
        hot = key_hot(w)
        by_slot = nn(hot, high) + nn(hot, low)
        high, low = split2(by_slot)
        rows = query_hot(w)
        table_grad = table_grad + nt(high, rows) + nt(low, rows)
    spread = (iota((entries, KW), 0) >> 4) == iota((entries, KW), 1)
    spread = jnp.where(spread, 1.0, 0.0).astype(BF)
    entry_grad = nn(spread, table_grad.astype(BF))
    shown = (iota((entries, KW), 0) & 15) == (iota((entries, KW), 1) & 15)
    shown = shown & (iota((entries, KW), 1) < 64)
    entry_grad = jnp.where(shown, entry_grad, 0.0).astype(BF)
    weight_of = jnp.concatenate(
        [jnp.broadcast_to(weight_rows[h : h + 1, :], (16, width)) for h in range(heads)] * 2, axis=0
    )
    hat = z_hat[...]
    pair_norm = (hat * pair_gain[...]).astype(BF)
    norm_grad = nn(entry_grad, weight_of).astype(BF).astype(F32)
    weight_part = tn(entry_grad, pair_norm)
    tail = [
        jnp.sum(weight_part[h * 16 : (h + 1) * 16], axis=0, keepdims=True) for h in range(heads)
    ]
    tail = tail + [scale_sum, jnp.sum(norm_grad * hat, axis=0, keepdims=True)]
    tail = tail + [jnp.zeros((10, width), F32)]
    band_part = norm_back(norm_grad * pair_gain[...], hat, pair_inv[...]).astype(BF)
    sums = jnp.concatenate(
        [project_sum[:, part * width : (part + 1) * width] for part in range(4)]
        + [combine_sum]
        + tail
        + [jnp.zeros((entries - 5 * width - 16, width), F32)],
        axis=0,
    ).astype(BF)
    part = entries // 16
    for c in range(16):
        outgoing[c, :part, :] = band_part[c * part : (c + 1) * part]
        outgoing[c, part:, :] = sums[c * part : (c + 1) * part]


def last_kernel(parts, project_grad, combine_grad, weight_grad, scale_grad, gain_grad):
    rows = jnp.concatenate([parts[c] for c in range(parts.shape[0])], axis=0)
    width = rows.shape[1]
    for part in range(4):
        project_grad[:, part * width : (part + 1) * width] = rows[part * width : (part + 1) * width]
    combine_grad[...] = rows[4 * width : 5 * width]
    tail = rows[5 * width : 5 * width + 16].astype(F32)
    weight_grad[...] = tail[:4].astype(BF)
    scale_grad[...] = tail[4:5]
    gain_grad[...] = tail[5:6]


def finish_kernel(atoms, cotangent, own_grad, from_before, from_after, atom_gain, result):
    samples, count, width = atoms.shape
    gain = atom_gain[...]
    for s in range(samples):
        x_hat, inv = norm(atoms[s].astype(F32))
        rim = jnp.zeros((count - RIM, width), F32)
        total = own_grad[s] + jnp.concatenate([from_before[s].astype(F32), rim], axis=0)
        total = total + jnp.concatenate([rim, from_after[s].astype(F32)], axis=0)
        g = total.astype(BF).astype(F32) * gain
        result[s] = (cotangent[s].astype(F32) + norm_back(g, x_hat, inv)).astype(BF)


def vmem(n):
    return [pl.BlockSpec(memory_space=pltpu.VMEM)] * n


def shards(
    atoms,
    cotangent,
    project,
    combine,
    atom_gain,
    pair_band,
    pair_gain,
    pair_weight,
    atom_token,
    key_range,
):
    samples, count, width = atoms.shape
    heads = pair_weight.shape[1]
    rows, cols = lax.axis_size("row"), lax.axis_size("col")
    peers = rows * cols
    device = lax.axis_index(("row", "col"))
    windows = count // QW
    block = pair_band.shape[0] // cols
    keys = pair_band.shape[1]
    up = [(i, i + 1) for i in range(peers - 1)]
    down = [(i + 1, i) for i in range(peers - 1)]

    shape = jax.ShapeDtypeStruct

    tiles = jnp.transpose(pair_band.reshape(cols, block, keys, width), (0, 2, 1, 3))
    tiles = lax.all_to_all(tiles, "col", 0, 0, tiled=True).reshape(cols * keys * block, width)

    local = atom_token - device * block
    to_before, to_after = pl.pallas_call(
        pack_kernel,
        out_shape=(shape((samples + 1, RIM, width), BF),) * 2,
        in_specs=vmem(2),
        out_specs=tuple(vmem(2)),
        name="pack",
    )(atoms, local.reshape(1, count))
    before = lax.ppermute(to_after, ("row", "col"), up)
    after = lax.ppermute(to_before, ("row", "col"), down)
    weight_rows = jnp.pad(pair_weight.T, ((0, 16 - heads), (0, 0)))
    gain = atom_gain.reshape(1, width)
    entries = tiles.shape[0]
    table, z_hat, pair_inv = pl.pallas_call(
        pair_kernel,
        out_shape=(
            shape((KW, KW), BF),
            shape((entries, width), F32),
            shape((entries, 1), F32),
        ),
        in_specs=vmem(3),
        out_specs=tuple(vmem(3)),
        cost_estimate=pl.CostEstimate(flops=10**9, bytes_accessed=10**7, transcendentals=0),
        name="pair",
    )(tiles, pair_gain.reshape(1, width), weight_rows)
    outgoing, to_before, to_after, own_grad = pl.pallas_call(
        attention_kernel,
        out_shape=(
            shape((cols, 2 * keys * block, width), BF),
            shape((samples, RIM, width), BF),
            shape((samples, RIM, width), BF),
            shape((samples, count, width), F32),
        ),
        in_specs=[pl.BlockSpec(memory_space=pltpu.SMEM)] * 2 + vmem(13),
        out_specs=tuple(vmem(4)),
        scratch_shapes=[
            pltpu.VMEM((windows, KW, KW), F32),
            pltpu.VMEM((windows, KW, KW), F32),
        ],
        compiler_params=pltpu.CompilerParams(vmem_limit_bytes=32 * 1024 * 1024),
        name="attention",
    )(
        key_range,
        device.astype(jnp.int32).reshape(1),
        atoms,
        cotangent,
        before,
        after,
        project,
        combine,
        gain,
        table,
        z_hat,
        pair_inv,
        pair_gain.reshape(1, width),
        weight_rows,
        local.reshape(1, count),
    )

    line = keys * block
    chunk = outgoing.shape[1] - line
    scattered = lax.all_to_all(outgoing, "col", 0, 0, tiled=True)
    band_grad = scattered[:, :line].reshape(cols, keys, block, width)
    band_grad = jnp.transpose(band_grad, (0, 2, 1, 3)).reshape(pair_band.shape)
    part = jnp.sum(scattered[:, line:].astype(F32), axis=0).astype(BF)

    def summed(x, groups):
        x = jnp.broadcast_to(x, (len(groups[0]), chunk, width))
        x = lax.all_to_all(x, "row", 0, 0, axis_index_groups=groups, tiled=True)
        return jnp.sum(x.astype(F32), axis=0).astype(BF)

    near = [
        [y * 8 + z * 2 + core for y in range(rows // 8) for core in range(2)] for z in range(4)
    ]
    far = [
        [y * 8 + z * 2 + core for z in range(4)] for y in range(rows // 8) for core in range(2)
    ]
    part = summed(part, near)

    part, to_before, to_after = lax.optimization_barrier((part, to_before, to_after))
    part = summed(part, far)
    from_before = lax.ppermute(to_after, ("row", "col"), up)
    from_after = lax.ppermute(to_before, ("row", "col"), down)
    part, from_before, from_after = lax.optimization_barrier((part, from_before, from_after))
    part = jnp.broadcast_to(part, (cols, chunk, width))
    part = lax.all_to_all(part, "col", 0, 0, tiled=True)
    atoms_grad = pl.pallas_call(
        finish_kernel,
        out_shape=shape(atoms.shape, BF),
        in_specs=vmem(6),
        out_specs=pl.BlockSpec(memory_space=pltpu.VMEM),
        name="finish",
    )(atoms, cotangent, own_grad, from_before, from_after, gain)
    part, atoms_grad, band_grad = lax.optimization_barrier((part, atoms_grad, band_grad))
    project_grad, combine_grad, weight_grad, scale_grad, gain_grad = pl.pallas_call(
        last_kernel,
        out_shape=(
            shape(project.shape, BF),
            shape(combine.shape, BF),
            shape((heads, width), BF),
            shape((1, width), F32),
            shape((1, width), F32),
        ),
        in_specs=vmem(1),
        out_specs=tuple(vmem(5)),
        name="last",
    )(part)
    return (
        atoms_grad,
        project_grad,
        combine_grad,
        scale_grad.reshape(width),
        band_grad,
        weight_grad.T,
        gain_grad.reshape(width),
    )


def solution(mesh):
    in_specs = (
        P(None, ("row", "col"), None),
        P(None, ("row", "col"), None),
        P(),
        P(),
        P(),
        P("row", "col", None),
        P(),
        P(),
        P(("row", "col")),
        P(("row", "col"), None),
    )
    out_specs = (P(None, ("row", "col"), None), P(), P(), P(), P("row", "col", None), P(), P())
    return jax.shard_map(shards, mesh=mesh, in_specs=in_specs, out_specs=out_specs, check_vma=False)
```

```python
import math

import jax
import jax.numpy as jnp
from jax import lax
from jax.experimental import pallas as pl
from jax.experimental.pallas import tpu as pltpu
from jax.sharding import PartitionSpec as P

QW = 32
KW = 128
RIM = 48
EPSILON = 1e-05
NEG_FILL = -1e30
F32 = jnp.float32
BF = jnp.bfloat16


LIMIT = pltpu.CompilerParams(vmem_limit_bytes=16 * 1024 * 1024)


def nn(a, b):
    return lax.dot_general(a, b, (((1,), (0,)), ((), ())), preferred_element_type=F32)


def nt(a, b):
    return lax.dot_general(a, b, (((1,), (1,)), ((), ())), preferred_element_type=F32)


def tn(a, b):
    return lax.dot_general(a, b, (((0,), (0,)), ((), ())), preferred_element_type=F32)


def split2(x):
    high = x.astype(BF)
    return high, (x - high.astype(F32)).astype(BF)


def norm(v):
    mean = jnp.mean(v, axis=-1, keepdims=True)
    centred = v - mean
    inv = lax.rsqrt(jnp.mean(centred * centred, axis=-1, keepdims=True) + EPSILON)
    return centred * inv, inv


def norm_back(g, hat, inv):
    first = jnp.mean(g, axis=-1, keepdims=True)
    second = jnp.mean(g * hat, axis=-1, keepdims=True)
    return inv * (g - first - hat * second)


def iota(shape, dim):
    return lax.broadcasted_iota(jnp.int32, shape, dim)


def fetch(pairs, sems):
    copies = [pltpu.make_async_copy(src, dst, sems.at[n]) for n, (src, dst) in enumerate(pairs)]
    for copy in copies:
        copy.start()
    return copies


def pack_kernel(device, atoms, tokens, to_before, to_after, line, sems):
    samples, count, width = atoms.shape
    copies = fetch(
        [
            (tokens, line),
            (atoms.at[:, :RIM], to_before.at[:samples]),
            (atoms.at[:, count - RIM :], to_after.at[:samples]),
        ],
        sems,
    )
    copies[0].wait()
    local = jnp.broadcast_to((line[...] - device[0] * 16).astype(F32), (RIM, width)).astype(BF)
    to_before[samples] = local
    to_after[samples] = local
    copies[1].wait()
    copies[2].wait()


def weight_lines(weights):
    rows = weights[...].astype(F32)
    return jnp.concatenate([rows, jnp.zeros((16 - rows.shape[0], rows.shape[1]), F32)], axis=0)


def weight_spread(weights):
    rows = weights[...].astype(F32)
    rows = [jnp.broadcast_to(rows[h : h + 1], (16, rows.shape[1])) for h in range(4)]
    return jnp.concatenate(rows * 2, axis=0).astype(BF)


def spread_slots(entries):
    hit = (iota((entries, KW), 0) >> 4) == iota((entries, KW), 1)
    return jnp.where(hit, 1.0, 0.0).astype(BF)


def entry_grads(table_grad, entries):
    grad = nn(spread_slots(entries), table_grad)
    column = iota((entries, KW), 1)
    shown = ((iota((entries, KW), 0) & 15) == (column & 15)) & (column < 64)
    return jnp.where(shown, grad, 0.0).astype(BF)


def pair_kernel(band, gain_hbm, weight_hbm, table, pair_norm, gain, weights, sems):
    heads = 4
    entries = band.shape[0]
    copies = fetch([(gain_hbm, gain), (weight_hbm, weights)], sems)
    hat, _ = norm(band[...].astype(F32))
    for copy in copies:
        copy.wait()
    normed = (hat * gain[...]).astype(BF)
    pair_norm[...] = normed
    bias_rows = nt(weight_lines(weights).astype(BF), normed)
    stacked = jnp.concatenate(
        [jnp.broadcast_to(bias_rows[h : h + 1], (16, entries)) for h in range(heads)], axis=0
    )
    own_token = (iota((64, entries), 0) & 15) == (iota((64, entries), 1) & 15)
    high, low = split2(jnp.where(own_token, stacked, 0.0))
    both = jnp.concatenate([high, low], axis=0)
    table[...] = nn(both, spread_slots(entries)).astype(BF)


def band_kernel(band, scattered, pair_gain, weights, band_grad):
    entries = band.shape[0]
    width = band.shape[1]
    rows = [scattered[c].astype(F32)[40:43] for c in range(scattered.shape[0])]
    rows = jnp.concatenate(rows + [jnp.zeros((KW - 3 * len(rows), width), F32)], axis=0).astype(BF)
    hat, inv = norm(band[...].astype(F32))
    norm_grad = nn(entry_grads(rows, entries), weight_spread(weights)).astype(BF).astype(F32)
    band_grad[...] = norm_back(norm_grad * pair_gain[...], hat, inv).astype(BF)


def attention_kernel(
    key_range,
    device,
    atoms_hbm,
    cotangent_hbm,
    project_hbm,
    combine_hbm,
    gain_hbm,
    tokens_hbm,
    before,
    after,
    table,
    pair_norm,
    outgoing,
    to_before,
    to_after,
    own_grad,
    bias,
    bias_grad,
    atoms,
    cotangent,
    project,
    combine,
    atom_gain,
    tokens,
    sems,
):
    samples, count, width = atoms.shape
    heads = 4
    windows = count // QW
    entries = pair_norm.shape[0]
    scale = 1.0 / math.sqrt(width // heads)
    copies = fetch(
        [
            (tokens_hbm, tokens),
            (gain_hbm, atom_gain),
            (atoms_hbm, atoms),
            (project_hbm, project),
            (cotangent_hbm, cotangent),
            (combine_hbm, combine),
        ],
        sems,
    )
    copies[0].wait()
    lane = iota((KW, KW), 1)
    line = iota((KW, KW), 0)

    own = jnp.broadcast_to((tokens[...] - device[0] * 16).astype(F32), (8, KW))
    left = before[samples][:16].astype(F32)[:8] - 16.0
    right = after[samples][:16].astype(F32)[:8] + 16.0
    row_lane = iota((8, KW), 1)
    turned = [own] + [pltpu.roll(own, h * QW, 1) for h in range(1, heads)]

    def query_row(w):
        row = turned[(-w) % heads]
        for h in range(1, heads):
            row = jnp.where((row_lane >> 5) == h, turned[(h - w) % heads], row)
        return row.astype(jnp.int32)[:1]

    def key_row(w):
        shift = RIM - w * QW
        first, second = (left, own) if shift > 0 else (own, right)
        shift = shift % KW
        row = jnp.where(row_lane < shift, pltpu.roll(first, shift, 1), pltpu.roll(second, shift, 1))
        return row.astype(jnp.int32)[:1] + 16

    def query_hot(w):
        hit = ((line & 15) == query_row(w)) & (((line >> 4) & 3) == (lane >> 5))
        return jnp.where(hit, 1.0, 0.0).astype(BF)

    def key_hot(w):
        return jnp.where(line == key_row(w), 1.0, 0.0).astype(BF)

    for w in range(windows):
        by_key = nn(table[...], key_hot(w)).astype(BF)
        values = tn(by_key, query_hot(w))
        first = device[0] * count - RIM + w * QW
        allowed = (line >= key_range[w, 0] - first) & (line < key_range[w, 1] - first)
        bias[w] = jnp.where(allowed, values, NEG_FILL)
        bias_grad[w] = jnp.zeros((KW, KW), F32)
    for copy in copies[1:]:
        copy.wait()
    gain = atom_gain[...]
    diag = jnp.where((line >> 5) == (lane >> 5), 1.0, 0.0).astype(BF)
    head_of = iota((QW, width), 1) >> 5

    def spread_heads(x):
        return jnp.concatenate([x] * heads, axis=0) * diag

    def gather_heads(x):
        total = x[:QW]
        for h in range(1, heads):
            total = jnp.where(head_of == h, x[h * QW : (h + 1) * QW], total)
        return total

    def overlap(parts):
        sums = []
        for m in range(windows + KW // QW - 1):
            total = None
            for w in range(windows):
                if 0 <= m - w < KW // QW:
                    term = parts[w][(m - w) * QW : (m - w + 1) * QW]
                    total = term if total is None else total + term
            sums.append(total)
        return jnp.concatenate(sums, axis=0).astype(BF)

    def sample(s, carry):
        project_sum, combine_sum = carry
        x = jnp.concatenate([before[s], atoms[s], after[s]], axis=0).astype(F32)
        x_hat, _ = norm(x)
        normed = (x_hat * gain).astype(BF)
        projected = nn(normed, project[...]).astype(BF)
        query = projected[RIM : RIM + count, :width]
        key = projected[:, width : 2 * width]
        value = projected[:, 2 * width : 3 * width]
        gate = projected[RIM : RIM + count, 3 * width :].astype(F32)
        out = cotangent[s]
        sigmoid = jax.nn.sigmoid(gate)
        gated_grad = nt(out, combine[...]).astype(BF).astype(F32)
        mixture_grad = (gated_grad * sigmoid).astype(BF)
        span = range(windows)
        q = [spread_heads(query[w * QW : (w + 1) * QW]) for w in span]
        g = [spread_heads(mixture_grad[w * QW : (w + 1) * QW]) for w in span]
        k = [key[w * QW : w * QW + KW] for w in span]
        v = [value[w * QW : w * QW + KW] for w in span]
        scores = [nt(k[w], q[w]) * scale + bias[w] for w in span]
        weights_grad = [nt(v[w], g[w]).astype(BF).astype(F32) for w in span]
        scores = [jnp.exp(x - jnp.max(x, axis=0, keepdims=True)) for x in scores]
        weights = [x * (1.0 / jnp.sum(x, axis=0, keepdims=True)) for x in scores]
        low = [x.astype(BF) for x in weights]
        mixture = jnp.concatenate([gather_heads(tn(low[w], v[w])) for w in span], axis=0)
        row_dot = [jnp.sum(weights[w] * weights_grad[w], axis=0, keepdims=True) for w in span]
        score_grad = [weights[w] * (weights_grad[w] - row_dot[w]) for w in span]
        for w in span:
            bias_grad[w] += score_grad[w]
        score_low = [(x * scale).astype(BF) for x in score_grad]
        query_grads = [gather_heads(tn(score_low[w], k[w])).astype(BF) for w in span]
        key_grad = overlap([nn(score_low[w], q[w]) for w in span])
        value_grad = overlap([nn(low[w], g[w]) for w in span])
        gated = (mixture * sigmoid).astype(BF)
        combine_sum = combine_sum + tn(gated, out)
        gate_grad = (gated_grad * mixture * sigmoid * (1.0 - sigmoid)).astype(BF)
        rim = jnp.zeros((RIM, width), BF)
        query_cols = jnp.concatenate([rim] + query_grads + [rim], axis=0)
        gate_cols = jnp.concatenate([rim, gate_grad, rim], axis=0)
        grad = jnp.concatenate([query_cols, key_grad, value_grad, gate_cols], axis=1)
        project_sum = project_sum + tn(normed, grad)
        normed_grad = nt(grad, project[...])
        to_before[s] = normed_grad[:RIM].astype(BF)
        to_after[s] = normed_grad[RIM + count :].astype(BF)
        own_grad[s] = normed_grad[RIM : RIM + count]
        return project_sum, combine_sum

    start = (
        jnp.zeros((width, 4 * width), F32),
        jnp.zeros((width, width), F32),
    )
    project_sum, combine_sum = lax.fori_loop(0, samples, sample, start, unroll=True)

    table_grad = jnp.zeros((KW, KW), F32)
    for w in range(windows):
        high, low = split2(bias_grad[w])
        hot = key_hot(w)
        by_slot = nn(hot, high) + nn(hot, low)
        high, low = split2(by_slot)
        rows = query_hot(w)
        table_grad = table_grad + nt(high, rows) + nt(low, rows)
    entry_grad = entry_grads(table_grad.astype(BF), entries)
    weight_part = tn(entry_grad, pair_norm[...])
    sums = jnp.concatenate(
        [project_sum[:, part * width : (part + 1) * width] for part in range(4)] + [combine_sum],
        axis=0,
    )
    peers = outgoing.shape[0]
    for c in range(peers):
        weight_row = jnp.zeros((1, width), F32)
        if c < heads:
            weight_row = jnp.sum(weight_part[c * 16 : (c + 1) * 16], axis=0, keepdims=True)
        parts = [sums[c * 40 : (c + 1) * 40], table_grad[3 * c : 3 * c + 3], weight_row]
        parts = parts + [jnp.zeros((4, width), F32)]
        outgoing[c] = jnp.concatenate(parts, axis=0).astype(BF)


def last_kernel(
    parts_hbm,
    project_hbm,
    atom_gain_hbm,
    pair_gain_hbm,
    weight_hbm,
    project_grad,
    combine_grad,
    weight_grad,
    scale_grad,
    gain_grad,
    parts,
    project,
    atom_gain,
    pair_gain,
    weights,
    sems,
):
    copies = fetch(
        [
            (parts_hbm, parts),
            (project_hbm, project),
            (atom_gain_hbm, atom_gain),
            (pair_gain_hbm, pair_gain),
            (weight_hbm, weights),
        ],
        sems,
    )
    for copy in copies:
        copy.wait()
    chunks = [parts[c].astype(F32) for c in range(parts.shape[0])]
    rows = jnp.concatenate([x[:40] for x in chunks], axis=0)
    width = rows.shape[1]
    dots = jnp.zeros((width, 1), F32)
    for part in range(4):
        columns = slice(part * width, (part + 1) * width)
        block = rows[part * width : (part + 1) * width]
        project_grad[:, columns] = block.astype(BF)
        dots = dots + jnp.sum(block * project[:, columns].astype(F32), axis=1, keepdims=True)
    combine_grad[...] = rows[4 * width :].astype(BF)
    dots = jnp.transpose(jnp.broadcast_to(dots, (width, width)))[:1]
    scale_grad[...] = dots / atom_gain[...]
    tail = jnp.concatenate([x[43:44] for x in chunks[:4]], axis=0)
    weight_grad[...] = tail.astype(BF)
    dots = jnp.sum(tail * weights[...].astype(F32), axis=0, keepdims=True)
    gain_grad[...] = dots / pair_gain[...]


def finish_kernel(atoms, cotangent, own_grad, from_before, from_after, atom_gain, result):
    samples, count, width = atoms.shape
    gain = atom_gain[...]
    for s in range(samples):
        x_hat, inv = norm(atoms[s].astype(F32))
        rim = jnp.zeros((count - RIM, width), F32)
        total = own_grad[s] + jnp.concatenate([from_before[s].astype(F32), rim], axis=0)
        total = total + jnp.concatenate([rim, from_after[s].astype(F32)], axis=0)
        g = total.astype(BF).astype(F32) * gain
        result[s] = (cotangent[s].astype(F32) + norm_back(g, x_hat, inv)).astype(BF)


def vmem(n):
    return [pl.BlockSpec(memory_space=pltpu.VMEM)] * n


def smem(n):
    return [pl.BlockSpec(memory_space=pltpu.SMEM)] * n


def anywhere(n):
    return [pl.BlockSpec(memory_space=pl.ANY)] * n


def copied(arrays):
    return [pltpu.VMEM(x.shape, x.dtype) for x in arrays] + [
        pltpu.SemaphoreType.DMA((len(arrays),))
    ]


def shards(
    atoms,
    cotangent,
    project,
    combine,
    atom_gain,
    pair_band,
    pair_gain,
    pair_weight,
    atom_token,
    key_range,
):
    samples, count, width = atoms.shape
    rows, cols = lax.axis_size("row"), lax.axis_size("col")
    peers = rows * cols
    device = lax.axis_index(("row", "col"))
    windows = count // QW
    block = pair_band.shape[0] // cols
    keys = pair_band.shape[1]
    up = [(i, i + 1) for i in range(peers - 1)]
    down = [(i + 1, i) for i in range(peers - 1)]

    shape = jax.ShapeDtypeStruct

    shape = jax.ShapeDtypeStruct
    device = device.astype(jnp.int32).reshape(1)
    tokens = atom_token.reshape(1, count)
    weights = pair_weight.T
    gain = atom_gain.reshape(1, width)
    band_gain = pair_gain.reshape(1, width)

    entries = cols * keys * block
    tiles = jnp.transpose(pair_band.reshape(cols, block, keys, width), (0, 2, 1, 3))
    band = lax.all_to_all(tiles, "col", 0, 0, tiled=True).reshape(entries, width)

    to_before, to_after = pl.pallas_call(
        pack_kernel,
        out_shape=(shape((samples + 1, RIM, width), BF),) * 2,
        in_specs=smem(1) + anywhere(2),
        out_specs=tuple(vmem(2)),
        scratch_shapes=[pltpu.VMEM((1, count), jnp.int32), pltpu.SemaphoreType.DMA((3,))],
        compiler_params=LIMIT,
        name="pack",
    )(device, atoms, tokens)
    before = lax.ppermute(to_after, ("row", "col"), up)
    after = lax.ppermute(to_before, ("row", "col"), down)

    fetched = [band_gain, weights]
    table, pair_norm = pl.pallas_call(
        pair_kernel,
        out_shape=(shape((KW, KW), BF), shape((entries, width), BF)),
        in_specs=vmem(1) + anywhere(2),
        out_specs=tuple(vmem(2)),
        scratch_shapes=copied(fetched),
        cost_estimate=pl.CostEstimate(flops=10**9, bytes_accessed=10**7, transcendentals=0),
        compiler_params=LIMIT,
        name="pair",
    )(band, *fetched)
    fetched = [atoms, cotangent, project, combine, gain, tokens]
    outgoing, to_before, to_after, own_grad = pl.pallas_call(
        attention_kernel,
        out_shape=(
            shape((cols, RIM, width), BF),
            shape((samples, RIM, width), BF),
            shape((samples, RIM, width), BF),
            shape((samples, count, width), F32),
        ),
        in_specs=smem(2) + anywhere(len(fetched)) + vmem(4),
        out_specs=tuple(vmem(4)),
        scratch_shapes=[
            pltpu.VMEM((windows, KW, KW), F32),
            pltpu.VMEM((windows, KW, KW), F32),
        ]
        + copied(fetched),
        compiler_params=LIMIT,
        name="attention",
    )(key_range, device, *fetched, before, after, table, pair_norm)

    chunk = outgoing.shape[1]
    scattered = lax.all_to_all(outgoing, "col", 0, 0, tiled=True)
    part = jnp.sum(scattered.astype(F32), axis=0).astype(BF)

    def summed(x, groups):
        x = jnp.broadcast_to(x, (len(groups[0]), chunk, width))
        x = lax.all_to_all(x, "row", 0, 0, axis_index_groups=groups, tiled=True)
        return jnp.sum(x.astype(F32), axis=0).astype(BF)

    near = [
        [y * 8 + z * 2 + core for y in range(rows // 8) for core in range(2)] for z in range(4)
    ]
    far = [
        [y * 8 + z * 2 + core for z in range(4)] for y in range(rows // 8) for core in range(2)
    ]
    part = summed(part, near)
    band_grad = pl.pallas_call(
        band_kernel,
        out_shape=shape((entries, width), BF),
        in_specs=vmem(4),
        out_specs=pl.BlockSpec(memory_space=pltpu.VMEM),
        compiler_params=LIMIT,
        name="band",
    )(tiles.reshape(entries, width), scattered, band_gain, weights)
    part, band_grad = lax.optimization_barrier((part, band_grad))
    band_grad = jnp.transpose(band_grad.reshape(cols, keys, block, width), (0, 2, 1, 3))
    band_grad = band_grad.reshape(pair_band.shape)

    part, to_before, to_after = lax.optimization_barrier((part, to_before, to_after))
    part = summed(part, far)
    from_before = lax.ppermute(to_after, ("row", "col"), up)
    from_after = lax.ppermute(to_before, ("row", "col"), down)
    part, from_before, from_after = lax.optimization_barrier((part, from_before, from_after))
    part = jnp.broadcast_to(part, (cols, chunk, width))
    part = lax.all_to_all(part, "col", 0, 0, tiled=True)
    atoms_grad = pl.pallas_call(
        finish_kernel,
        out_shape=shape(atoms.shape, BF),
        in_specs=vmem(6),
        out_specs=pl.BlockSpec(memory_space=pltpu.VMEM),
        compiler_params=LIMIT,
        name="finish",
    )(atoms, cotangent, own_grad, from_before, from_after, gain)
    part, atoms_grad, band_grad = lax.optimization_barrier((part, atoms_grad, band_grad))
    fetched = [part, project, gain, band_gain, weights]
    project_grad, combine_grad, weight_grad, scale_grad, gain_grad = pl.pallas_call(
        last_kernel,
        out_shape=(
            shape(project.shape, BF),
            shape(combine.shape, BF),
            shape(weights.shape, BF),
            shape((1, width), F32),
            shape((1, width), F32),
        ),
        in_specs=anywhere(5),
        out_specs=tuple(vmem(5)),
        scratch_shapes=copied(fetched),
        compiler_params=LIMIT,
        name="last",
    )(*fetched)
    return (
        atoms_grad,
        project_grad,
        combine_grad,
        scale_grad.reshape(width),
        band_grad,
        weight_grad.T,
        gain_grad.reshape(width),
    )


def solution(mesh):
    in_specs = (
        P(None, ("row", "col"), None),
        P(None, ("row", "col"), None),
        P(),
        P(),
        P(),
        P("row", "col", None),
        P(),
        P(),
        P(("row", "col")),
        P(("row", "col"), None),
    )
    out_specs = (P(None, ("row", "col"), None), P(), P(), P(), P("row", "col", None), P(), P())
    return jax.shard_map(shards, mesh=mesh, in_specs=in_specs, out_specs=out_specs, check_vma=False)
```

```python
import math

import jax
import jax.numpy as jnp
from jax import lax
from jax.experimental import pallas as pl
from jax.experimental.pallas import tpu as pltpu
from jax.sharding import PartitionSpec as P

QW = 32
KW = 128
RIM = 48
EPSILON = 1e-05
NEG_FILL = -1e30
F32 = jnp.float32
BF = jnp.bfloat16


LIMIT = pltpu.CompilerParams(vmem_limit_bytes=16 * 1024 * 1024)


def nn(a, b):
    return lax.dot_general(a, b, (((1,), (0,)), ((), ())), preferred_element_type=F32)


def nt(a, b):
    return lax.dot_general(a, b, (((1,), (1,)), ((), ())), preferred_element_type=F32)


def tn(a, b):
    return lax.dot_general(a, b, (((0,), (0,)), ((), ())), preferred_element_type=F32)


def split2(x):
    high = x.astype(BF)
    return high, (x - high.astype(F32)).astype(BF)


def norm(v):
    mean = jnp.mean(v, axis=-1, keepdims=True)
    centred = v - mean
    inv = lax.rsqrt(jnp.mean(centred * centred, axis=-1, keepdims=True) + EPSILON)
    return centred * inv, inv


def norm_back(g, hat, inv):
    first = jnp.mean(g, axis=-1, keepdims=True)
    second = jnp.mean(g * hat, axis=-1, keepdims=True)
    return inv * (g - first - hat * second)


def iota(shape, dim):
    return lax.broadcasted_iota(jnp.int32, shape, dim)


def fetch(pairs, sems):
    copies = [pltpu.make_async_copy(src, dst, sems.at[n]) for n, (src, dst) in enumerate(pairs)]
    for copy in copies:
        copy.start()
    return copies


def pack_kernel(device, atoms, tokens, first, second, line, sems):
    samples, count, width = atoms.shape
    odd = device[0] & 1
    low = pl.multiple_of((1 - odd) * (count - RIM), 16)
    high = pl.multiple_of(odd * (count - RIM), 16)
    copies = fetch(
        [
            (tokens, line),
            (atoms.at[:, pl.ds(low, RIM)], first.at[:samples]),
            (atoms.at[:, pl.ds(high, RIM)], second.at[:samples]),
        ],
        sems,
    )
    copies[0].wait()
    local = jnp.broadcast_to((line[...] - device[0] * 16).astype(F32), (RIM, width)).astype(BF)
    first[samples] = local
    second[samples] = local
    copies[1].wait()
    copies[2].wait()


def weight_lines(weights):
    rows = weights[...].astype(F32)
    return jnp.concatenate([rows, jnp.zeros((16 - rows.shape[0], rows.shape[1]), F32)], axis=0)


def weight_spread(weights):
    rows = weights[...].astype(F32)
    rows = [jnp.broadcast_to(rows[h : h + 1], (16, rows.shape[1])) for h in range(4)]
    return jnp.concatenate(rows * 2, axis=0).astype(BF)


def spread_slots(entries):
    hit = (iota((entries, KW), 0) >> 4) == iota((entries, KW), 1)
    return jnp.where(hit, 1.0, 0.0).astype(BF)


def entry_grads(table_grad, entries):
    grad = nn(spread_slots(entries), table_grad)
    column = iota((entries, KW), 1)
    shown = ((iota((entries, KW), 0) & 15) == (column & 15)) & (column < 64)
    return jnp.where(shown, grad, 0.0).astype(BF)


def pair_kernel(band, gain_hbm, weight_hbm, table, pair_norm, gain, weights, sems):
    heads = 4
    entries = band.shape[0]
    copies = fetch([(gain_hbm, gain), (weight_hbm, weights)], sems)
    hat, _ = norm(band[...].astype(F32))
    for copy in copies:
        copy.wait()
    normed = (hat * gain[...]).astype(BF)
    pair_norm[...] = normed
    bias_rows = nt(weight_lines(weights).astype(BF), normed)
    stacked = jnp.concatenate(
        [jnp.broadcast_to(bias_rows[h : h + 1], (16, entries)) for h in range(heads)], axis=0
    )
    own_token = (iota((64, entries), 0) & 15) == (iota((64, entries), 1) & 15)
    high, low = split2(jnp.where(own_token, stacked, 0.0))
    both = jnp.concatenate([high, low], axis=0)
    table[...] = nn(both, spread_slots(entries)).astype(BF)


def band_kernel(device, band, scattered, pair_gain, weights, band_grad):
    entries = band.shape[0]
    width = band.shape[1]
    peers = scattered.shape[0] // 2
    core = (device[0] // peers) & 1
    rows = [scattered[core * peers + c].astype(F32)[20:23] for c in range(peers)]
    rows = jnp.concatenate(rows + [jnp.zeros((KW - 3 * len(rows), width), F32)], axis=0).astype(BF)
    hat, inv = norm(band[...].astype(F32))
    norm_grad = nn(entry_grads(rows, entries), weight_spread(weights)).astype(BF).astype(F32)
    band_grad[...] = norm_back(norm_grad * pair_gain[...], hat, inv).astype(BF)


def attention_kernel(
    key_range,
    device,
    atoms_hbm,
    cotangent_hbm,
    project_hbm,
    combine_hbm,
    gain_hbm,
    tokens_hbm,
    first,
    second,
    table,
    pair_norm,
    outgoing,
    to_first,
    to_second,
    own_grad,
    bias,
    bias_grad,
    atoms,
    cotangent,
    project,
    combine,
    atom_gain,
    tokens,
    sems,
):
    samples, count, width = atoms.shape
    heads = 4
    windows = count // QW
    entries = pair_norm.shape[0]
    scale = 1.0 / math.sqrt(width // heads)
    copies = fetch(
        [
            (tokens_hbm, tokens),
            (gain_hbm, atom_gain),
            (atoms_hbm, atoms),
            (project_hbm, project),
            (cotangent_hbm, cotangent),
            (combine_hbm, combine),
        ],
        sems,
    )
    copies[0].wait()
    lane = iota((KW, KW), 1)
    line = iota((KW, KW), 0)

    own = jnp.broadcast_to((tokens[...] - device[0] * 16).astype(F32), (8, KW))
    odd = (device[0] & 1) == 1

    def sides(x, y):
        return jnp.where(odd, x, y), jnp.where(odd, y, x)

    left, right = sides(first[samples].astype(F32), second[samples].astype(F32))
    left = left[:8] - 16.0
    right = right[:8] + 16.0
    row_lane = iota((8, KW), 1)
    turned = [own] + [pltpu.roll(own, h * QW, 1) for h in range(1, heads)]

    def query_row(w):
        row = turned[(-w) % heads]
        for h in range(1, heads):
            row = jnp.where((row_lane >> 5) == h, turned[(h - w) % heads], row)
        return row.astype(jnp.int32)[:1]

    def key_row(w):
        shift = RIM - w * QW
        one, two = (left, own) if shift > 0 else (own, right)
        shift = shift % KW
        row = jnp.where(row_lane < shift, pltpu.roll(one, shift, 1), pltpu.roll(two, shift, 1))
        return row.astype(jnp.int32)[:1] + 16

    def query_hot(w):
        hit = ((line & 15) == query_row(w)) & (((line >> 4) & 3) == (lane >> 5))
        return jnp.where(hit, 1.0, 0.0).astype(BF)

    def key_hot(w):
        return jnp.where(line == key_row(w), 1.0, 0.0).astype(BF)

    for w in range(windows):
        by_key = nn(table[...], key_hot(w)).astype(BF)
        values = tn(by_key, query_hot(w))
        begin = device[0] * count - RIM + w * QW
        allowed = (line >= key_range[w, 0] - begin) & (line < key_range[w, 1] - begin)
        bias[w] = jnp.where(allowed, values, NEG_FILL)
        bias_grad[w] = jnp.zeros((KW, KW), F32)
    for copy in copies[1:]:
        copy.wait()
    gain = atom_gain[...]
    diag = jnp.where((line >> 5) == (lane >> 5), 1.0, 0.0).astype(BF)
    head_of = iota((QW, width), 1) >> 5

    def spread_heads(x):
        return jnp.concatenate([x] * heads, axis=0) * diag

    def gather_heads(x):
        total = x[:QW]
        for h in range(1, heads):
            total = jnp.where(head_of == h, x[h * QW : (h + 1) * QW], total)
        return total

    def overlap(parts):
        sums = []
        for m in range(windows + KW // QW - 1):
            total = None
            for w in range(windows):
                if 0 <= m - w < KW // QW:
                    term = parts[w][(m - w) * QW : (m - w + 1) * QW]
                    total = term if total is None else total + term
            sums.append(total)
        return jnp.concatenate(sums, axis=0).astype(BF)

    def sample(s, carry):
        project_sum, combine_sum = carry
        before, after = sides(first[s].astype(F32), second[s].astype(F32))
        x = jnp.concatenate([before, atoms[s].astype(F32), after], axis=0)
        x_hat, _ = norm(x)
        normed = (x_hat * gain).astype(BF)
        projected = nn(normed, project[...]).astype(BF)
        query = projected[RIM : RIM + count, :width]
        key = projected[:, width : 2 * width]
        value = projected[:, 2 * width : 3 * width]
        gate = projected[RIM : RIM + count, 3 * width :].astype(F32)
        out = cotangent[s]
        sigmoid = jax.nn.sigmoid(gate)
        gated_grad = nt(out, combine[...]).astype(BF).astype(F32)
        mixture_grad = (gated_grad * sigmoid).astype(BF)
        span = range(windows)
        q = [spread_heads(query[w * QW : (w + 1) * QW]) for w in span]
        g = [spread_heads(mixture_grad[w * QW : (w + 1) * QW]) for w in span]
        k = [key[w * QW : w * QW + KW] for w in span]
        v = [value[w * QW : w * QW + KW] for w in span]
        scores = [nt(k[w], q[w]) * scale + bias[w] for w in span]
        weights_grad = [nt(v[w], g[w]).astype(BF).astype(F32) for w in span]
        scores = [jnp.exp(x - jnp.max(x, axis=0, keepdims=True)) for x in scores]
        weights = [x * (1.0 / jnp.sum(x, axis=0, keepdims=True)) for x in scores]
        low = [x.astype(BF) for x in weights]
        mixture = jnp.concatenate([gather_heads(tn(low[w], v[w])) for w in span], axis=0)
        row_dot = [jnp.sum(weights[w] * weights_grad[w], axis=0, keepdims=True) for w in span]
        score_grad = [weights[w] * (weights_grad[w] - row_dot[w]) for w in span]
        for w in span:
            bias_grad[w] += score_grad[w]
        score_low = [(x * scale).astype(BF) for x in score_grad]
        query_grads = [gather_heads(tn(score_low[w], k[w])).astype(BF) for w in span]
        key_grad = overlap([nn(score_low[w], q[w]) for w in span])
        value_grad = overlap([nn(low[w], g[w]) for w in span])
        gated = (mixture * sigmoid).astype(BF)
        combine_sum = combine_sum + tn(gated, out)
        gate_grad = (gated_grad * mixture * sigmoid * (1.0 - sigmoid)).astype(BF)
        rim = jnp.zeros((RIM, width), BF)
        query_cols = jnp.concatenate([rim] + query_grads + [rim], axis=0)
        gate_cols = jnp.concatenate([rim, gate_grad, rim], axis=0)
        grad = jnp.concatenate([query_cols, key_grad, value_grad, gate_cols], axis=1)
        project_sum = project_sum + tn(normed, grad)
        normed_grad = nt(grad, project[...])
        before, after = sides(normed_grad[:RIM], normed_grad[RIM + count :])
        to_first[s] = before.astype(BF)
        to_second[s] = after.astype(BF)
        own_grad[s] = normed_grad[RIM : RIM + count]
        return project_sum, combine_sum

    start = (
        jnp.zeros((width, 4 * width), F32),
        jnp.zeros((width, width), F32),
    )
    project_sum, combine_sum = lax.fori_loop(0, samples, sample, start, unroll=True)

    table_grad = jnp.zeros((KW, KW), F32)
    for w in range(windows):
        high, low = split2(bias_grad[w])
        hot = key_hot(w)
        by_slot = nn(hot, high) + nn(hot, low)
        high, low = split2(by_slot)
        rows = query_hot(w)
        table_grad = table_grad + nt(high, rows) + nt(low, rows)
    entry_grad = entry_grads(table_grad.astype(BF), entries)
    weight_part = tn(entry_grad, pair_norm[...])
    peers = outgoing.shape[0]
    for p in range(peers):
        part, row = divmod(16 * p, width)
        weight_row = jnp.zeros((1, width), F32)
        if p < heads:
            weight_row = jnp.sum(weight_part[p * 16 : (p + 1) * 16], axis=0, keepdims=True)
        slot = 3 * (p % (peers // 2))
        parts = [
            project_sum[row : row + 16, part * width : (part + 1) * width],
            combine_sum[4 * p : 4 * p + 4],
            table_grad[slot : slot + 3],
            weight_row,
        ]
        outgoing[p] = jnp.concatenate(parts, axis=0).astype(BF)


def last_kernel(
    parts_hbm,
    project_hbm,
    atom_gain_hbm,
    pair_gain_hbm,
    weight_hbm,
    project_grad,
    combine_grad,
    weight_grad,
    scale_grad,
    gain_grad,
    parts,
    project,
    atom_gain,
    pair_gain,
    weights,
    sems,
):
    copies = fetch(
        [
            (parts_hbm, parts),
            (project_hbm, project),
            (atom_gain_hbm, atom_gain),
            (pair_gain_hbm, pair_gain),
            (weight_hbm, weights),
        ],
        sems,
    )
    for copy in copies:
        copy.wait()
    chunks = [parts[p].astype(F32) for p in range(parts.shape[0])]
    rows = jnp.concatenate([x[:16] for x in chunks], axis=0)
    width = rows.shape[1]
    dots = jnp.zeros((width, 1), F32)
    for part in range(4):
        columns = slice(part * width, (part + 1) * width)
        block = rows[part * width : (part + 1) * width]
        project_grad[:, columns] = block.astype(BF)
        dots = dots + jnp.sum(block * project[:, columns].astype(F32), axis=1, keepdims=True)
    combine_grad[...] = jnp.concatenate([x[16:20] for x in chunks], axis=0).astype(BF)
    dots = jnp.transpose(jnp.broadcast_to(dots, (width, width)))[:1]
    scale_grad[...] = dots / atom_gain[...]
    tail = jnp.concatenate([x[23:24] for x in chunks[:4]], axis=0)
    weight_grad[...] = tail.astype(BF)
    dots = jnp.sum(tail * weights[...].astype(F32), axis=0, keepdims=True)
    gain_grad[...] = dots / pair_gain[...]


def finish_kernel(device, atoms, cotangent, own_grad, first, second, atom_gain, result):
    samples, count, width = atoms.shape
    odd = (device[0] & 1) == 1
    gain = atom_gain[...]
    for s in range(samples):
        x_hat, inv = norm(atoms[s].astype(F32))
        rim = jnp.zeros((count - RIM, width), F32)
        one, two = first[s].astype(F32), second[s].astype(F32)
        total = own_grad[s] + jnp.concatenate([jnp.where(odd, one, two), rim], axis=0)
        total = total + jnp.concatenate([rim, jnp.where(odd, two, one)], axis=0)
        g = total.astype(BF).astype(F32) * gain
        result[s] = (cotangent[s].astype(F32) + norm_back(g, x_hat, inv)).astype(BF)


def vmem(n):
    return [pl.BlockSpec(memory_space=pltpu.VMEM)] * n


def smem(n):
    return [pl.BlockSpec(memory_space=pltpu.SMEM)] * n


def anywhere(n):
    return [pl.BlockSpec(memory_space=pl.ANY)] * n


def copied(arrays):
    return [pltpu.VMEM(x.shape, x.dtype) for x in arrays] + [
        pltpu.SemaphoreType.DMA((len(arrays),))
    ]


def shards(
    atoms,
    cotangent,
    project,
    combine,
    atom_gain,
    pair_band,
    pair_gain,
    pair_weight,
    atom_token,
    key_range,
):
    samples, count, width = atoms.shape
    rows, cols = lax.axis_size("row"), lax.axis_size("col")
    peers = rows * cols
    device = lax.axis_index(("row", "col"))
    windows = count // QW
    block = pair_band.shape[0] // cols
    keys = pair_band.shape[1]
    pairs = [(i, i ^ 1) for i in range(peers)]
    odd_pairs = [(i + j, i + 1 - j) for i in range(1, peers - 1, 2) for j in range(2)]

    shape = jax.ShapeDtypeStruct

    shape = jax.ShapeDtypeStruct
    device = device.astype(jnp.int32).reshape(1)
    tokens = atom_token.reshape(1, count)
    weights = pair_weight.T
    gain = atom_gain.reshape(1, width)
    band_gain = pair_gain.reshape(1, width)

    entries = cols * keys * block
    tiles = jnp.transpose(pair_band.reshape(cols, block, keys, width), (0, 2, 1, 3))
    band = lax.all_to_all(tiles, "col", 0, 0, tiled=True).reshape(entries, width)

    first, second = pl.pallas_call(
        pack_kernel,
        out_shape=(shape((samples + 1, RIM, width), BF),) * 2,
        in_specs=smem(1) + anywhere(2),
        out_specs=tuple(vmem(2)),
        scratch_shapes=[pltpu.VMEM((1, count), jnp.int32), pltpu.SemaphoreType.DMA((3,))],
        compiler_params=LIMIT,
        name="pack",
    )(device, atoms, tokens)
    first = lax.ppermute(first, ("row", "col"), pairs)
    second = lax.ppermute(second, ("row", "col"), odd_pairs)

    fetched = [band_gain, weights]
    table, pair_norm = pl.pallas_call(
        pair_kernel,
        out_shape=(shape((KW, KW), BF), shape((entries, width), BF)),
        in_specs=vmem(1) + anywhere(2),
        out_specs=tuple(vmem(2)),
        scratch_shapes=copied(fetched),
        cost_estimate=pl.CostEstimate(flops=10**9, bytes_accessed=10**7, transcendentals=0),
        compiler_params=LIMIT,
        name="pair",
    )(band, *fetched)
    fetched = [atoms, cotangent, project, combine, gain, tokens]
    outgoing, first, second, own_grad = pl.pallas_call(
        attention_kernel,
        out_shape=(
            shape((2 * cols, 24, width), BF),
            shape((samples, RIM, width), BF),
            shape((samples, RIM, width), BF),
            shape((samples, count, width), F32),
        ),
        in_specs=smem(2) + anywhere(len(fetched)) + vmem(4),
        out_specs=tuple(vmem(4)),
        scratch_shapes=[
            pltpu.VMEM((windows, KW, KW), F32),
            pltpu.VMEM((windows, KW, KW), F32),
        ]
        + copied(fetched),
        compiler_params=LIMIT,
        name="attention",
    )(key_range, device, *fetched, first, second, table, pair_norm)

    near = [list(range(i, i + 2 * cols)) for i in range(0, peers, 2 * cols)]
    far = [list(range(i, rows, 2)) for i in range(2)]
    scattered = lax.all_to_all(
        outgoing, ("row", "col"), 0, 0, axis_index_groups=near, tiled=True
    )
    part = jnp.sum(scattered.astype(F32), axis=0).astype(BF)

    part, first, second = lax.optimization_barrier((part, first, second))
    part = jnp.broadcast_to(part, (rows // 2,) + part.shape)
    part = lax.all_to_all(part, "row", 0, 0, axis_index_groups=far, tiled=True)
    first = lax.ppermute(first, ("row", "col"), pairs)
    second = lax.ppermute(second, ("row", "col"), odd_pairs)
    part = jnp.sum(part.astype(F32), axis=0).astype(BF)
    part, first, second = lax.optimization_barrier((part, first, second))
    part = jnp.broadcast_to(part, (2 * cols,) + part.shape)
    part = lax.all_to_all(part, ("row", "col"), 0, 0, axis_index_groups=near, tiled=True)
    band_grad = pl.pallas_call(
        band_kernel,
        out_shape=shape((entries, width), BF),
        in_specs=smem(1) + vmem(4),
        out_specs=pl.BlockSpec(memory_space=pltpu.VMEM),
        compiler_params=LIMIT,
        name="band",
    )(device, tiles.reshape(entries, width), scattered, band_gain, weights)
    band_grad = jnp.transpose(band_grad.reshape(cols, keys, block, width), (0, 2, 1, 3))
    band_grad = band_grad.reshape(pair_band.shape)
    atoms_grad = pl.pallas_call(
        finish_kernel,
        out_shape=shape(atoms.shape, BF),
        in_specs=smem(1) + vmem(6),
        out_specs=pl.BlockSpec(memory_space=pltpu.VMEM),
        compiler_params=LIMIT,
        name="finish",
    )(device, atoms, cotangent, own_grad, first, second, gain)
    part, atoms_grad, band_grad = lax.optimization_barrier((part, atoms_grad, band_grad))
    fetched = [part, project, gain, band_gain, weights]
    project_grad, combine_grad, weight_grad, scale_grad, gain_grad = pl.pallas_call(
        last_kernel,
        out_shape=(
            shape(project.shape, BF),
            shape(combine.shape, BF),
            shape(weights.shape, BF),
            shape((1, width), F32),
            shape((1, width), F32),
        ),
        in_specs=anywhere(5),
        out_specs=tuple(vmem(5)),
        scratch_shapes=copied(fetched),
        compiler_params=LIMIT,
        name="last",
    )(*fetched)
    return (
        atoms_grad,
        project_grad,
        combine_grad,
        scale_grad.reshape(width),
        band_grad,
        weight_grad.T,
        gain_grad.reshape(width),
    )


def solution(mesh):
    in_specs = (
        P(None, ("row", "col"), None),
        P(None, ("row", "col"), None),
        P(),
        P(),
        P(),
        P("row", "col", None),
        P(),
        P(),
        P(("row", "col")),
        P(("row", "col"), None),
    )
    out_specs = (P(None, ("row", "col"), None), P(), P(), P(), P("row", "col", None), P(), P())
    return jax.shard_map(shards, mesh=mesh, in_specs=in_specs, out_specs=out_specs, check_vma=False)
```

```python
import math

import jax
import jax.numpy as jnp
from jax import lax
from jax.experimental import pallas as pl
from jax.experimental.pallas import tpu as pltpu
from jax.sharding import PartitionSpec as P

QW = 32
KW = 128
RIM = 48
EPSILON = 1e-05
NEG_FILL = -1e30
F32 = jnp.float32
BF = jnp.bfloat16


LIMIT = pltpu.CompilerParams(vmem_limit_bytes=16 * 1024 * 1024)


def nn(a, b):
    return lax.dot_general(a, b, (((1,), (0,)), ((), ())), preferred_element_type=F32)


def nt(a, b):
    return lax.dot_general(a, b, (((1,), (1,)), ((), ())), preferred_element_type=F32)


def tn(a, b):
    return lax.dot_general(a, b, (((0,), (0,)), ((), ())), preferred_element_type=F32)


def split2(x):
    high = x.astype(BF)
    return high, (x - high.astype(F32)).astype(BF)


def norm(v):
    mean = jnp.mean(v, axis=-1, keepdims=True)
    centred = v - mean
    inv = lax.rsqrt(jnp.mean(centred * centred, axis=-1, keepdims=True) + EPSILON)
    return centred * inv, inv


def norm_back(g, hat, inv):
    first = jnp.mean(g, axis=-1, keepdims=True)
    second = jnp.mean(g * hat, axis=-1, keepdims=True)
    return inv * (g - first - hat * second)


def iota(shape, dim):
    return lax.broadcasted_iota(jnp.int32, shape, dim)


def fetch(pairs, sems):
    copies = [pltpu.make_async_copy(src, dst, sems.at[n]) for n, (src, dst) in enumerate(pairs)]
    for copy in copies:
        copy.start()
    return copies


def start_kernel(device, band, atoms, tokens, tiles, first, second, line, lines, sems):
    samples, count, width = atoms.shape
    odd = device[0] & 1
    low = pl.multiple_of((1 - odd) * (count - RIM), 16)
    high = pl.multiple_of(odd * (count - RIM), 16)
    copies = fetch(
        [(tokens, line)]
        + [(band.at[k], tiles.at[:, k]) for k in range(band.shape[0])]
        + [
            (atoms.at[:, pl.ds(low, RIM)], first.at[:samples]),
            (atoms.at[:, pl.ds(high, RIM)], second.at[:samples]),
        ],
        sems.at[0],
    )
    copies[0].wait()
    local = (line[...] - device[0] * 16).astype(F32)
    lines[...] = jnp.broadcast_to(local, (RIM, width)).astype(BF)
    copies = copies[1:] + fetch(
        [(lines, first.at[samples]), (lines, second.at[samples])], sems.at[1]
    )
    for copy in copies:
        copy.wait()


def weight_lines(weights):
    rows = weights[...].astype(F32)
    return jnp.concatenate([rows, jnp.zeros((16 - rows.shape[0], rows.shape[1]), F32)], axis=0)


def weight_spread(weights):
    rows = weights[...].astype(F32)
    rows = [jnp.broadcast_to(rows[h : h + 1], (16, rows.shape[1])) for h in range(4)]
    return jnp.concatenate(rows * 2, axis=0).astype(BF)


def spread_slots(entries):
    hit = (iota((entries, KW), 0) >> 4) == iota((entries, KW), 1)
    return jnp.where(hit, 1.0, 0.0).astype(BF)


def entry_grads(table_grad, entries):
    grad = nn(spread_slots(entries), table_grad)
    column = iota((entries, KW), 1)
    shown = ((iota((entries, KW), 0) & 15) == (column & 15)) & (column < 64)
    return jnp.where(shown, grad, 0.0).astype(BF)


def pair_kernel(band, gain, weights, atom_gain, tokens, table, pair_norm, atom_gain_out, tokens_out):
    heads = 4
    entries = band.shape[0]
    atom_gain_out[...] = atom_gain[...]
    tokens_out[...] = tokens[...]
    hat, _ = norm(band[...].astype(F32))
    normed = (hat * gain[...]).astype(BF)
    pair_norm[...] = normed
    bias_rows = nt(weight_lines(weights).astype(BF), normed)
    stacked = jnp.concatenate(
        [jnp.broadcast_to(bias_rows[h : h + 1], (16, entries)) for h in range(heads)], axis=0
    )
    own_token = (iota((64, entries), 0) & 15) == (iota((64, entries), 1) & 15)
    high, low = split2(jnp.where(own_token, stacked, 0.0))
    both = jnp.concatenate([high, low], axis=0)
    table[...] = nn(both, spread_slots(entries)).astype(BF)


def band_kernel(device, band, scattered, pair_gain, weights, band_grad):
    entries = band.shape[0]
    width = band.shape[1]
    peers = scattered.shape[0] // 2
    core = (device[0] // peers) & 1
    rows = [scattered[core * peers + c].astype(F32)[20:23] for c in range(peers)]
    rows = jnp.concatenate(rows + [jnp.zeros((KW - 3 * len(rows), width), F32)], axis=0).astype(BF)
    hat, inv = norm(band[...].astype(F32))
    norm_grad = nn(entry_grads(rows, entries), weight_spread(weights)).astype(BF).astype(F32)
    band_grad[...] = norm_back(norm_grad * pair_gain[...], hat, inv).astype(BF)


def attention_kernel(
    key_range,
    device,
    atoms_hbm,
    cotangent_hbm,
    project_hbm,
    combine_hbm,
    gain_hbm,
    tokens_hbm,
    first,
    second,
    table,
    pair_norm,
    outgoing,
    to_first,
    to_second,
    own_grad,
    bias,
    bias_grad,
    atoms,
    cotangent,
    project,
    combine,
    atom_gain,
    tokens,
    sems,
):
    samples, count, width = atoms.shape
    heads = 4
    windows = count // QW
    entries = pair_norm.shape[0]
    scale = 1.0 / math.sqrt(width // heads)
    copies = fetch(
        [
            (tokens_hbm, tokens),
            (gain_hbm, atom_gain),
            (atoms_hbm, atoms),
            (project_hbm, project),
            (cotangent_hbm, cotangent),
            (combine_hbm, combine),
        ],
        sems,
    )
    copies[0].wait()
    lane = iota((KW, KW), 1)
    line = iota((KW, KW), 0)

    own = jnp.broadcast_to((tokens[...] - device[0] * 16).astype(F32), (8, KW))
    odd = (device[0] & 1) == 1

    def sides(x, y):
        return jnp.where(odd, x, y), jnp.where(odd, y, x)

    left, right = sides(first[samples].astype(F32), second[samples].astype(F32))
    left = left[:8] - 16.0
    right = right[:8] + 16.0
    row_lane = iota((8, KW), 1)
    turned = [own] + [pltpu.roll(own, h * QW, 1) for h in range(1, heads)]

    def query_row(w):
        row = turned[(-w) % heads]
        for h in range(1, heads):
            row = jnp.where((row_lane >> 5) == h, turned[(h - w) % heads], row)
        return row.astype(jnp.int32)[:1]

    def key_row(w):
        shift = RIM - w * QW
        one, two = (left, own) if shift > 0 else (own, right)
        shift = shift % KW
        row = jnp.where(row_lane < shift, pltpu.roll(one, shift, 1), pltpu.roll(two, shift, 1))
        return row.astype(jnp.int32)[:1] + 16

    def query_hot(w):
        hit = ((line & 15) == query_row(w)) & (((line >> 4) & 3) == (lane >> 5))
        return jnp.where(hit, 1.0, 0.0).astype(BF)

    def key_hot(w):
        return jnp.where(line == key_row(w), 1.0, 0.0).astype(BF)

    for w in range(windows):
        by_key = nn(table[...], key_hot(w)).astype(BF)
        values = tn(by_key, query_hot(w))
        begin = device[0] * count - RIM + w * QW
        allowed = (line >= key_range[w, 0] - begin) & (line < key_range[w, 1] - begin)
        bias[w] = jnp.where(allowed, values, NEG_FILL)
        bias_grad[w] = jnp.zeros((KW, KW), F32)
    for copy in copies[1:]:
        copy.wait()
    gain = atom_gain[...]
    diag = jnp.where((line >> 5) == (lane >> 5), 1.0, 0.0).astype(BF)
    head_of = iota((QW, width), 1) >> 5

    def spread_heads(x):
        return jnp.concatenate([x] * heads, axis=0) * diag

    def gather_heads(x):
        total = x[:QW]
        for h in range(1, heads):
            total = jnp.where(head_of == h, x[h * QW : (h + 1) * QW], total)
        return total

    def overlap(parts):
        sums = []
        for m in range(windows + KW // QW - 1):
            total = None
            for w in range(windows):
                if 0 <= m - w < KW // QW:
                    term = parts[w][(m - w) * QW : (m - w + 1) * QW]
                    total = term if total is None else total + term
            sums.append(total)
        return jnp.concatenate(sums, axis=0).astype(BF)

    def sample(s, carry):
        project_sum, combine_sum = carry
        before, after = sides(first[s].astype(F32), second[s].astype(F32))
        x = jnp.concatenate([before, atoms[s].astype(F32), after], axis=0)
        x_hat, _ = norm(x)
        normed = (x_hat * gain).astype(BF)
        projected = nn(normed, project[...]).astype(BF)
        query = projected[RIM : RIM + count, :width]
        key = projected[:, width : 2 * width]
        value = projected[:, 2 * width : 3 * width]
        gate = projected[RIM : RIM + count, 3 * width :].astype(F32)
        out = cotangent[s]
        sigmoid = jax.nn.sigmoid(gate)
        gated_grad = nt(out, combine[...]).astype(BF).astype(F32)
        mixture_grad = (gated_grad * sigmoid).astype(BF)
        span = range(windows)
        q = [spread_heads(query[w * QW : (w + 1) * QW]) for w in span]
        g = [spread_heads(mixture_grad[w * QW : (w + 1) * QW]) for w in span]
        k = [key[w * QW : w * QW + KW] for w in span]
        v = [value[w * QW : w * QW + KW] for w in span]
        scores = [nt(k[w], q[w]) * scale + bias[w] for w in span]
        weights_grad = [nt(v[w], g[w]).astype(BF).astype(F32) for w in span]
        scores = [jnp.exp(x - jnp.max(x, axis=0, keepdims=True)) for x in scores]
        weights = [x * (1.0 / jnp.sum(x, axis=0, keepdims=True)) for x in scores]
        low = [x.astype(BF) for x in weights]
        mixture = jnp.concatenate([gather_heads(tn(low[w], v[w])) for w in span], axis=0)
        row_dot = [jnp.sum(weights[w] * weights_grad[w], axis=0, keepdims=True) for w in span]
        score_grad = [weights[w] * (weights_grad[w] - row_dot[w]) for w in span]
        for w in span:
            bias_grad[w] += score_grad[w]
        score_low = [(x * scale).astype(BF) for x in score_grad]
        query_grads = [gather_heads(tn(score_low[w], k[w])).astype(BF) for w in span]
        key_grad = overlap([nn(score_low[w], q[w]) for w in span])
        value_grad = overlap([nn(low[w], g[w]) for w in span])
        gated = (mixture * sigmoid).astype(BF)
        combine_sum = combine_sum + tn(gated, out)
        gate_grad = (gated_grad * mixture * sigmoid * (1.0 - sigmoid)).astype(BF)
        rim = jnp.zeros((RIM, width), BF)
        query_cols = jnp.concatenate([rim] + query_grads + [rim], axis=0)
        gate_cols = jnp.concatenate([rim, gate_grad, rim], axis=0)
        grad = jnp.concatenate([query_cols, key_grad, value_grad, gate_cols], axis=1)
        project_sum = project_sum + tn(normed, grad)
        normed_grad = nt(grad, project[...])
        before, after = sides(normed_grad[:RIM], normed_grad[RIM + count :])
        to_first[s] = before.astype(BF)
        to_second[s] = after.astype(BF)
        own_grad[s] = normed_grad[RIM : RIM + count]
        return project_sum, combine_sum

    start = (
        jnp.zeros((width, 4 * width), F32),
        jnp.zeros((width, width), F32),
    )
    project_sum, combine_sum = lax.fori_loop(0, samples, sample, start, unroll=True)

    table_grad = jnp.zeros((KW, KW), F32)
    for w in range(windows):
        high, low = split2(bias_grad[w])
        hot = key_hot(w)
        by_slot = nn(hot, high) + nn(hot, low)
        high, low = split2(by_slot)
        rows = query_hot(w)
        table_grad = table_grad + nt(high, rows) + nt(low, rows)
    entry_grad = entry_grads(table_grad.astype(BF), entries)
    weight_part = tn(entry_grad, pair_norm[...])
    peers = outgoing.shape[0]
    for p in range(peers):
        part, row = divmod(16 * p, width)
        weight_row = jnp.zeros((1, width), F32)
        if p < heads:
            weight_row = jnp.sum(weight_part[p * 16 : (p + 1) * 16], axis=0, keepdims=True)
        slot = 3 * (p % (peers // 2))
        parts = [
            project_sum[row : row + 16, part * width : (part + 1) * width],
            combine_sum[4 * p : 4 * p + 4],
            table_grad[slot : slot + 3],
            weight_row,
        ]
        outgoing[p] = jnp.concatenate(parts, axis=0).astype(BF)


def last_kernel(
    parts_hbm,
    project_hbm,
    atom_gain_hbm,
    pair_gain_hbm,
    weight_hbm,
    project_grad,
    combine_grad,
    weight_grad,
    scale_grad,
    gain_grad,
    parts,
    project,
    atom_gain,
    pair_gain,
    weights,
    sems,
):
    copies = fetch(
        [
            (parts_hbm, parts),
            (project_hbm, project),
            (atom_gain_hbm, atom_gain),
            (pair_gain_hbm, pair_gain),
            (weight_hbm, weights),
        ],
        sems,
    )
    for copy in copies:
        copy.wait()
    chunks = [parts[p].astype(F32) for p in range(parts.shape[0])]
    rows = jnp.concatenate([x[:16] for x in chunks], axis=0)
    width = rows.shape[1]
    dots = jnp.zeros((width, 1), F32)
    for part in range(4):
        columns = slice(part * width, (part + 1) * width)
        block = rows[part * width : (part + 1) * width]
        project_grad[:, columns] = block.astype(BF)
        dots = dots + jnp.sum(block * project[:, columns].astype(F32), axis=1, keepdims=True)
    combine_grad[...] = jnp.concatenate([x[16:20] for x in chunks], axis=0).astype(BF)
    dots = jnp.transpose(jnp.broadcast_to(dots, (width, width)))[:1]
    scale_grad[...] = dots / atom_gain[...]
    tail = jnp.concatenate([x[23:24] for x in chunks[:4]], axis=0)
    weight_grad[...] = tail.astype(BF)
    dots = jnp.sum(tail * weights[...].astype(F32), axis=0, keepdims=True)
    gain_grad[...] = dots / pair_gain[...]


def finish_kernel(device, atoms, cotangent, own_grad, first, second, atom_gain, result):
    samples, count, width = atoms.shape
    odd = (device[0] & 1) == 1
    gain = atom_gain[...]
    for s in range(samples):
        x_hat, inv = norm(atoms[s].astype(F32))
        rim = jnp.zeros((count - RIM, width), F32)
        one, two = first[s].astype(F32), second[s].astype(F32)
        total = own_grad[s] + jnp.concatenate([jnp.where(odd, one, two), rim], axis=0)
        total = total + jnp.concatenate([rim, jnp.where(odd, two, one)], axis=0)
        g = total.astype(BF).astype(F32) * gain
        result[s] = (cotangent[s].astype(F32) + norm_back(g, x_hat, inv)).astype(BF)


def vmem(n):
    return [pl.BlockSpec(memory_space=pltpu.VMEM)] * n


def smem(n):
    return [pl.BlockSpec(memory_space=pltpu.SMEM)] * n


def anywhere(n):
    return [pl.BlockSpec(memory_space=pl.ANY)] * n


def copied(arrays):
    return [pltpu.VMEM(x.shape, x.dtype) for x in arrays] + [
        pltpu.SemaphoreType.DMA((len(arrays),))
    ]


def shards(
    atoms,
    cotangent,
    project,
    combine,
    atom_gain,
    pair_band,
    pair_gain,
    pair_weight,
    atom_token,
    key_range,
):
    samples, count, width = atoms.shape
    rows, cols = lax.axis_size("row"), lax.axis_size("col")
    peers = rows * cols
    device = lax.axis_index(("row", "col"))
    windows = count // QW
    block = pair_band.shape[0] // cols
    keys = pair_band.shape[1]
    pairs = [(i, i ^ 1) for i in range(peers)]
    odd_pairs = [(i + j, i + 1 - j) for i in range(1, peers - 1, 2) for j in range(2)]

    shape = jax.ShapeDtypeStruct

    shape = jax.ShapeDtypeStruct
    device = device.astype(jnp.int32).reshape(1)
    tokens = atom_token.reshape(1, count)
    weights = pair_weight.T
    gain = atom_gain.reshape(1, width)
    band_gain = pair_gain.reshape(1, width)

    entries = cols * keys * block
    tiles, first, second = pl.pallas_call(
        start_kernel,
        out_shape=(
            shape((cols, keys, block, width), BF),
            shape((samples + 1, RIM, width), BF),
            shape((samples + 1, RIM, width), BF),
        ),
        in_specs=smem(1) + anywhere(3),
        out_specs=tuple(anywhere(3)),
        scratch_shapes=[
            pltpu.VMEM((1, count), jnp.int32),
            pltpu.VMEM((RIM, width), BF),
            pltpu.SemaphoreType.DMA((2, 3 + keys)),
        ],
        compiler_params=pltpu.CompilerParams(vmem_limit_bytes=60 * 1024 * 1024),
        name="start",
    )(
        device,
        jnp.transpose(pair_band, (1, 0, 2)).reshape(keys, cols, block, width),
        atoms,
        tokens,
    )
    band = lax.all_to_all(tiles, "col", 0, 0, tiled=True).reshape(entries, width)

    first = lax.ppermute(first, ("row", "col"), pairs)
    second = lax.ppermute(second, ("row", "col"), odd_pairs)

    table, pair_norm, kept_gain, tokens = pl.pallas_call(
        pair_kernel,
        out_shape=(
            shape((KW, KW), BF),
            shape((entries, width), BF),
            shape(gain.shape, F32),
            shape(tokens.shape, jnp.int32),
        ),
        in_specs=vmem(5),
        out_specs=tuple(vmem(4)),
        cost_estimate=pl.CostEstimate(flops=10**9, bytes_accessed=10**7, transcendentals=0),
        compiler_params=LIMIT,
        name="pair",
    )(band, band_gain, weights, gain, tokens)
    fetched = [atoms, cotangent, project, combine, kept_gain, tokens]
    outgoing, first, second, own_grad = pl.pallas_call(
        attention_kernel,
        out_shape=(
            shape((2 * cols, 24, width), BF),
            shape((samples, RIM, width), BF),
            shape((samples, RIM, width), BF),
            shape((samples, count, width), F32),
        ),
        in_specs=smem(2) + anywhere(len(fetched)) + vmem(4),
        out_specs=tuple(vmem(4)),
        scratch_shapes=[
            pltpu.VMEM((windows, KW, KW), F32),
            pltpu.VMEM((windows, KW, KW), F32),
        ]
        + copied(fetched),
        compiler_params=LIMIT,
        name="attention",
    )(key_range, device, *fetched, first, second, table, pair_norm)

    near = [list(range(i, i + 2 * cols)) for i in range(0, peers, 2 * cols)]
    far = [list(range(i, rows, 2)) for i in range(2)]
    scattered = lax.all_to_all(
        outgoing, ("row", "col"), 0, 0, axis_index_groups=near, tiled=True
    )
    part = jnp.sum(scattered.astype(F32), axis=0).astype(BF)

    part, first, second = lax.optimization_barrier((part, first, second))
    part = jnp.broadcast_to(part, (rows // 2,) + part.shape)
    part = lax.all_to_all(part, "row", 0, 0, axis_index_groups=far, tiled=True)
    first = lax.ppermute(first, ("row", "col"), pairs)
    second = lax.ppermute(second, ("row", "col"), odd_pairs)
    part = jnp.sum(part.astype(F32), axis=0).astype(BF)
    part, first, second = lax.optimization_barrier((part, first, second))
    part = jnp.broadcast_to(part, (2 * cols,) + part.shape)
    part = lax.all_to_all(part, ("row", "col"), 0, 0, axis_index_groups=near, tiled=True)
    band_grad = pl.pallas_call(
        band_kernel,
        out_shape=shape((entries, width), BF),
        in_specs=smem(1) + vmem(4),
        out_specs=pl.BlockSpec(memory_space=pltpu.VMEM),
        compiler_params=LIMIT,
        name="band",
    )(device, tiles.reshape(entries, width), scattered, band_gain, weights)
    band_grad = jnp.transpose(band_grad.reshape(cols, keys, block, width), (0, 2, 1, 3))
    band_grad = band_grad.reshape(pair_band.shape)
    atoms_grad = pl.pallas_call(
        finish_kernel,
        out_shape=shape(atoms.shape, BF),
        in_specs=smem(1) + vmem(6),
        out_specs=pl.BlockSpec(memory_space=pltpu.VMEM),
        compiler_params=LIMIT,
        name="finish",
    )(device, atoms, cotangent, own_grad, first, second, gain)
    part, atoms_grad, band_grad = lax.optimization_barrier((part, atoms_grad, band_grad))
    fetched = [part, project, gain, band_gain, weights]
    project_grad, combine_grad, weight_grad, scale_grad, gain_grad = pl.pallas_call(
        last_kernel,
        out_shape=(
            shape(project.shape, BF),
            shape(combine.shape, BF),
            shape(weights.shape, BF),
            shape((1, width), F32),
            shape((1, width), F32),
        ),
        in_specs=anywhere(5),
        out_specs=tuple(vmem(5)),
        scratch_shapes=copied(fetched),
        compiler_params=LIMIT,
        name="last",
    )(*fetched)
    return (
        atoms_grad,
        project_grad,
        combine_grad,
        scale_grad.reshape(width),
        band_grad,
        weight_grad.T,
        gain_grad.reshape(width),
    )


def solution(mesh):
    in_specs = (
        P(None, ("row", "col"), None),
        P(None, ("row", "col"), None),
        P(),
        P(),
        P(),
        P("row", "col", None),
        P(),
        P(),
        P(("row", "col")),
        P(("row", "col"), None),
    )
    out_specs = (P(None, ("row", "col"), None), P(), P(), P(), P("row", "col", None), P(), P())
    return jax.shard_map(shards, mesh=mesh, in_specs=in_specs, out_specs=out_specs, check_vma=False)
```

```python
import math

import jax
import jax.numpy as jnp
from jax import lax
from jax.experimental import pallas as pl
from jax.experimental.pallas import tpu as pltpu
from jax.sharding import PartitionSpec as P

QW = 32
KW = 128
RIM = 48
EPSILON = 1e-05
NEG_FILL = -1e30
F32 = jnp.float32
BF = jnp.bfloat16


LIMIT = pltpu.CompilerParams(vmem_limit_bytes=16 * 1024 * 1024)


def nn(a, b):
    return lax.dot_general(a, b, (((1,), (0,)), ((), ())), preferred_element_type=F32)


def nt(a, b):
    return lax.dot_general(a, b, (((1,), (1,)), ((), ())), preferred_element_type=F32)


def tn(a, b):
    return lax.dot_general(a, b, (((0,), (0,)), ((), ())), preferred_element_type=F32)


def split2(x):
    high = x.astype(BF)
    return high, (x - high.astype(F32)).astype(BF)


def norm(v):
    mean = jnp.mean(v, axis=-1, keepdims=True)
    centred = v - mean
    inv = lax.rsqrt(jnp.mean(centred * centred, axis=-1, keepdims=True) + EPSILON)
    return centred * inv, inv


def norm_back(g, hat, inv):
    first = jnp.mean(g, axis=-1, keepdims=True)
    second = jnp.mean(g * hat, axis=-1, keepdims=True)
    return inv * (g - first - hat * second)


def iota(shape, dim):
    return lax.broadcasted_iota(jnp.int32, shape, dim)


def fetch(pairs, sems):
    copies = [pltpu.make_async_copy(src, dst, sems.at[n]) for n, (src, dst) in enumerate(pairs)]
    for copy in copies:
        copy.start()
    return copies


def start_kernel(device, band, atoms, tokens, tiles, first, second, line, sems):
    samples, count, width = atoms.shape
    odd = device[0] & 1
    low = pl.multiple_of((1 - odd) * (count - RIM), 16)
    high = pl.multiple_of(odd * (count - RIM), 16)
    copies = fetch(
        [(tokens, line)]
        + [(band.at[k], tiles.at[:, k]) for k in range(band.shape[0])]
        + [
            (atoms.at[:, pl.ds(low, RIM)], first.at[:samples]),
            (atoms.at[:, pl.ds(high, RIM)], second.at[:samples]),
        ],
        sems,
    )
    copies[0].wait()
    local = jnp.broadcast_to((line[...] - device[0] * 16).astype(F32), (RIM, width)).astype(BF)
    first[samples] = local
    second[samples] = local
    for copy in copies[1:]:
        copy.wait()


def weight_lines(weights):
    rows = weights[...].astype(F32)
    return jnp.concatenate([rows, jnp.zeros((16 - rows.shape[0], rows.shape[1]), F32)], axis=0)


def weight_spread(weights):
    rows = weights[...].astype(F32)
    rows = [jnp.broadcast_to(rows[h : h + 1], (16, rows.shape[1])) for h in range(4)]
    return jnp.concatenate(rows * 2, axis=0).astype(BF)


def spread_slots(entries):
    hit = (iota((entries, KW), 0) >> 4) == iota((entries, KW), 1)
    return jnp.where(hit, 1.0, 0.0).astype(BF)


def entry_grads(table_grad, entries):
    grad = nn(spread_slots(entries), table_grad)
    column = iota((entries, KW), 1)
    shown = ((iota((entries, KW), 0) & 15) == (column & 15)) & (column < 64)
    return jnp.where(shown, grad, 0.0).astype(BF)


def pair_kernel(band, gain, weights, atom_gain, tokens, table, pair_norm, atom_gain_out, tokens_out):
    heads = 4
    entries = band.shape[0]
    atom_gain_out[...] = atom_gain[...]
    tokens_out[...] = tokens[...]
    hat, _ = norm(band[...].astype(F32))
    normed = (hat * gain[...]).astype(BF)
    pair_norm[...] = normed
    bias_rows = nt(weight_lines(weights).astype(BF), normed)
    stacked = jnp.concatenate(
        [jnp.broadcast_to(bias_rows[h : h + 1], (16, entries)) for h in range(heads)], axis=0
    )
    own_token = (iota((64, entries), 0) & 15) == (iota((64, entries), 1) & 15)
    high, low = split2(jnp.where(own_token, stacked, 0.0))
    both = jnp.concatenate([high, low], axis=0)
    table[...] = nn(both, spread_slots(entries)).astype(BF)


def middle_kernel(device, scattered, outgoing):
    width = scattered.shape[2]
    total = scattered[0].astype(F32)
    for p in range(1, scattered.shape[0]):
        total = total + scattered[p].astype(F32)
    first = ((device[0] >> 7) & 3) * 8 + ((device[0] >> 4) & 1) * 4
    blocks = [scattered[first + x].astype(F32)[24:32] for x in range(4)]
    turned = [pltpu.roll(b, 64, 1) for b in blocks]
    left = iota((8, width), 1) < 64
    for z_lo in range(4):
        rows = slice(3 * (z_lo // 2), 3 * (z_lo // 2) + 3)
        lows, highs = (blocks, turned) if z_lo % 2 == 0 else (turned, blocks)
        pairs = [jnp.where(left, lows[x], highs[x + 1])[rows] for x in (0, 2)]
        tables = pairs + [jnp.zeros((2, width), F32)]
        result = jnp.concatenate([total[:24]] + tables, axis=0).astype(BF)
        for z_hi in range(4):
            outgoing[z_hi * 4 + z_lo] = result


def band_kernel(device, band, scattered, pair_gain, weights, band_grad):
    entries = band.shape[0]
    width = band.shape[1]
    z_hi = (device[0] >> 5) & 3
    rows = []
    for z_lo in range(4):
        block = scattered[z_hi * 4 + z_lo].astype(F32)[24:32]
        turned = pltpu.roll(block, 64, 1)
        rows = rows + [block[:3], turned[:3], block[3:6], turned[3:6]]
    rows = jnp.concatenate(rows + [jnp.zeros((KW - 48, width), F32)], axis=0).astype(BF)
    hat, inv = norm(band[...].astype(F32))
    norm_grad = nn(entry_grads(rows, entries), weight_spread(weights)).astype(BF).astype(F32)
    band_grad[...] = norm_back(norm_grad * pair_gain[...], hat, inv).astype(BF)


def attention_kernel(
    key_range,
    device,
    atoms_hbm,
    cotangent_hbm,
    project_hbm,
    combine_hbm,
    gain_hbm,
    tokens_hbm,
    first,
    second,
    table,
    pair_norm,
    outgoing,
    to_first,
    to_second,
    own_grad,
    bias,
    bias_grad,
    atoms,
    cotangent,
    project,
    combine,
    atom_gain,
    tokens,
    sems,
):
    samples, count, width = atoms.shape
    heads = 4
    windows = count // QW
    entries = pair_norm.shape[0]
    scale = 1.0 / math.sqrt(width // heads)
    copies = fetch(
        [
            (tokens_hbm, tokens),
            (gain_hbm, atom_gain),
            (atoms_hbm, atoms),
            (project_hbm, project),
            (cotangent_hbm, cotangent),
            (combine_hbm, combine),
        ],
        sems,
    )
    copies[0].wait()
    lane = iota((KW, KW), 1)
    line = iota((KW, KW), 0)

    own = jnp.broadcast_to((tokens[...] - device[0] * 16).astype(F32), (8, KW))
    odd = (device[0] & 1) == 1

    def sides(x, y):
        return jnp.where(odd, x, y), jnp.where(odd, y, x)

    left, right = sides(first[samples].astype(F32), second[samples].astype(F32))
    left = left[:8] - 16.0
    right = right[:8] + 16.0
    row_lane = iota((8, KW), 1)
    turned = [own] + [pltpu.roll(own, h * QW, 1) for h in range(1, heads)]

    def query_row(w):
        row = turned[(-w) % heads]
        for h in range(1, heads):
            row = jnp.where((row_lane >> 5) == h, turned[(h - w) % heads], row)
        return row.astype(jnp.int32)[:1]

    def key_row(w):
        shift = RIM - w * QW
        one, two = (left, own) if shift > 0 else (own, right)
        shift = shift % KW
        row = jnp.where(row_lane < shift, pltpu.roll(one, shift, 1), pltpu.roll(two, shift, 1))
        return row.astype(jnp.int32)[:1] + 16

    def query_hot(w):
        hit = ((line & 15) == query_row(w)) & (((line >> 4) & 3) == (lane >> 5))
        return jnp.where(hit, 1.0, 0.0).astype(BF)

    def key_hot(w):
        return jnp.where(line == key_row(w), 1.0, 0.0).astype(BF)

    for w in range(windows):
        by_key = nn(table[...], key_hot(w)).astype(BF)
        values = tn(by_key, query_hot(w))
        begin = device[0] * count - RIM + w * QW
        allowed = (line >= key_range[w, 0] - begin) & (line < key_range[w, 1] - begin)
        bias[w] = jnp.where(allowed, values, NEG_FILL)
        bias_grad[w] = jnp.zeros((KW, KW), F32)
    for copy in copies[1:]:
        copy.wait()
    gain = atom_gain[...]
    diag = jnp.where((line >> 5) == (lane >> 5), 1.0, 0.0).astype(BF)
    head_of = iota((QW, width), 1) >> 5

    def spread_heads(x):
        return jnp.concatenate([x] * heads, axis=0) * diag

    def gather_heads(x):
        total = x[:QW]
        for h in range(1, heads):
            total = jnp.where(head_of == h, x[h * QW : (h + 1) * QW], total)
        return total

    def overlap(parts):
        sums = []
        for m in range(windows + KW // QW - 1):
            total = None
            for w in range(windows):
                if 0 <= m - w < KW // QW:
                    term = parts[w][(m - w) * QW : (m - w + 1) * QW]
                    total = term if total is None else total + term
            sums.append(total)
        return jnp.concatenate(sums, axis=0).astype(BF)

    def sample(s, carry):
        project_sum, combine_sum = carry
        before, after = sides(first[s].astype(F32), second[s].astype(F32))
        x = jnp.concatenate([before, atoms[s].astype(F32), after], axis=0)
        x_hat, _ = norm(x)
        normed = (x_hat * gain).astype(BF)
        projected = nn(normed, project[...]).astype(BF)
        query = projected[RIM : RIM + count, :width]
        key = projected[:, width : 2 * width]
        value = projected[:, 2 * width : 3 * width]
        gate = projected[RIM : RIM + count, 3 * width :].astype(F32)
        out = cotangent[s]
        sigmoid = jax.nn.sigmoid(gate)
        gated_grad = nt(out, combine[...]).astype(BF).astype(F32)
        mixture_grad = (gated_grad * sigmoid).astype(BF)
        span = range(windows)
        q = [spread_heads(query[w * QW : (w + 1) * QW]) for w in span]
        g = [spread_heads(mixture_grad[w * QW : (w + 1) * QW]) for w in span]
        k = [key[w * QW : w * QW + KW] for w in span]
        v = [value[w * QW : w * QW + KW] for w in span]
        scores = [nt(k[w], q[w]) * scale + bias[w] for w in span]
        weights_grad = [nt(v[w], g[w]).astype(BF).astype(F32) for w in span]
        scores = [jnp.exp(x - jnp.max(x, axis=0, keepdims=True)) for x in scores]
        weights = [x * (1.0 / jnp.sum(x, axis=0, keepdims=True)) for x in scores]
        low = [x.astype(BF) for x in weights]
        mixture = jnp.concatenate([gather_heads(tn(low[w], v[w])) for w in span], axis=0)
        row_dot = [jnp.sum(weights[w] * weights_grad[w], axis=0, keepdims=True) for w in span]
        score_grad = [weights[w] * (weights_grad[w] - row_dot[w]) for w in span]
        for w in span:
            bias_grad[w] += score_grad[w]
        score_low = [(x * scale).astype(BF) for x in score_grad]
        query_grads = [gather_heads(tn(score_low[w], k[w])).astype(BF) for w in span]
        key_grad = overlap([nn(score_low[w], q[w]) for w in span])
        value_grad = overlap([nn(low[w], g[w]) for w in span])
        gated = (mixture * sigmoid).astype(BF)
        combine_sum = combine_sum + tn(gated, out)
        gate_grad = (gated_grad * mixture * sigmoid * (1.0 - sigmoid)).astype(BF)
        rim = jnp.zeros((RIM, width), BF)
        query_cols = jnp.concatenate([rim] + query_grads + [rim], axis=0)
        gate_cols = jnp.concatenate([rim, gate_grad, rim], axis=0)
        grad = jnp.concatenate([query_cols, key_grad, value_grad, gate_cols], axis=1)
        project_sum = project_sum + tn(normed, grad)
        normed_grad = nt(grad, project[...])
        before, after = sides(normed_grad[:RIM], normed_grad[RIM + count :])
        to_first[s] = before.astype(BF)
        to_second[s] = after.astype(BF)
        own_grad[s] = normed_grad[RIM : RIM + count]
        return project_sum, combine_sum

    start = (
        jnp.zeros((width, 4 * width), F32),
        jnp.zeros((width, width), F32),
    )
    project_sum, combine_sum = lax.fori_loop(0, samples, sample, start, unroll=True)

    table_grad = jnp.zeros((KW, KW), F32)
    for w in range(windows):
        high, low = split2(bias_grad[w])
        hot = key_hot(w)
        by_slot = nn(hot, high) + nn(hot, low)
        high, low = split2(by_slot)
        rows = query_hot(w)
        table_grad = table_grad + nt(high, rows) + nt(low, rows)
    entry_grad = entry_grads(table_grad.astype(BF), entries)
    weight_part = tn(entry_grad, pair_norm[...])
    left = iota((3, width), 1) < 64
    tables = []
    for x in range(4):
        by_z = [table_grad[3 * (4 * z + x) : 3 * (4 * z + x) + 3] for z in range(4)]
        pairs = [jnp.where(left, by_z[z], by_z[z + 1]) for z in (0, 2)]
        tables.append(jnp.concatenate(pairs + [jnp.zeros((2, width), F32)], axis=0))
    peers = outgoing.shape[0]
    for p in range(peers):
        part, row = divmod(16 * p, width)
        weight_row = jnp.zeros((1, width), F32)
        if p < heads:
            weight_row = jnp.sum(weight_part[p * 16 : (p + 1) * 16], axis=0, keepdims=True)
        parts = [
            project_sum[row : row + 16, part * width : (part + 1) * width],
            combine_sum[4 * p : 4 * p + 4],
            weight_row,
            jnp.zeros((3, width), F32),
            tables[p % 4],
        ]
        outgoing[p] = jnp.concatenate(parts, axis=0).astype(BF)


def last_kernel(
    parts_hbm,
    project_hbm,
    atom_gain_hbm,
    pair_gain_hbm,
    weight_hbm,
    project_grad,
    combine_grad,
    weight_grad,
    scale_grad,
    gain_grad,
    parts,
    project,
    atom_gain,
    pair_gain,
    weights,
    sems,
):
    copies = fetch(
        [
            (parts_hbm, parts),
            (project_hbm, project),
            (atom_gain_hbm, atom_gain),
            (pair_gain_hbm, pair_gain),
            (weight_hbm, weights),
        ],
        sems,
    )
    for copy in copies:
        copy.wait()
    chunks = [parts[p].astype(F32) for p in range(parts.shape[0])]
    rows = jnp.concatenate([x[:16] for x in chunks], axis=0)
    width = rows.shape[1]
    dots = jnp.zeros((width, 1), F32)
    for part in range(4):
        columns = slice(part * width, (part + 1) * width)
        block = rows[part * width : (part + 1) * width]
        project_grad[:, columns] = block.astype(BF)
        dots = dots + jnp.sum(block * project[:, columns].astype(F32), axis=1, keepdims=True)
    combine_grad[...] = jnp.concatenate([x[16:20] for x in chunks], axis=0).astype(BF)
    dots = jnp.transpose(jnp.broadcast_to(dots, (width, width)))[:1]
    scale_grad[...] = dots / atom_gain[...]
    tail = jnp.concatenate([x[20:21] for x in chunks[:4]], axis=0)
    weight_grad[...] = tail.astype(BF)
    dots = jnp.sum(tail * weights[...].astype(F32), axis=0, keepdims=True)
    gain_grad[...] = dots / pair_gain[...]


def finish_kernel(device, atoms, cotangent, own_grad, first, second, atom_gain, result):
    samples, count, width = atoms.shape
    odd = (device[0] & 1) == 1
    gain = atom_gain[...]
    for s in range(samples):
        x_hat, inv = norm(atoms[s].astype(F32))
        rim = jnp.zeros((count - RIM, width), F32)
        one, two = first[s].astype(F32), second[s].astype(F32)
        total = own_grad[s] + jnp.concatenate([jnp.where(odd, one, two), rim], axis=0)
        total = total + jnp.concatenate([rim, jnp.where(odd, two, one)], axis=0)
        g = total.astype(BF).astype(F32) * gain
        result[s] = (cotangent[s].astype(F32) + norm_back(g, x_hat, inv)).astype(BF)


def vmem(n):
    return [pl.BlockSpec(memory_space=pltpu.VMEM)] * n


def smem(n):
    return [pl.BlockSpec(memory_space=pltpu.SMEM)] * n


def anywhere(n):
    return [pl.BlockSpec(memory_space=pl.ANY)] * n


def copied(arrays):
    return [pltpu.VMEM(x.shape, x.dtype) for x in arrays] + [
        pltpu.SemaphoreType.DMA((len(arrays),))
    ]


def shards(
    atoms,
    cotangent,
    project,
    combine,
    atom_gain,
    pair_band,
    pair_gain,
    pair_weight,
    atom_token,
    key_range,
):
    samples, count, width = atoms.shape
    cols = lax.axis_size("col")
    peers = lax.axis_size("row") * cols
    device = lax.axis_index(("row", "col"))
    windows = count // QW
    block = pair_band.shape[0] // cols
    keys = pair_band.shape[1]
    pairs = [(i, i ^ 1) for i in range(peers)]
    odd_pairs = [(i + j, i + 1 - j) for i in range(1, peers - 1, 2) for j in range(2)]

    shape = jax.ShapeDtypeStruct

    shape = jax.ShapeDtypeStruct
    device = device.astype(jnp.int32).reshape(1)
    tokens = atom_token.reshape(1, count)
    weights = pair_weight.T
    gain = atom_gain.reshape(1, width)
    band_gain = pair_gain.reshape(1, width)

    entries = cols * keys * block
    tiles, first, second = pl.pallas_call(
        start_kernel,
        out_shape=(
            shape((cols, keys, block, width), BF),
            shape((samples + 1, RIM, width), BF),
            shape((samples + 1, RIM, width), BF),
        ),
        in_specs=smem(1) + anywhere(3),
        out_specs=tuple(vmem(3)),
        scratch_shapes=[
            pltpu.VMEM((1, count), jnp.int32),
            pltpu.SemaphoreType.DMA((3 + keys,)),
        ],
        compiler_params=pltpu.CompilerParams(vmem_limit_bytes=60 * 1024 * 1024),
        name="start",
    )(
        device,
        jnp.transpose(pair_band, (1, 0, 2)).reshape(keys, cols, block, width),
        atoms,
        tokens,
    )
    band = lax.all_to_all(tiles, "col", 0, 0, tiled=True).reshape(entries, width)

    first = lax.ppermute(first, ("row", "col"), pairs)
    second = lax.ppermute(second, ("row", "col"), odd_pairs)

    table, pair_norm, kept_gain, tokens = pl.pallas_call(
        pair_kernel,
        out_shape=(
            shape((KW, KW), BF),
            shape((entries, width), BF),
            shape(gain.shape, F32),
            shape(tokens.shape, jnp.int32),
        ),
        in_specs=vmem(5),
        out_specs=tuple(vmem(4)),
        cost_estimate=pl.CostEstimate(flops=10**9, bytes_accessed=10**7, transcendentals=0),
        compiler_params=LIMIT,
        name="pair",
    )(band, band_gain, weights, gain, tokens)
    fetched = [atoms, cotangent, project, combine, kept_gain, tokens]
    outgoing, first, second, own_grad = pl.pallas_call(
        attention_kernel,
        out_shape=(
            shape((32, 32, width), BF),
            shape((samples, RIM, width), BF),
            shape((samples, RIM, width), BF),
            shape((samples, count, width), F32),
        ),
        in_specs=smem(2) + anywhere(len(fetched)) + vmem(4),
        out_specs=tuple(vmem(4)),
        scratch_shapes=[
            pltpu.VMEM((windows, KW, KW), F32),
            pltpu.VMEM((windows, KW, KW), F32),
        ]
        + copied(fetched),
        compiler_params=LIMIT,
        name="attention",
    )(key_range, device, *fetched, first, second, table, pair_norm)

    def place(y, z_hi, core, z_lo, x):
        return ((y * 4 + z_hi) * 2 + core) * 16 + z_lo * 4 + x

    four = range(4)
    planes = [
        [place(y, z_hi, core, z_lo, x) for y in four for core in range(2) for x in four]
        for z_hi in four
        for z_lo in four
    ]
    lines = [
        [place(y, z_hi, core, z_lo, x) for z_hi in four for z_lo in four]
        for y in four
        for core in range(2)
        for x in four
    ]
    axes = ("row", "col")
    part = lax.all_to_all(outgoing, axes, 0, 0, axis_index_groups=planes, tiled=True)
    part = pl.pallas_call(
        middle_kernel,
        out_shape=shape((16, 32, width), BF),
        in_specs=smem(1) + vmem(1),
        out_specs=pl.BlockSpec(memory_space=pltpu.VMEM),
        compiler_params=LIMIT,
        name="middle",
    )(device, part)

    part, first, second = lax.optimization_barrier((part, first, second))
    scattered = lax.all_to_all(part, axes, 0, 0, axis_index_groups=lines, tiled=True)
    first = lax.ppermute(first, ("row", "col"), pairs)
    second = lax.ppermute(second, ("row", "col"), odd_pairs)
    part = jnp.sum(scattered[:, :24].astype(F32), axis=0).astype(BF)
    part, first, second = lax.optimization_barrier((part, first, second))
    part = jnp.broadcast_to(part, (32,) + part.shape)
    part = lax.all_to_all(part, axes, 0, 0, axis_index_groups=planes, tiled=True)
    band_grad = pl.pallas_call(
        band_kernel,
        out_shape=shape((entries, width), BF),
        in_specs=smem(1) + vmem(4),
        out_specs=pl.BlockSpec(memory_space=pltpu.VMEM),
        compiler_params=LIMIT,
        name="band",
    )(device, tiles.reshape(entries, width), scattered, band_gain, weights)
    band_grad = jnp.transpose(band_grad.reshape(cols, keys, block, width), (0, 2, 1, 3))
    band_grad = band_grad.reshape(pair_band.shape)
    atoms_grad = pl.pallas_call(
        finish_kernel,
        out_shape=shape(atoms.shape, BF),
        in_specs=smem(1) + vmem(6),
        out_specs=pl.BlockSpec(memory_space=pltpu.VMEM),
        compiler_params=LIMIT,
        name="finish",
    )(device, atoms, cotangent, own_grad, first, second, gain)
    part, atoms_grad, band_grad = lax.optimization_barrier((part, atoms_grad, band_grad))
    fetched = [part, project, gain, band_gain, weights]
    project_grad, combine_grad, weight_grad, scale_grad, gain_grad = pl.pallas_call(
        last_kernel,
        out_shape=(
            shape(project.shape, BF),
            shape(combine.shape, BF),
            shape(weights.shape, BF),
            shape((1, width), F32),
            shape((1, width), F32),
        ),
        in_specs=anywhere(5),
        out_specs=tuple(vmem(5)),
        scratch_shapes=copied(fetched),
        compiler_params=LIMIT,
        name="last",
    )(*fetched)
    return (
        atoms_grad,
        project_grad,
        combine_grad,
        scale_grad.reshape(width),
        band_grad,
        weight_grad.T,
        gain_grad.reshape(width),
    )


def solution(mesh):
    in_specs = (
        P(None, ("row", "col"), None),
        P(None, ("row", "col"), None),
        P(),
        P(),
        P(),
        P("row", "col", None),
        P(),
        P(),
        P(("row", "col")),
        P(("row", "col"), None),
    )
    out_specs = (P(None, ("row", "col"), None), P(), P(), P(), P("row", "col", None), P(), P())
    return jax.shard_map(shards, mesh=mesh, in_specs=in_specs, out_specs=out_specs, check_vma=False)
```

```python
import math

import jax
import jax.numpy as jnp
from jax import lax
from jax.experimental import pallas as pl
from jax.experimental.pallas import tpu as pltpu
from jax.sharding import PartitionSpec as P

QW = 32
KW = 128
RIM = 48
EPSILON = 1e-05
NEG_FILL = -1e30
F32 = jnp.float32
BF = jnp.bfloat16


LIMIT = pltpu.CompilerParams(vmem_limit_bytes=16 * 1024 * 1024)


def nn(a, b):
    return lax.dot_general(a, b, (((1,), (0,)), ((), ())), preferred_element_type=F32)


def nt(a, b):
    return lax.dot_general(a, b, (((1,), (1,)), ((), ())), preferred_element_type=F32)


def tn(a, b):
    return lax.dot_general(a, b, (((0,), (0,)), ((), ())), preferred_element_type=F32)


def split2(x):
    high = x.astype(BF)
    return high, (x - high.astype(F32)).astype(BF)


def norm(v):
    mean = jnp.mean(v, axis=-1, keepdims=True)
    centred = v - mean
    inv = lax.rsqrt(jnp.mean(centred * centred, axis=-1, keepdims=True) + EPSILON)
    return centred * inv, inv


def norm_back(g, hat, inv):
    first = jnp.mean(g, axis=-1, keepdims=True)
    second = jnp.mean(g * hat, axis=-1, keepdims=True)
    return inv * (g - first - hat * second)


def iota(shape, dim):
    return lax.broadcasted_iota(jnp.int32, shape, dim)


def fetch(pairs, sems):
    copies = [pltpu.make_async_copy(src, dst, sems.at[n]) for n, (src, dst) in enumerate(pairs)]
    for copy in copies:
        copy.start()
    return copies


def start_kernel(device, band, atoms, tokens, tiles, first, second, line, sems):
    samples, count, width = atoms.shape
    odd = (device[0] + 1) & 1
    low = pl.multiple_of((1 - odd) * (count - RIM), 16)
    high = pl.multiple_of(odd * (count - RIM), 16)
    copies = fetch(
        [(tokens, line)]
        + [(band.at[k], tiles.at[:, k]) for k in range(band.shape[0])]
        + [
            (atoms.at[:, pl.ds(low, RIM)], first.at[:samples]),
            (atoms.at[:, pl.ds(high, RIM)], second.at[:samples]),
        ],
        sems,
    )
    copies[0].wait()
    local = jnp.broadcast_to((line[...] - device[0] * 16).astype(F32), (RIM, width)).astype(BF)
    first[samples] = local
    second[samples] = local
    for copy in copies[1:]:
        copy.wait()


def weight_lines(weights):
    rows = weights[...].astype(F32)
    return jnp.concatenate([rows, jnp.zeros((16 - rows.shape[0], rows.shape[1]), F32)], axis=0)


def weight_spread(weights):
    rows = weights[...].astype(F32)
    rows = [jnp.broadcast_to(rows[h : h + 1], (16, rows.shape[1])) for h in range(4)]
    return jnp.concatenate(rows * 2, axis=0).astype(BF)


def spread_slots(entries):
    hit = (iota((entries, KW), 0) >> 4) == iota((entries, KW), 1)
    return jnp.where(hit, 1.0, 0.0).astype(BF)


def entry_grads(table_grad, entries):
    grad = nn(spread_slots(entries), table_grad)
    column = iota((entries, KW), 1)
    shown = ((iota((entries, KW), 0) & 15) == (column & 15)) & (column < 64)
    return jnp.where(shown, grad, 0.0).astype(BF)


def keep_kernel(*refs):
    half = len(refs) // 2
    for source, kept in zip(refs[:half], refs[half:]):
        kept[...] = source[...]


def pair_kernel(band, gain, weights, table, pair_norm):
    heads = 4
    entries = band.shape[0]
    hat, _ = norm(band[...].astype(F32))
    normed = (hat * gain[...]).astype(BF)
    pair_norm[...] = normed
    bias_rows = nt(weight_lines(weights).astype(BF), normed)
    stacked = jnp.concatenate(
        [jnp.broadcast_to(bias_rows[h : h + 1], (16, entries)) for h in range(heads)], axis=0
    )
    own_token = (iota((64, entries), 0) & 15) == (iota((64, entries), 1) & 15)
    high, low = split2(jnp.where(own_token, stacked, 0.0))
    both = jnp.concatenate([high, low], axis=0)
    table[...] = nn(both, spread_slots(entries)).astype(BF)


def middle_kernel(device, scattered, outgoing):
    width = scattered.shape[2]
    total = scattered[0].astype(F32)
    for p in range(1, scattered.shape[0]):
        total = total + scattered[p].astype(F32)
    first = ((device[0] >> 7) & 3) * 8 + ((device[0] >> 4) & 1) * 4
    blocks = [scattered[first + x].astype(F32)[24:32] for x in range(4)]
    turned = [pltpu.roll(b, 64, 1) for b in blocks]
    left = iota((8, width), 1) < 64
    for z_lo in range(4):
        rows = slice(3 * (z_lo // 2), 3 * (z_lo // 2) + 3)
        lows, highs = (blocks, turned) if z_lo % 2 == 0 else (turned, blocks)
        pairs = [jnp.where(left, lows[x], highs[x + 1])[rows] for x in (0, 2)]
        tables = pairs + [jnp.zeros((2, width), F32)]
        result = jnp.concatenate([total[:24]] + tables, axis=0).astype(BF)
        for z_hi in range(4):
            outgoing[z_hi * 4 + z_lo] = result


def band_kernel(device, band, scattered, pair_gain, weights, band_grad):
    entries = band.shape[0]
    width = band.shape[1]
    z_hi = (device[0] >> 5) & 3
    rows = []
    for z_lo in range(4):
        block = scattered[z_hi * 4 + z_lo].astype(F32)[24:32]
        turned = pltpu.roll(block, 64, 1)
        rows = rows + [block[:3], turned[:3], block[3:6], turned[3:6]]
    rows = jnp.concatenate(rows + [jnp.zeros((KW - 48, width), F32)], axis=0).astype(BF)
    hat, inv = norm(band[...].astype(F32))
    norm_grad = nn(entry_grads(rows, entries), weight_spread(weights)).astype(BF).astype(F32)
    result = norm_back(norm_grad * pair_gain[...], hat, inv).astype(BF)
    slots = band_grad.shape[0]
    for n in range(entries // 16):
        block, slot = divmod(n, slots)
        band_grad[slot, 16 * block : 16 * block + 16, :] = result[16 * n : 16 * n + 16]


def attention_kernel(
    key_range,
    device,
    atoms,
    cotangent,
    project,
    combine,
    atom_gain,
    tokens,
    first,
    second,
    table,
    pair_norm,
    outgoing,
    to_first,
    to_second,
    own_grad,
    bias,
    bias_grad,
):
    samples, count, width = atoms.shape
    heads = 4
    windows = count // QW
    entries = pair_norm.shape[0]
    scale = 1.0 / math.sqrt(width // heads)
    lane = iota((KW, KW), 1)
    line = iota((KW, KW), 0)

    own = jnp.broadcast_to((tokens[...] - device[0] * 16).astype(F32), (8, KW))
    odd = (device[0] & 1) == 0

    def sides(x, y):
        return jnp.where(odd, x, y), jnp.where(odd, y, x)

    left, right = sides(first[samples].astype(F32), second[samples].astype(F32))
    left = left[:8] - 16.0
    right = right[:8] + 16.0
    row_lane = iota((8, KW), 1)
    turned = [own] + [pltpu.roll(own, h * QW, 1) for h in range(1, heads)]

    def query_row(w):
        row = turned[(-w) % heads]
        for h in range(1, heads):
            row = jnp.where((row_lane >> 5) == h, turned[(h - w) % heads], row)
        return row.astype(jnp.int32)[:1]

    def key_row(w):
        shift = RIM - w * QW
        one, two = (left, own) if shift > 0 else (own, right)
        shift = shift % KW
        row = jnp.where(row_lane < shift, pltpu.roll(one, shift, 1), pltpu.roll(two, shift, 1))
        return row.astype(jnp.int32)[:1] + 16

    def query_hot(w):
        hit = ((line & 15) == query_row(w)) & (((line >> 4) & 3) == (lane >> 5))
        return jnp.where(hit, 1.0, 0.0).astype(BF)

    def key_hot(w):
        return jnp.where(line == key_row(w), 1.0, 0.0).astype(BF)

    for w in range(windows):
        by_key = nn(table[...], key_hot(w)).astype(BF)
        values = tn(by_key, query_hot(w))
        begin = device[0] * count - RIM + w * QW
        allowed = (line >= key_range[w, 0] - begin) & (line < key_range[w, 1] - begin)
        bias[w] = jnp.where(allowed, values, NEG_FILL)
        bias_grad[w] = jnp.zeros((KW, KW), F32)
    gain = atom_gain[...]
    diag = jnp.where((line >> 5) == (lane >> 5), 1.0, 0.0).astype(BF)
    head_of = iota((QW, width), 1) >> 5

    def spread_heads(x):
        return jnp.concatenate([x] * heads, axis=0) * diag

    def gather_heads(x):
        total = x[:QW]
        for h in range(1, heads):
            total = jnp.where(head_of == h, x[h * QW : (h + 1) * QW], total)
        return total

    def overlap(parts):
        sums = []
        for m in range(windows + KW // QW - 1):
            total = None
            for w in range(windows):
                if 0 <= m - w < KW // QW:
                    term = parts[w][(m - w) * QW : (m - w + 1) * QW]
                    total = term if total is None else total + term
            sums.append(total)
        return jnp.concatenate(sums, axis=0).astype(BF)

    def sample(s, carry):
        project_sum, combine_sum = carry
        before, after = sides(first[s].astype(F32), second[s].astype(F32))
        x = jnp.concatenate([before, atoms[s].astype(F32), after], axis=0)
        x_hat, _ = norm(x)
        normed = (x_hat * gain).astype(BF)
        projected = nn(normed, project[...]).astype(BF)
        query = projected[RIM : RIM + count, :width]
        key = projected[:, width : 2 * width]
        value = projected[:, 2 * width : 3 * width]
        gate = projected[RIM : RIM + count, 3 * width :].astype(F32)
        out = cotangent[s]
        sigmoid = jax.nn.sigmoid(gate)
        gated_grad = nt(out, combine[...]).astype(BF).astype(F32)
        mixture_grad = (gated_grad * sigmoid).astype(BF)
        span = range(windows)
        q = [spread_heads(query[w * QW : (w + 1) * QW]) for w in span]
        g = [spread_heads(mixture_grad[w * QW : (w + 1) * QW]) for w in span]
        k = [key[w * QW : w * QW + KW] for w in span]
        v = [value[w * QW : w * QW + KW] for w in span]
        scores = [nt(k[w], q[w]) * scale + bias[w] for w in span]
        weights_grad = [nt(v[w], g[w]).astype(BF).astype(F32) for w in span]
        scores = [jnp.exp(x - jnp.max(x, axis=0, keepdims=True)) for x in scores]
        weights = [x * (1.0 / jnp.sum(x, axis=0, keepdims=True)) for x in scores]
        low = [x.astype(BF) for x in weights]
        mixture = jnp.concatenate([gather_heads(tn(low[w], v[w])) for w in span], axis=0)
        row_dot = [jnp.sum(weights[w] * weights_grad[w], axis=0, keepdims=True) for w in span]
        score_grad = [weights[w] * (weights_grad[w] - row_dot[w]) for w in span]
        for w in span:
            bias_grad[w] += score_grad[w]
        score_low = [(x * scale).astype(BF) for x in score_grad]
        query_grads = [gather_heads(tn(score_low[w], k[w])).astype(BF) for w in span]
        key_grad = overlap([nn(score_low[w], q[w]) for w in span])
        value_grad = overlap([nn(low[w], g[w]) for w in span])
        gated = (mixture * sigmoid).astype(BF)
        combine_sum = combine_sum + tn(gated, out)
        gate_grad = (gated_grad * mixture * sigmoid * (1.0 - sigmoid)).astype(BF)
        rim = jnp.zeros((RIM, width), BF)
        query_cols = jnp.concatenate([rim] + query_grads + [rim], axis=0)
        gate_cols = jnp.concatenate([rim, gate_grad, rim], axis=0)
        grad = jnp.concatenate([query_cols, key_grad, value_grad, gate_cols], axis=1)
        project_sum = project_sum + tn(normed, grad)
        normed_grad = nt(grad, project[...])
        before, after = sides(normed_grad[:RIM], normed_grad[RIM + count :])
        to_first[s] = before.astype(BF)
        to_second[s] = after.astype(BF)
        own_grad[s] = normed_grad[RIM : RIM + count]
        return project_sum, combine_sum

    start = (
        jnp.zeros((width, 4 * width), F32),
        jnp.zeros((width, width), F32),
    )
    project_sum, combine_sum = lax.fori_loop(0, samples, sample, start, unroll=True)

    table_grad = jnp.zeros((KW, KW), F32)
    for w in range(windows):
        high, low = split2(bias_grad[w])
        hot = key_hot(w)
        by_slot = nn(hot, high) + nn(hot, low)
        high, low = split2(by_slot)
        rows = query_hot(w)
        table_grad = table_grad + nt(high, rows) + nt(low, rows)
    spread = iota((KW, entries), 0) == (iota((KW, entries), 1) >> 4)
    spread = jnp.where(spread, 1.0, 0.0).astype(BF)
    entry_grad = tn(table_grad.astype(BF), spread)
    shown = (iota((KW, entries), 0) & 15) == (iota((KW, entries), 1) & 15)
    entry_grad = jnp.where(shown, entry_grad, 0.0).astype(BF)
    weight_part = nn(entry_grad, pair_norm[...])
    left = iota((3, width), 1) < 64
    tables = []
    for x in range(4):
        by_z = [table_grad[3 * (4 * z + x) : 3 * (4 * z + x) + 3] for z in range(4)]
        pairs = [jnp.where(left, by_z[z], by_z[z + 1]) for z in (0, 2)]
        tables.append(jnp.concatenate(pairs + [jnp.zeros((2, width), F32)], axis=0))
    peers = outgoing.shape[0]
    for p in range(peers):
        part, row = divmod(16 * p, width)
        weight_row = jnp.zeros((1, width), F32)
        if p < heads:
            weight_row = jnp.sum(weight_part[p * 16 : (p + 1) * 16], axis=0, keepdims=True)
        parts = [
            project_sum[row : row + 16, part * width : (part + 1) * width],
            combine_sum[4 * p : 4 * p + 4],
            weight_row,
            jnp.zeros((3, width), F32),
            tables[p % 4],
        ]
        outgoing[p] = jnp.concatenate(parts, axis=0).astype(BF)


def last_kernel(
    parts,
    project,
    atom_gain,
    pair_gain,
    weights,
    project_grad,
    combine_grad,
    weight_grad,
    scale_grad,
    gain_grad,
):
    chunks = [parts[p].astype(F32) for p in range(parts.shape[0])]
    rows = jnp.concatenate([x[:16] for x in chunks], axis=0)
    width = rows.shape[1]
    dots = jnp.zeros((width, 1), F32)
    for part in range(4):
        columns = slice(part * width, (part + 1) * width)
        block = rows[part * width : (part + 1) * width]
        project_grad[:, columns] = block.astype(BF)
        dots = dots + jnp.sum(block * project[:, columns].astype(F32), axis=1, keepdims=True)
    combine_grad[...] = jnp.concatenate([x[16:20] for x in chunks], axis=0).astype(BF)
    dots = jnp.transpose(jnp.broadcast_to(dots, (width, width)))[:1]
    scale_grad[...] = dots / atom_gain[...]
    tail = jnp.concatenate([x[20:21] for x in chunks[:4]], axis=0)
    weight_grad[...] = tail.astype(BF)
    dots = jnp.sum(tail * weights[...].astype(F32), axis=0, keepdims=True)
    gain_grad[...] = dots / pair_gain[...]


def finish_kernel(device, atoms, cotangent, own_grad, first, second, atom_gain, result):
    samples, count, width = atoms.shape
    odd = (device[0] & 1) == 0
    gain = atom_gain[...]
    for s in range(samples):
        x_hat, inv = norm(atoms[s].astype(F32))
        rim = jnp.zeros((count - RIM, width), F32)
        one, two = first[s].astype(F32), second[s].astype(F32)
        total = own_grad[s] + jnp.concatenate([jnp.where(odd, one, two), rim], axis=0)
        total = total + jnp.concatenate([rim, jnp.where(odd, two, one)], axis=0)
        g = total.astype(BF).astype(F32) * gain
        result[s] = (cotangent[s].astype(F32) + norm_back(g, x_hat, inv)).astype(BF)


def vmem(n):
    return [pl.BlockSpec(memory_space=pltpu.VMEM)] * n


def smem(n):
    return [pl.BlockSpec(memory_space=pltpu.SMEM)] * n


def anywhere(n):
    return [pl.BlockSpec(memory_space=pl.ANY)] * n


def shards(
    atoms,
    cotangent,
    project,
    combine,
    atom_gain,
    pair_band,
    pair_gain,
    pair_weight,
    atom_token,
    key_range,
):
    samples, count, width = atoms.shape
    cols = lax.axis_size("col")
    peers = lax.axis_size("row") * cols
    device = lax.axis_index(("row", "col"))
    windows = count // QW
    block = pair_band.shape[0] // cols
    keys = pair_band.shape[1]
    pairs = [(i + j, i + 1 - j) for i in range(1, peers - 1, 2) for j in range(2)]
    odd_pairs = [(i, i ^ 1) for i in range(peers)]

    shape = jax.ShapeDtypeStruct

    shape = jax.ShapeDtypeStruct
    device = device.astype(jnp.int32).reshape(1)
    tokens = atom_token.reshape(1, count)
    weights = pair_weight.T
    gain = atom_gain.reshape(1, width)
    band_gain = pair_gain.reshape(1, width)

    entries = cols * keys * block
    tiles, first, second = pl.pallas_call(
        start_kernel,
        out_shape=(
            shape((cols, keys, block, width), BF),
            shape((samples + 1, RIM, width), BF),
            shape((samples + 1, RIM, width), BF),
        ),
        in_specs=smem(1) + anywhere(3),
        out_specs=tuple(vmem(3)),
        scratch_shapes=[
            pltpu.VMEM((1, count), jnp.int32),
            pltpu.SemaphoreType.DMA((3 + keys,)),
        ],
        compiler_params=pltpu.CompilerParams(vmem_limit_bytes=60 * 1024 * 1024),
        name="start",
    )(
        device,
        jnp.transpose(pair_band, (1, 0, 2)).reshape(keys, cols, block, width),
        atoms,
        tokens,
    )
    band = lax.all_to_all(tiles, "col", 0, 0, tiled=True).reshape(entries, width)

    first = lax.ppermute(first, ("row", "col"), pairs)
    second = lax.ppermute(second, ("row", "col"), odd_pairs)

    small = [band_gain, weights, gain, tokens]
    band_gain, weights, gain, tokens = pl.pallas_call(
        keep_kernel,
        out_shape=tuple(shape(x.shape, x.dtype) for x in small),
        in_specs=vmem(4),
        out_specs=tuple(vmem(4)),
        compiler_params=LIMIT,
        name="keep",
    )(*small)
    table, pair_norm = pl.pallas_call(
        pair_kernel,
        out_shape=(shape((KW, KW), BF), shape((entries, width), BF)),
        in_specs=vmem(3),
        out_specs=tuple(vmem(2)),
        cost_estimate=pl.CostEstimate(flops=10**9, bytes_accessed=10**7, transcendentals=0),
        compiler_params=LIMIT,
        name="pair",
    )(band, band_gain, weights)
    outgoing, first, second, own_grad = pl.pallas_call(
        attention_kernel,
        out_shape=(
            shape((32, 32, width), BF),
            shape((samples, RIM, width), BF),
            shape((samples, RIM, width), BF),
            shape((samples, count, width), F32),
        ),
        in_specs=smem(2) + vmem(10),
        out_specs=tuple(vmem(4)),
        scratch_shapes=[
            pltpu.VMEM((windows, KW, KW), F32),
            pltpu.VMEM((windows, KW, KW), F32),
        ],
        compiler_params=LIMIT,
        name="attention",
    )(
        key_range,
        device,
        atoms,
        cotangent,
        project,
        combine,
        gain,
        tokens,
        first,
        second,
        table,
        pair_norm,
    )

    def place(y, z_hi, core, z_lo, x):
        return ((y * 4 + z_hi) * 2 + core) * 16 + z_lo * 4 + x

    four = range(4)
    planes = [
        [place(y, z_hi, core, z_lo, x) for y in four for core in range(2) for x in four]
        for z_hi in four
        for z_lo in four
    ]
    lines = [
        [place(y, z_hi, core, z_lo, x) for z_hi in four for z_lo in four]
        for y in four
        for core in range(2)
        for x in four
    ]
    axes = ("row", "col")
    part = lax.all_to_all(outgoing, axes, 0, 0, axis_index_groups=planes, tiled=True)
    part = pl.pallas_call(
        middle_kernel,
        out_shape=shape((16, 32, width), BF),
        in_specs=smem(1) + vmem(1),
        out_specs=pl.BlockSpec(memory_space=pltpu.VMEM),
        compiler_params=LIMIT,
        name="middle",
    )(device, part)

    part, first, second = lax.optimization_barrier((part, first, second))
    scattered = lax.all_to_all(part, axes, 0, 0, axis_index_groups=lines, tiled=True)
    first = lax.ppermute(first, ("row", "col"), pairs)
    second = lax.ppermute(second, ("row", "col"), odd_pairs)
    part = jnp.sum(scattered[:, :24].astype(F32), axis=0).astype(BF)
    part, first, second = lax.optimization_barrier((part, first, second))
    part = jnp.broadcast_to(part, (32,) + part.shape)
    part = lax.all_to_all(part, axes, 0, 0, axis_index_groups=planes, tiled=True)
    band_grad = pl.pallas_call(
        band_kernel,
        out_shape=shape((keys, cols * block, width), BF),
        in_specs=smem(1) + vmem(4),
        out_specs=pl.BlockSpec(memory_space=pltpu.VMEM),
        compiler_params=LIMIT,
        name="band",
    )(device, tiles.reshape(entries, width), scattered, band_gain, weights)
    band_grad = jnp.transpose(band_grad, (1, 0, 2))
    atoms_grad = pl.pallas_call(
        finish_kernel,
        out_shape=shape(atoms.shape, BF),
        in_specs=smem(1) + vmem(6),
        out_specs=pl.BlockSpec(memory_space=pltpu.VMEM),
        compiler_params=LIMIT,
        name="finish",
    )(device, atoms, cotangent, own_grad, first, second, gain)
    part, atoms_grad, band_grad = lax.optimization_barrier((part, atoms_grad, band_grad))
    project_grad, combine_grad, weight_grad, scale_grad, gain_grad = pl.pallas_call(
        last_kernel,
        out_shape=(
            shape(project.shape, BF),
            shape(combine.shape, BF),
            shape(weights.shape, BF),
            shape((1, width), F32),
            shape((1, width), F32),
        ),
        in_specs=vmem(5),
        out_specs=tuple(vmem(5)),
        compiler_params=LIMIT,
        name="last",
    )(part, project, gain, band_gain, weights)
    return (
        atoms_grad,
        project_grad,
        combine_grad,
        scale_grad.reshape(width),
        band_grad,
        weight_grad.T,
        gain_grad.reshape(width),
    )


def solution(mesh):
    in_specs = (
        P(None, ("row", "col"), None),
        P(None, ("row", "col"), None),
        P(),
        P(),
        P(),
        P("row", "col", None),
        P(),
        P(),
        P(("row", "col")),
        P(("row", "col"), None),
    )
    out_specs = (P(None, ("row", "col"), None), P(), P(), P(), P("row", "col", None), P(), P())
    return jax.shard_map(shards, mesh=mesh, in_specs=in_specs, out_specs=out_specs, check_vma=False)
```

```python
import math

import jax
import jax.numpy as jnp
from jax import lax
from jax.experimental import pallas as pl
from jax.experimental.pallas import tpu as pltpu
from jax.sharding import PartitionSpec as P

QW = 32
KW = 128
RIM = 48
EPSILON = 1e-05
NEG_FILL = -1e30
F32 = jnp.float32
BF = jnp.bfloat16


LIMIT = pltpu.CompilerParams(vmem_limit_bytes=16 * 1024 * 1024)


def nn(a, b):
    return lax.dot_general(a, b, (((1,), (0,)), ((), ())), preferred_element_type=F32)


def nt(a, b):
    return lax.dot_general(a, b, (((1,), (1,)), ((), ())), preferred_element_type=F32)


def tn(a, b):
    return lax.dot_general(a, b, (((0,), (0,)), ((), ())), preferred_element_type=F32)


def split2(x):
    high = x.astype(BF)
    return high, (x - high.astype(F32)).astype(BF)


def norm(v):
    mean = jnp.mean(v, axis=-1, keepdims=True)
    centred = v - mean
    inv = lax.rsqrt(jnp.mean(centred * centred, axis=-1, keepdims=True) + EPSILON)
    return centred * inv, inv


def norm_back(g, hat, inv):
    first = jnp.mean(g, axis=-1, keepdims=True)
    second = jnp.mean(g * hat, axis=-1, keepdims=True)
    return inv * (g - first - hat * second)


def iota(shape, dim):
    return lax.broadcasted_iota(jnp.int32, shape, dim)


def fetch(pairs, sems):
    copies = [pltpu.make_async_copy(src, dst, sems.at[n]) for n, (src, dst) in enumerate(pairs)]
    for copy in copies:
        copy.start()
    return copies


def split3(x):
    high = x.astype(BF).astype(F32)
    middle = (x - high).astype(BF).astype(F32)
    return [high, middle, x - high - middle]


def small(sent):
    block = sent[sent.shape[0] - 1].astype(F32)
    atom_gain = block[20:21] + block[21:22] + block[22:23]
    pair_gain = block[23:24] + block[24:25] + block[25:26]
    return block[:1], block[16:20], atom_gain, pair_gain


def start_kernel(
    device,
    band,
    atoms,
    tokens,
    weights_hbm,
    atom_gain_hbm,
    pair_gain_hbm,
    tiles,
    first,
    second,
    line,
    weights,
    atom_gain,
    pair_gain,
    sems,
):
    samples, count, width = atoms.shape
    odd = (device[0] + 1) & 1
    low = pl.multiple_of((1 - odd) * (count - RIM), 16)
    high = pl.multiple_of(odd * (count - RIM), 16)
    copies = fetch(
        [
            (tokens, line),
            (weights_hbm, weights),
            (atom_gain_hbm, atom_gain),
            (pair_gain_hbm, pair_gain),
        ]
        + [(band.at[k], tiles.at[:, k]) for k in range(band.shape[0])]
        + [
            (atoms.at[:, pl.ds(low, RIM)], first.at[:samples]),
            (atoms.at[:, pl.ds(high, RIM)], second.at[:samples]),
        ],
        sems,
    )
    for copy in copies[:4]:
        copy.wait()
    local = jnp.broadcast_to((line[...] - device[0] * 16).astype(F32), (16, width))
    rows = [local, weights[...].astype(F32)] + split3(atom_gain[...]) + split3(pair_gain[...])
    block = jnp.concatenate(rows + [jnp.zeros((RIM - 26, width), F32)], axis=0).astype(BF)
    first[samples] = block
    second[samples] = block
    for copy in copies[4:]:
        copy.wait()


def weight_lines(rows):
    return jnp.concatenate([rows, jnp.zeros((16 - rows.shape[0], rows.shape[1]), F32)], axis=0)


def weight_spread(rows):
    rows = [jnp.broadcast_to(rows[h : h + 1], (16, rows.shape[1])) for h in range(4)]
    return jnp.concatenate(rows * 2, axis=0).astype(BF)


def spread_slots(entries):
    hit = (iota((entries, KW), 0) >> 4) == iota((entries, KW), 1)
    return jnp.where(hit, 1.0, 0.0).astype(BF)


def entry_grads(table_grad, entries):
    grad = nn(spread_slots(entries), table_grad)
    column = iota((entries, KW), 1)
    shown = ((iota((entries, KW), 0) & 15) == (column & 15)) & (column < 64)
    return jnp.where(shown, grad, 0.0).astype(BF)


def pair_kernel(band, sent, table, pair_norm):
    heads = 4
    entries = band.shape[0]
    _, weights, _, gain = small(sent)
    hat, _ = norm(band[...].astype(F32))
    normed = (hat * gain).astype(BF)
    pair_norm[...] = normed
    bias_rows = nt(weight_lines(weights).astype(BF), normed)
    stacked = jnp.concatenate(
        [jnp.broadcast_to(bias_rows[h : h + 1], (16, entries)) for h in range(heads)], axis=0
    )
    own_token = (iota((64, entries), 0) & 15) == (iota((64, entries), 1) & 15)
    high, low = split2(jnp.where(own_token, stacked, 0.0))
    both = jnp.concatenate([high, low], axis=0)
    table[...] = nn(both, spread_slots(entries)).astype(BF)


def middle_kernel(device, scattered, outgoing):
    width = scattered.shape[2]
    total = scattered[0].astype(F32)
    for p in range(1, scattered.shape[0]):
        total = total + scattered[p].astype(F32)
    first = ((device[0] >> 7) & 3) * 8 + ((device[0] >> 4) & 1) * 4
    blocks = [scattered[first + x].astype(F32)[24:32] for x in range(4)]
    turned = [pltpu.roll(b, 64, 1) for b in blocks]
    left = iota((8, width), 1) < 64
    for z_lo in range(4):
        rows = slice(3 * (z_lo // 2), 3 * (z_lo // 2) + 3)
        lows, highs = (blocks, turned) if z_lo % 2 == 0 else (turned, blocks)
        pairs = [jnp.where(left, lows[x], highs[x + 1])[rows] for x in (0, 2)]
        tables = pairs + [jnp.zeros((2, width), F32)]
        result = jnp.concatenate([total[:24]] + tables, axis=0).astype(BF)
        for z_hi in range(4):
            outgoing[z_hi * 4 + z_lo] = result


def band_kernel(device, band, scattered, sent, band_grad):
    entries = band.shape[0]
    width = band.shape[1]
    z_hi = (device[0] >> 5) & 3
    rows = []
    for z_lo in range(4):
        block = scattered[z_hi * 4 + z_lo].astype(F32)[24:32]
        turned = pltpu.roll(block, 64, 1)
        rows = rows + [block[:3], turned[:3], block[3:6], turned[3:6]]
    rows = jnp.concatenate(rows + [jnp.zeros((KW - 48, width), F32)], axis=0).astype(BF)
    hat, inv = norm(band[...].astype(F32))
    _, weights, _, pair_gain = small(sent)
    norm_grad = nn(entry_grads(rows, entries), weight_spread(weights)).astype(BF).astype(F32)
    result = norm_back(norm_grad * pair_gain, hat, inv).astype(BF)
    slots = band_grad.shape[0]
    for n in range(entries // 16):
        block, slot = divmod(n, slots)
        band_grad[slot, 16 * block : 16 * block + 16, :] = result[16 * n : 16 * n + 16]


def head_tokens(own, w):
    lane = iota((8, KW), 1)
    row = pltpu.roll(own, (-w % 4) * QW, 1)
    for h in range(1, 4):
        row = jnp.where((lane >> 5) == h, pltpu.roll(own, ((h - w) % 4) * QW, 1), row)
    return row.astype(jnp.int32)[:1]


def query_hot(own, w):
    lane = iota((KW, KW), 1)
    line = iota((KW, KW), 0)
    hit = ((line & 15) == head_tokens(own, w)) & (((line >> 4) & 3) == (lane >> 5))
    return jnp.where(hit, 1.0, 0.0).astype(BF)


def prepare_kernel(
    table, sent, atoms, cotangent, project, combine, rows, normed, projected, gates, gated_grad
):
    samples, count, width = atoms.shape
    tokens, _, gain, _ = small(sent)
    own = jnp.broadcast_to(tokens, (8, KW))
    for w in range(count // QW):
        high, low = split2(tn(table[...], query_hot(own, w)))
        rows[w] = jnp.concatenate([high, low], axis=0)
    for s in range(samples):
        x_hat, _ = norm(atoms[s].astype(F32))
        x = (x_hat * gain).astype(BF)
        normed[s] = x
        columns = nn(x, project[...]).astype(BF)
        projected[s] = columns
        gates[s] = jax.nn.sigmoid(columns[:, 3 * width :].astype(F32))
        gated_grad[s] = nt(cotangent[s], combine[...]).astype(BF)


def attention_kernel(
    key_range,
    device,
    cotangent,
    project,
    sent,
    first,
    second,
    rows,
    normed_own,
    projected_own,
    gates,
    gated_grads,
    pair_norm,
    outgoing,
    to_first,
    to_second,
    own_grad,
    bias,
    bias_grad,
):
    samples, count, width = cotangent.shape
    heads = 4
    windows = count // QW
    entries = pair_norm.shape[0]
    scale = 1.0 / math.sqrt(width // heads)
    lane = iota((KW, KW), 1)
    line = iota((KW, KW), 0)

    tokens, _, gain, _ = small(sent)
    own = jnp.broadcast_to(tokens, (8, KW))
    odd = (device[0] & 1) == 0

    def sides(x, y):
        return jnp.where(odd, x, y), jnp.where(odd, y, x)

    left, right = sides(first[samples].astype(F32), second[samples].astype(F32))
    left = left[:8] - 16.0
    right = right[:8] + 16.0
    row_lane = iota((8, KW), 1)

    def key_row(w):
        shift = RIM - w * QW
        one, two = (left, own) if shift > 0 else (own, right)
        shift = shift % KW
        row = jnp.where(row_lane < shift, pltpu.roll(one, shift, 1), pltpu.roll(two, shift, 1))
        return row.astype(jnp.int32)[:1] + 16

    def key_hot(w):
        return jnp.where(line == key_row(w), 1.0, 0.0).astype(BF)

    for w in range(windows):
        hot = key_hot(w)
        values = tn(jnp.concatenate([hot, hot], axis=0), rows[w])
        begin = device[0] * count - RIM + w * QW
        allowed = (line >= key_range[w, 0] - begin) & (line < key_range[w, 1] - begin)
        bias[w] = jnp.where(allowed, values, NEG_FILL)
        bias_grad[w] = jnp.zeros((KW, KW), F32)
    diag = jnp.where((line >> 5) == (lane >> 5), 1.0, 0.0).astype(BF)
    head_of = iota((QW, width), 1) >> 5

    def spread_heads(x):
        return jnp.concatenate([x] * heads, axis=0) * diag

    def gather_heads(x):
        total = x[:QW]
        for h in range(1, heads):
            total = jnp.where(head_of == h, x[h * QW : (h + 1) * QW], total)
        return total

    def overlap(parts):
        sums = []
        for m in range(windows + KW // QW - 1):
            total = None
            for w in range(windows):
                if 0 <= m - w < KW // QW:
                    term = parts[w][(m - w) * QW : (m - w + 1) * QW]
                    total = term if total is None else total + term
            sums.append(total)
        return jnp.concatenate(sums, axis=0).astype(BF)

    def sample(s, carry):
        project_sum, combine_sum = carry
        before, after = sides(first[s].astype(F32), second[s].astype(F32))
        x_hat, _ = norm(jnp.concatenate([before, after], axis=0))
        rims = (x_hat * gain).astype(BF)
        columns = nn(rims, project[:, width : 3 * width]).astype(BF)
        own_columns = projected_own[s]
        normed = jnp.concatenate([rims[:RIM], normed_own[s], rims[RIM:]], axis=0)
        query = own_columns[:, :width]
        key, value = [
            jnp.concatenate(
                [
                    columns[:RIM, n * width : (n + 1) * width],
                    own_columns[:, (n + 1) * width : (n + 2) * width],
                    columns[RIM:, n * width : (n + 1) * width],
                ],
                axis=0,
            )
            for n in range(2)
        ]
        out = cotangent[s]
        sigmoid = gates[s]
        gated_grad = gated_grads[s].astype(F32)
        mixture_grad = (gated_grad * sigmoid).astype(BF)
        span = range(windows)
        q = [spread_heads(query[w * QW : (w + 1) * QW]) for w in span]
        g = [spread_heads(mixture_grad[w * QW : (w + 1) * QW]) for w in span]
        k = [key[w * QW : w * QW + KW] for w in span]
        v = [value[w * QW : w * QW + KW] for w in span]
        scores = [nt(k[w], q[w]) * scale + bias[w] for w in span]
        weights_grad = [nt(v[w], g[w]).astype(BF).astype(F32) for w in span]
        scores = [jnp.exp(x - jnp.max(x, axis=0, keepdims=True)) for x in scores]
        weights = [x * (1.0 / jnp.sum(x, axis=0, keepdims=True)) for x in scores]
        low = [x.astype(BF) for x in weights]
        mixture = jnp.concatenate([gather_heads(tn(low[w], v[w])) for w in span], axis=0)
        row_dot = [jnp.sum(weights[w] * weights_grad[w], axis=0, keepdims=True) for w in span]
        score_grad = [weights[w] * (weights_grad[w] - row_dot[w]) for w in span]
        for w in span:
            bias_grad[w] += score_grad[w]
        score_low = [(x * scale).astype(BF) for x in score_grad]
        query_grads = [gather_heads(tn(score_low[w], k[w])).astype(BF) for w in span]
        key_grad = overlap([nn(score_low[w], q[w]) for w in span])
        value_grad = overlap([nn(low[w], g[w]) for w in span])
        gated = (mixture * sigmoid).astype(BF)
        combine_sum = combine_sum + tn(gated, out)
        gate_grad = (gated_grad * mixture * sigmoid * (1.0 - sigmoid)).astype(BF)
        rim = jnp.zeros((RIM, width), BF)
        query_cols = jnp.concatenate([rim] + query_grads + [rim], axis=0)
        gate_cols = jnp.concatenate([rim, gate_grad, rim], axis=0)
        grad = jnp.concatenate([query_cols, key_grad, value_grad, gate_cols], axis=1)
        project_sum = project_sum + tn(normed, grad)
        normed_grad = nt(grad, project[...])
        before, after = sides(normed_grad[:RIM], normed_grad[RIM + count :])
        to_first[s] = before.astype(BF)
        to_second[s] = after.astype(BF)
        own_grad[s] = normed_grad[RIM : RIM + count]
        return project_sum, combine_sum

    start = (
        jnp.zeros((width, 4 * width), F32),
        jnp.zeros((width, width), F32),
    )
    project_sum, combine_sum = lax.fori_loop(0, samples, sample, start, unroll=True)

    table_grad = jnp.zeros((KW, KW), F32)
    for w in range(windows):
        high, low = split2(bias_grad[w])
        hot = key_hot(w)
        by_slot = nn(hot, high) + nn(hot, low)
        high, low = split2(by_slot)
        queries = query_hot(own, w)
        table_grad = table_grad + nt(high, queries) + nt(low, queries)
    spread = iota((KW, entries), 0) == (iota((KW, entries), 1) >> 4)
    spread = jnp.where(spread, 1.0, 0.0).astype(BF)
    entry_grad = tn(table_grad.astype(BF), spread)
    shown = (iota((KW, entries), 0) & 15) == (iota((KW, entries), 1) & 15)
    entry_grad = jnp.where(shown, entry_grad, 0.0).astype(BF)
    weight_part = nn(entry_grad, pair_norm[...])
    left = iota((3, width), 1) < 64
    tables = []
    for x in range(4):
        by_z = [table_grad[3 * (4 * z + x) : 3 * (4 * z + x) + 3] for z in range(4)]
        pairs = [jnp.where(left, by_z[z], by_z[z + 1]) for z in (0, 2)]
        tables.append(jnp.concatenate(pairs + [jnp.zeros((2, width), F32)], axis=0))
    peers = outgoing.shape[0]
    for p in range(peers):
        part, row = divmod(16 * p, width)
        weight_row = jnp.zeros((1, width), F32)
        if p < heads:
            weight_row = jnp.sum(weight_part[p * 16 : (p + 1) * 16], axis=0, keepdims=True)
        parts = [
            project_sum[row : row + 16, part * width : (part + 1) * width],
            combine_sum[4 * p : 4 * p + 4],
            weight_row,
            jnp.zeros((3, width), F32),
            tables[p % 4],
        ]
        outgoing[p] = jnp.concatenate(parts, axis=0).astype(BF)


def last_kernel(
    parts,
    project,
    sent,
    project_grad,
    combine_grad,
    weight_grad,
    scale_grad,
    gain_grad,
):
    _, weights, atom_gain, pair_gain = small(sent)
    chunks = [parts[p].astype(F32) for p in range(parts.shape[0])]
    rows = jnp.concatenate([x[:16] for x in chunks], axis=0)
    width = rows.shape[1]
    dots = jnp.zeros((width, 1), F32)
    for part in range(4):
        columns = slice(part * width, (part + 1) * width)
        block = rows[part * width : (part + 1) * width]
        project_grad[:, columns] = block.astype(BF)
        dots = dots + jnp.sum(block * project[:, columns].astype(F32), axis=1, keepdims=True)
    combine_grad[...] = jnp.concatenate([x[16:20] for x in chunks], axis=0).astype(BF)
    dots = jnp.transpose(jnp.broadcast_to(dots, (width, width)))[:1]
    scale_grad[...] = dots / atom_gain
    tail = jnp.concatenate([x[20:21] for x in chunks[:4]], axis=0)
    weight_grad[...] = tail.astype(BF)
    dots = jnp.sum(tail * weights, axis=0, keepdims=True)
    gain_grad[...] = dots / pair_gain


def finish_kernel(device, atoms, cotangent, own_grad, first, second, sent, result):
    samples, count, width = atoms.shape
    odd = (device[0] & 1) == 0
    _, _, gain, _ = small(sent)
    for s in range(samples):
        x_hat, inv = norm(atoms[s].astype(F32))
        rim = jnp.zeros((count - RIM, width), F32)
        one, two = first[s].astype(F32), second[s].astype(F32)
        total = own_grad[s] + jnp.concatenate([jnp.where(odd, one, two), rim], axis=0)
        total = total + jnp.concatenate([rim, jnp.where(odd, two, one)], axis=0)
        g = total.astype(BF).astype(F32) * gain
        result[s] = (cotangent[s].astype(F32) + norm_back(g, x_hat, inv)).astype(BF)


def vmem(n):
    return [pl.BlockSpec(memory_space=pltpu.VMEM)] * n


def smem(n):
    return [pl.BlockSpec(memory_space=pltpu.SMEM)] * n


def anywhere(n):
    return [pl.BlockSpec(memory_space=pl.ANY)] * n


def shards(
    atoms,
    cotangent,
    project,
    combine,
    atom_gain,
    pair_band,
    pair_gain,
    pair_weight,
    atom_token,
    key_range,
):
    samples, count, width = atoms.shape
    cols = lax.axis_size("col")
    peers = lax.axis_size("row") * cols
    device = lax.axis_index(("row", "col"))
    windows = count // QW
    block = pair_band.shape[0] // cols
    keys = pair_band.shape[1]
    pairs = [(i + j, i + 1 - j) for i in range(1, peers - 1, 2) for j in range(2)]
    odd_pairs = [(i, i ^ 1) for i in range(peers)]

    shape = jax.ShapeDtypeStruct

    shape = jax.ShapeDtypeStruct
    device = device.astype(jnp.int32).reshape(1)
    tokens = atom_token.reshape(1, count)
    weights = pair_weight.T
    gain = atom_gain.reshape(1, width)
    band_gain = pair_gain.reshape(1, width)

    entries = cols * keys * block
    tiles, first, sent = pl.pallas_call(
        start_kernel,
        out_shape=(
            shape((cols, keys, block, width), BF),
            shape((samples + 1, RIM, width), BF),
            shape((samples + 1, RIM, width), BF),
        ),
        in_specs=smem(1) + anywhere(6),
        out_specs=tuple(vmem(3)),
        scratch_shapes=[
            pltpu.VMEM((1, count), jnp.int32),
            pltpu.VMEM(weights.shape, BF),
            pltpu.VMEM(gain.shape, F32),
            pltpu.VMEM(band_gain.shape, F32),
            pltpu.SemaphoreType.DMA((6 + keys,)),
        ],
        compiler_params=pltpu.CompilerParams(vmem_limit_bytes=60 * 1024 * 1024),
        name="start",
    )(
        device,
        jnp.transpose(pair_band, (1, 0, 2)).reshape(keys, cols, block, width),
        atoms,
        tokens,
        weights,
        gain,
        band_gain,
    )
    band = lax.all_to_all(tiles, "col", 0, 0, tiled=True).reshape(entries, width)

    first = lax.ppermute(first, ("row", "col"), pairs)
    second = lax.ppermute(sent, ("row", "col"), odd_pairs)

    table, pair_norm = pl.pallas_call(
        pair_kernel,
        out_shape=(shape((KW, KW), BF), shape((entries, width), BF)),
        in_specs=vmem(2),
        out_specs=tuple(vmem(2)),
        cost_estimate=pl.CostEstimate(flops=10**9, bytes_accessed=10**7, transcendentals=0),
        compiler_params=LIMIT,
        name="pair",
    )(band, sent)
    rows, normed, projected, gates, gated_grads = pl.pallas_call(
        prepare_kernel,
        out_shape=(
            shape((windows, 2 * KW, KW), BF),
            shape((samples, count, width), BF),
            shape((samples, count, 4 * width), BF),
            shape((samples, count, width), F32),
            shape((samples, count, width), BF),
        ),
        in_specs=vmem(6),
        out_specs=tuple(vmem(5)),
        cost_estimate=pl.CostEstimate(flops=10**9, bytes_accessed=10**7, transcendentals=0),
        compiler_params=LIMIT,
        name="prepare",
    )(table, sent, atoms, cotangent, project, combine)
    outgoing, first, second, own_grad = pl.pallas_call(
        attention_kernel,
        out_shape=(
            shape((32, 32, width), BF),
            shape((samples, RIM, width), BF),
            shape((samples, RIM, width), BF),
            shape((samples, count, width), F32),
        ),
        in_specs=smem(2) + vmem(11),
        out_specs=tuple(vmem(4)),
        scratch_shapes=[
            pltpu.VMEM((windows, KW, KW), F32),
            pltpu.VMEM((windows, KW, KW), F32),
        ],
        compiler_params=LIMIT,
        name="attention",
    )(
        key_range,
        device,
        cotangent,
        project,
        sent,
        first,
        second,
        rows,
        normed,
        projected,
        gates,
        gated_grads,
        pair_norm,
    )

    def place(y, z_hi, core, z_lo, x):
        return ((y * 4 + z_hi) * 2 + core) * 16 + z_lo * 4 + x

    four = range(4)
    planes = [
        [place(y, z_hi, core, z_lo, x) for y in four for core in range(2) for x in four]
        for z_hi in four
        for z_lo in four
    ]
    lines = [
        [place(y, z_hi, core, z_lo, x) for z_hi in four for z_lo in four]
        for y in four
        for core in range(2)
        for x in four
    ]
    axes = ("row", "col")
    part = lax.all_to_all(outgoing, axes, 0, 0, axis_index_groups=planes, tiled=True)
    part = pl.pallas_call(
        middle_kernel,
        out_shape=shape((16, 32, width), BF),
        in_specs=smem(1) + vmem(1),
        out_specs=pl.BlockSpec(memory_space=pltpu.VMEM),
        compiler_params=LIMIT,
        name="middle",
    )(device, part)

    part, first, second = lax.optimization_barrier((part, first, second))
    scattered = lax.all_to_all(part, axes, 0, 0, axis_index_groups=lines, tiled=True)
    first = lax.ppermute(first, ("row", "col"), pairs)
    second = lax.ppermute(second, ("row", "col"), odd_pairs)
    part = jnp.sum(scattered[:, :24].astype(F32), axis=0).astype(BF)
    part, first, second = lax.optimization_barrier((part, first, second))
    part = jnp.broadcast_to(part, (32,) + part.shape)
    part = lax.all_to_all(part, axes, 0, 0, axis_index_groups=planes, tiled=True)
    band_grad = pl.pallas_call(
        band_kernel,
        out_shape=shape((keys, cols * block, width), BF),
        in_specs=smem(1) + vmem(3),
        out_specs=pl.BlockSpec(memory_space=pltpu.VMEM),
        compiler_params=LIMIT,
        name="band",
    )(device, tiles.reshape(entries, width), scattered, sent)
    band_grad = jnp.transpose(band_grad, (1, 0, 2))
    atoms_grad = pl.pallas_call(
        finish_kernel,
        out_shape=shape(atoms.shape, BF),
        in_specs=smem(1) + vmem(6),
        out_specs=pl.BlockSpec(memory_space=pltpu.VMEM),
        compiler_params=LIMIT,
        name="finish",
    )(device, atoms, cotangent, own_grad, first, second, sent)
    part, atoms_grad, band_grad = lax.optimization_barrier((part, atoms_grad, band_grad))
    project_grad, combine_grad, weight_grad, scale_grad, gain_grad = pl.pallas_call(
        last_kernel,
        out_shape=(
            shape(project.shape, BF),
            shape(combine.shape, BF),
            shape(weights.shape, BF),
            shape((1, width), F32),
            shape((1, width), F32),
        ),
        in_specs=vmem(3),
        out_specs=tuple(vmem(5)),
        compiler_params=LIMIT,
        name="last",
    )(part, project, sent)
    return (
        atoms_grad,
        project_grad,
        combine_grad,
        scale_grad.reshape(width),
        band_grad,
        weight_grad.T,
        gain_grad.reshape(width),
    )


def solution(mesh):
    in_specs = (
        P(None, ("row", "col"), None),
        P(None, ("row", "col"), None),
        P(),
        P(),
        P(),
        P("row", "col", None),
        P(),
        P(),
        P(("row", "col")),
        P(("row", "col"), None),
    )
    out_specs = (P(None, ("row", "col"), None), P(), P(), P(), P("row", "col", None), P(), P())
    return jax.shard_map(shards, mesh=mesh, in_specs=in_specs, out_specs=out_specs, check_vma=False)
```

```python
import math

import jax
import jax.numpy as jnp
from jax import lax
from jax.experimental import pallas as pl
from jax.experimental.pallas import tpu as pltpu
from jax.sharding import PartitionSpec as P

QW = 32
KW = 128
RIM = 48
EPSILON = 1e-05
NEG_FILL = -1e30
F32 = jnp.float32
BF = jnp.bfloat16


LIMIT = pltpu.CompilerParams(vmem_limit_bytes=16 * 1024 * 1024)


def nn(a, b):
    return lax.dot_general(a, b, (((1,), (0,)), ((), ())), preferred_element_type=F32)


def nt(a, b):
    return lax.dot_general(a, b, (((1,), (1,)), ((), ())), preferred_element_type=F32)


def tn(a, b):
    return lax.dot_general(a, b, (((0,), (0,)), ((), ())), preferred_element_type=F32)


def split2(x):
    high = x.astype(BF)
    return high, (x - high.astype(F32)).astype(BF)


def norm(v):
    mean = jnp.mean(v, axis=-1, keepdims=True)
    centred = v - mean
    inv = lax.rsqrt(jnp.mean(centred * centred, axis=-1, keepdims=True) + EPSILON)
    return centred * inv, inv


def norm_back(g, hat, inv):
    first = jnp.mean(g, axis=-1, keepdims=True)
    second = jnp.mean(g * hat, axis=-1, keepdims=True)
    return inv * (g - first - hat * second)


def iota(shape, dim):
    return lax.broadcasted_iota(jnp.int32, shape, dim)


def fetch(pairs, sems):
    copies = [pltpu.make_async_copy(src, dst, sems.at[n]) for n, (src, dst) in enumerate(pairs)]
    for copy in copies:
        copy.start()
    return copies


def split3(x):
    high = x.astype(BF).astype(F32)
    middle = (x - high).astype(BF).astype(F32)
    return [high, middle, x - high - middle]


def small(sent):
    block = sent[sent.shape[0] - 1].astype(F32)
    atom_gain = block[20:21] + block[21:22] + block[22:23]
    pair_gain = block[23:24] + block[24:25] + block[25:26]
    return block[:1], block[16:20], atom_gain, pair_gain


def start_kernel(
    device,
    band,
    atoms,
    tokens,
    weights_hbm,
    atom_gain_hbm,
    pair_gain_hbm,
    tiles,
    first,
    second,
    line,
    weights,
    atom_gain,
    pair_gain,
    sems,
):
    samples, count, width = atoms.shape
    odd = (device[0] + 1) & 1
    low = pl.multiple_of((1 - odd) * (count - RIM), 16)
    high = pl.multiple_of(odd * (count - RIM), 16)
    copies = fetch(
        [
            (tokens, line),
            (weights_hbm, weights),
            (atom_gain_hbm, atom_gain),
            (pair_gain_hbm, pair_gain),
        ]
        + [(band.at[k], tiles.at[:, k]) for k in range(band.shape[0])]
        + [
            (atoms.at[:, pl.ds(low, RIM)], first.at[:samples]),
            (atoms.at[:, pl.ds(high, RIM)], second.at[:samples]),
        ],
        sems,
    )
    for copy in copies[:4]:
        copy.wait()
    local = jnp.broadcast_to((line[...] - device[0] * 16).astype(F32), (16, width))
    rows = [local, weights[...].astype(F32)] + split3(atom_gain[...]) + split3(pair_gain[...])
    block = jnp.concatenate(rows + [jnp.zeros((RIM - 26, width), F32)], axis=0).astype(BF)
    first[samples] = block
    second[samples] = block
    for copy in copies[4:]:
        copy.wait()


def weight_lines(rows):
    return jnp.concatenate([rows, jnp.zeros((16 - rows.shape[0], rows.shape[1]), F32)], axis=0)


def weight_spread(rows):
    rows = [jnp.broadcast_to(rows[h : h + 1], (16, rows.shape[1])) for h in range(4)]
    return jnp.concatenate(rows * 2, axis=0).astype(BF)


def spread_slots(entries):
    hit = (iota((entries, KW), 0) >> 4) == iota((entries, KW), 1)
    return jnp.where(hit, 1.0, 0.0).astype(BF)


def entry_grads(table_grad, entries):
    grad = nn(spread_slots(entries), table_grad)
    column = iota((entries, KW), 1)
    shown = ((iota((entries, KW), 0) & 15) == (column & 15)) & (column < 64)
    return jnp.where(shown, grad, 0.0).astype(BF)


def pair_kernel(band, sent, table, pair_norm):
    heads = 4
    entries = band.shape[0]
    _, weights, _, gain = small(sent)
    hat, _ = norm(band[...].astype(F32))
    normed = (hat * gain).astype(BF)
    pair_norm[...] = normed
    bias_rows = nt(weight_lines(weights).astype(BF), normed)
    stacked = jnp.concatenate(
        [jnp.broadcast_to(bias_rows[h : h + 1], (16, entries)) for h in range(heads)], axis=0
    )
    own_token = (iota((64, entries), 0) & 15) == (iota((64, entries), 1) & 15)
    high, low = split2(jnp.where(own_token, stacked, 0.0))
    both = jnp.concatenate([high, low], axis=0)
    table[...] = nn(both, spread_slots(entries)).astype(BF)


def middle_kernel(device, scattered, outgoing):
    width = scattered.shape[2]
    total = scattered[0].astype(F32)
    for p in range(1, scattered.shape[0]):
        total = total + scattered[p].astype(F32)
    first = ((device[0] >> 7) & 3) * 8 + ((device[0] >> 4) & 1) * 4
    blocks = [scattered[first + x].astype(F32)[24:32] for x in range(4)]
    turned = [pltpu.roll(b, 64, 1) for b in blocks]
    left = iota((8, width), 1) < 64
    for z_lo in range(4):
        rows = slice(3 * (z_lo // 2), 3 * (z_lo // 2) + 3)
        lows, highs = (blocks, turned) if z_lo % 2 == 0 else (turned, blocks)
        pairs = [jnp.where(left, lows[x], highs[x + 1])[rows] for x in (0, 2)]
        tables = pairs + [jnp.zeros((2, width), F32)]
        result = jnp.concatenate([total[:24]] + tables, axis=0).astype(BF)
        for z_hi in range(4):
            outgoing[z_hi * 4 + z_lo] = result


def spread_kernel(scattered, outgoing):
    total = scattered[0].astype(F32)
    for q in range(1, scattered.shape[0]):
        total = total + scattered[q].astype(F32)
    total = total[:24].astype(BF)
    for p in range(outgoing.shape[0]):
        outgoing[p] = total


def band_kernel(device, band, scattered, sent, band_grad):
    entries = band.shape[0]
    width = band.shape[1]
    z_hi = (device[0] >> 5) & 3
    rows = []
    for z_lo in range(4):
        block = scattered[z_hi * 4 + z_lo].astype(F32)[24:32]
        turned = pltpu.roll(block, 64, 1)
        rows = rows + [block[:3], turned[:3], block[3:6], turned[3:6]]
    rows = jnp.concatenate(rows + [jnp.zeros((KW - 48, width), F32)], axis=0).astype(BF)
    hat, inv = norm(band[...].astype(F32))
    _, weights, _, pair_gain = small(sent)
    norm_grad = nn(entry_grads(rows, entries), weight_spread(weights)).astype(BF).astype(F32)
    result = norm_back(norm_grad * pair_gain, hat, inv).astype(BF)
    slots = band_grad.shape[0]
    for n in range(entries // 16):
        block, slot = divmod(n, slots)
        band_grad[slot, 16 * block : 16 * block + 16, :] = result[16 * n : 16 * n + 16]


def head_tokens(own, w):
    lane = iota((8, KW), 1)
    row = pltpu.roll(own, (-w % 4) * QW, 1)
    for h in range(1, 4):
        row = jnp.where((lane >> 5) == h, pltpu.roll(own, ((h - w) % 4) * QW, 1), row)
    return row.astype(jnp.int32)[:1]


def query_hot(own, w):
    lane = iota((KW, KW), 1)
    line = iota((KW, KW), 0)
    hit = ((line & 15) == head_tokens(own, w)) & (((line >> 4) & 3) == (lane >> 5))
    return jnp.where(hit, 1.0, 0.0).astype(BF)


def prepare_kernel(
    table, sent, atoms, cotangent, project, combine, rows, normed, projected, gates, gated_grad
):
    samples, count, width = atoms.shape
    tokens, _, gain, _ = small(sent)
    own = jnp.broadcast_to(tokens, (8, KW))
    for w in range(count // QW):
        high, low = split2(tn(table[...], query_hot(own, w)))
        rows[w] = jnp.concatenate([high, low], axis=0)
    for s in range(samples):
        x_hat, _ = norm(atoms[s].astype(F32))
        x = (x_hat * gain).astype(BF)
        normed[s] = x
        columns = nn(x, project[...]).astype(BF)
        projected[s] = columns
        gates[s] = jax.nn.sigmoid(columns[:, 3 * width :].astype(F32))
        gated_grad[s] = nt(cotangent[s], combine[...]).astype(BF)


def attention_kernel(
    key_range,
    device,
    cotangent,
    project,
    sent,
    first,
    second,
    rows,
    normed_own,
    projected_own,
    gates,
    gated_grads,
    pair_norm,
    outgoing,
    to_first,
    to_second,
    own_grad,
    bias,
    bias_grad,
):
    samples, count, width = cotangent.shape
    heads = 4
    windows = count // QW
    entries = pair_norm.shape[0]
    scale = 1.0 / math.sqrt(width // heads)
    lane = iota((KW, KW), 1)
    line = iota((KW, KW), 0)

    tokens, _, gain, _ = small(sent)
    own = jnp.broadcast_to(tokens, (8, KW))
    odd = (device[0] & 1) == 0

    def sides(x, y):
        return jnp.where(odd, x, y), jnp.where(odd, y, x)

    left, right = sides(first[samples].astype(F32), second[samples].astype(F32))
    left = left[:8] - 16.0
    right = right[:8] + 16.0
    row_lane = iota((8, KW), 1)

    def key_row(w):
        shift = RIM - w * QW
        one, two = (left, own) if shift > 0 else (own, right)
        shift = shift % KW
        row = jnp.where(row_lane < shift, pltpu.roll(one, shift, 1), pltpu.roll(two, shift, 1))
        return row.astype(jnp.int32)[:1] + 16

    def key_hot(w):
        return jnp.where(line == key_row(w), 1.0, 0.0).astype(BF)

    for w in range(windows):
        hot = key_hot(w)
        values = tn(jnp.concatenate([hot, hot], axis=0), rows[w])
        begin = device[0] * count - RIM + w * QW
        allowed = (line >= key_range[w, 0] - begin) & (line < key_range[w, 1] - begin)
        bias[w] = jnp.where(allowed, values, NEG_FILL)
        bias_grad[w] = jnp.zeros((KW, KW), F32)
    diag = jnp.where((line >> 5) == (lane >> 5), 1.0, 0.0).astype(BF)
    head_of = iota((QW, width), 1) >> 5

    def spread_heads(x):
        return jnp.concatenate([x] * heads, axis=0) * diag

    def gather_heads(x):
        total = x[:QW]
        for h in range(1, heads):
            total = jnp.where(head_of == h, x[h * QW : (h + 1) * QW], total)
        return total

    def overlap(parts):
        sums = []
        for m in range(windows + KW // QW - 1):
            total = None
            for w in range(windows):
                if 0 <= m - w < KW // QW:
                    term = parts[w][(m - w) * QW : (m - w + 1) * QW]
                    total = term if total is None else total + term
            sums.append(total)
        return jnp.concatenate(sums, axis=0).astype(BF)

    def sample(s, carry):
        project_sum, combine_sum = carry
        before, after = sides(first[s].astype(F32), second[s].astype(F32))
        x_hat, _ = norm(jnp.concatenate([before, after], axis=0))
        rims = (x_hat * gain).astype(BF)
        columns = nn(rims, project[:, width : 3 * width]).astype(BF)
        own_columns = projected_own[s]
        normed = jnp.concatenate([rims[:RIM], normed_own[s], rims[RIM:]], axis=0)
        query = own_columns[:, :width]
        key, value = [
            jnp.concatenate(
                [
                    columns[:RIM, n * width : (n + 1) * width],
                    own_columns[:, (n + 1) * width : (n + 2) * width],
                    columns[RIM:, n * width : (n + 1) * width],
                ],
                axis=0,
            )
            for n in range(2)
        ]
        out = cotangent[s]
        sigmoid = gates[s]
        gated_grad = gated_grads[s].astype(F32)
        mixture_grad = (gated_grad * sigmoid).astype(BF)
        span = range(windows)
        q = [spread_heads(query[w * QW : (w + 1) * QW]) for w in span]
        g = [spread_heads(mixture_grad[w * QW : (w + 1) * QW]) for w in span]
        k = [key[w * QW : w * QW + KW] for w in span]
        v = [value[w * QW : w * QW + KW] for w in span]
        scores = [nt(k[w], q[w]) * scale + bias[w] for w in span]
        weights_grad = [nt(v[w], g[w]).astype(BF).astype(F32) for w in span]
        scores = [jnp.exp(x - jnp.max(x, axis=0, keepdims=True)) for x in scores]
        weights = [x * (1.0 / jnp.sum(x, axis=0, keepdims=True)) for x in scores]
        low = [x.astype(BF) for x in weights]
        mixture = jnp.concatenate([gather_heads(tn(low[w], v[w])) for w in span], axis=0)
        row_dot = [jnp.sum(weights[w] * weights_grad[w], axis=0, keepdims=True) for w in span]
        score_grad = [weights[w] * (weights_grad[w] - row_dot[w]) for w in span]
        for w in span:
            bias_grad[w] += score_grad[w]
        score_low = [(x * scale).astype(BF) for x in score_grad]
        query_grads = [gather_heads(tn(score_low[w], k[w])).astype(BF) for w in span]
        key_grad = overlap([nn(score_low[w], q[w]) for w in span])
        value_grad = overlap([nn(low[w], g[w]) for w in span])
        gated = (mixture * sigmoid).astype(BF)
        combine_sum = combine_sum + tn(gated, out)
        gate_grad = (gated_grad * mixture * sigmoid * (1.0 - sigmoid)).astype(BF)
        rim = jnp.zeros((RIM, width), BF)
        query_cols = jnp.concatenate([rim] + query_grads + [rim], axis=0)
        gate_cols = jnp.concatenate([rim, gate_grad, rim], axis=0)
        grad = jnp.concatenate([query_cols, key_grad, value_grad, gate_cols], axis=1)
        project_sum = project_sum + tn(normed, grad)
        normed_grad = nt(grad, project[...])
        before, after = sides(normed_grad[:RIM], normed_grad[RIM + count :])
        to_first[s] = after.astype(BF)
        to_second[s] = before.astype(BF)
        own_grad[s] = normed_grad[RIM : RIM + count]
        return project_sum, combine_sum

    start = (
        jnp.zeros((width, 4 * width), F32),
        jnp.zeros((width, width), F32),
    )
    project_sum, combine_sum = lax.fori_loop(0, samples, sample, start, unroll=True)

    table_grad = jnp.zeros((KW, KW), F32)
    for w in range(windows):
        high, low = split2(bias_grad[w])
        hot = key_hot(w)
        by_slot = nn(hot, high) + nn(hot, low)
        high, low = split2(by_slot)
        queries = query_hot(own, w)
        table_grad = table_grad + nt(high, queries) + nt(low, queries)
    spread = iota((KW, entries), 0) == (iota((KW, entries), 1) >> 4)
    spread = jnp.where(spread, 1.0, 0.0).astype(BF)
    entry_grad = tn(table_grad.astype(BF), spread)
    shown = (iota((KW, entries), 0) & 15) == (iota((KW, entries), 1) & 15)
    entry_grad = jnp.where(shown, entry_grad, 0.0).astype(BF)
    weight_part = nn(entry_grad, pair_norm[...])
    left = iota((3, width), 1) < 64
    tables = []
    for x in range(4):
        by_z = [table_grad[3 * (4 * z + x) : 3 * (4 * z + x) + 3] for z in range(4)]
        pairs = [jnp.where(left, by_z[z], by_z[z + 1]) for z in (0, 2)]
        tables.append(jnp.concatenate(pairs + [jnp.zeros((2, width), F32)], axis=0))
    peers = outgoing.shape[0]
    for p in range(peers):
        part, row = divmod(16 * p, width)
        weight_row = jnp.zeros((1, width), F32)
        if p < heads:
            weight_row = jnp.sum(weight_part[p * 16 : (p + 1) * 16], axis=0, keepdims=True)
        parts = [
            project_sum[row : row + 16, part * width : (part + 1) * width],
            combine_sum[4 * p : 4 * p + 4],
            weight_row,
            jnp.zeros((3, width), F32),
            tables[p % 4],
        ]
        outgoing[p] = jnp.concatenate(parts, axis=0).astype(BF)


def last_kernel(
    parts,
    project,
    sent,
    project_grad,
    combine_grad,
    weight_grad,
    scale_grad,
    gain_grad,
):
    _, weights, atom_gain, pair_gain = small(sent)
    chunks = [parts[p].astype(F32) for p in range(parts.shape[0])]
    rows = jnp.concatenate([x[:16] for x in chunks], axis=0)
    width = rows.shape[1]
    dots = jnp.zeros((width, 1), F32)
    for part in range(4):
        columns = slice(part * width, (part + 1) * width)
        block = rows[part * width : (part + 1) * width]
        project_grad[:, columns] = block.astype(BF)
        dots = dots + jnp.sum(block * project[:, columns].astype(F32), axis=1, keepdims=True)
    combine_grad[...] = jnp.concatenate([x[16:20] for x in chunks], axis=0).astype(BF)
    dots = jnp.transpose(jnp.broadcast_to(dots, (width, width)))[:1]
    scale_grad[...] = dots / atom_gain
    tail = jnp.concatenate([x[20:21] for x in chunks[:4]], axis=0)
    weight_grad[...] = tail.astype(BF)
    dots = jnp.sum(tail * weights, axis=0, keepdims=True)
    gain_grad[...] = dots / pair_gain


def finish_kernel(device, atoms, cotangent, own_grad, first, second, sent, result):
    samples, count, width = atoms.shape
    odd = (device[0] & 1) == 1
    _, _, gain, _ = small(sent)
    for s in range(samples):
        x_hat, inv = norm(atoms[s].astype(F32))
        rim = jnp.zeros((count - RIM, width), F32)
        one, two = first[s].astype(F32), second[s].astype(F32)
        total = own_grad[s] + jnp.concatenate([jnp.where(odd, one, two), rim], axis=0)
        total = total + jnp.concatenate([rim, jnp.where(odd, two, one)], axis=0)
        g = total.astype(BF).astype(F32) * gain
        result[s] = (cotangent[s].astype(F32) + norm_back(g, x_hat, inv)).astype(BF)


def vmem(n):
    return [pl.BlockSpec(memory_space=pltpu.VMEM)] * n


def smem(n):
    return [pl.BlockSpec(memory_space=pltpu.SMEM)] * n


def anywhere(n):
    return [pl.BlockSpec(memory_space=pl.ANY)] * n


def shards(
    atoms,
    cotangent,
    project,
    combine,
    atom_gain,
    pair_band,
    pair_gain,
    pair_weight,
    atom_token,
    key_range,
):
    samples, count, width = atoms.shape
    cols = lax.axis_size("col")
    peers = lax.axis_size("row") * cols
    device = lax.axis_index(("row", "col"))
    windows = count // QW
    block = pair_band.shape[0] // cols
    keys = pair_band.shape[1]
    pairs = [(i + j, i + 1 - j) for i in range(1, peers - 1, 2) for j in range(2)]
    odd_pairs = [(i, i ^ 1) for i in range(peers)]

    shape = jax.ShapeDtypeStruct

    shape = jax.ShapeDtypeStruct
    device = device.astype(jnp.int32).reshape(1)
    tokens = atom_token.reshape(1, count)
    weights = pair_weight.T
    gain = atom_gain.reshape(1, width)
    band_gain = pair_gain.reshape(1, width)

    entries = cols * keys * block
    tiles, first, sent = pl.pallas_call(
        start_kernel,
        out_shape=(
            shape((cols, keys, block, width), BF),
            shape((samples + 1, RIM, width), BF),
            shape((samples + 1, RIM, width), BF),
        ),
        in_specs=smem(1) + anywhere(6),
        out_specs=tuple(vmem(3)),
        scratch_shapes=[
            pltpu.VMEM((1, count), jnp.int32),
            pltpu.VMEM(weights.shape, BF),
            pltpu.VMEM(gain.shape, F32),
            pltpu.VMEM(band_gain.shape, F32),
            pltpu.SemaphoreType.DMA((6 + keys,)),
        ],
        compiler_params=pltpu.CompilerParams(vmem_limit_bytes=60 * 1024 * 1024),
        name="start",
    )(
        device,
        jnp.transpose(pair_band, (1, 0, 2)).reshape(keys, cols, block, width),
        atoms,
        tokens,
        weights,
        gain,
        band_gain,
    )
    band = lax.all_to_all(tiles, "col", 0, 0, tiled=True).reshape(entries, width)

    first = lax.ppermute(first, ("row", "col"), pairs)
    second = lax.ppermute(sent, ("row", "col"), odd_pairs)

    table, pair_norm = pl.pallas_call(
        pair_kernel,
        out_shape=(shape((KW, KW), BF), shape((entries, width), BF)),
        in_specs=vmem(2),
        out_specs=tuple(vmem(2)),
        cost_estimate=pl.CostEstimate(flops=10**9, bytes_accessed=10**7, transcendentals=0),
        compiler_params=LIMIT,
        name="pair",
    )(band, sent)
    rows, normed, projected, gates, gated_grads = pl.pallas_call(
        prepare_kernel,
        out_shape=(
            shape((windows, 2 * KW, KW), BF),
            shape((samples, count, width), BF),
            shape((samples, count, 4 * width), BF),
            shape((samples, count, width), F32),
            shape((samples, count, width), BF),
        ),
        in_specs=vmem(6),
        out_specs=tuple(vmem(5)),
        cost_estimate=pl.CostEstimate(flops=10**9, bytes_accessed=10**7, transcendentals=0),
        compiler_params=LIMIT,
        name="prepare",
    )(table, sent, atoms, cotangent, project, combine)
    outgoing, first, second, own_grad = pl.pallas_call(
        attention_kernel,
        out_shape=(
            shape((32, 32, width), BF),
            shape((samples, RIM, width), BF),
            shape((samples, RIM, width), BF),
            shape((samples, count, width), F32),
        ),
        in_specs=smem(2) + vmem(11),
        out_specs=tuple(vmem(4)),
        scratch_shapes=[
            pltpu.VMEM((windows, KW, KW), F32),
            pltpu.VMEM((windows, KW, KW), F32),
        ],
        compiler_params=LIMIT,
        name="attention",
    )(
        key_range,
        device,
        cotangent,
        project,
        sent,
        first,
        second,
        rows,
        normed,
        projected,
        gates,
        gated_grads,
        pair_norm,
    )

    def place(y, z_hi, core, z_lo, x):
        return ((y * 4 + z_hi) * 2 + core) * 16 + z_lo * 4 + x

    four = range(4)
    planes = [
        [place(y, z_hi, core, z_lo, x) for y in four for core in range(2) for x in four]
        for z_hi in four
        for z_lo in four
    ]
    lines = [
        [place(y, z_hi, core, z_lo, x) for z_hi in four for z_lo in four]
        for y in four
        for core in range(2)
        for x in four
    ]
    axes = ("row", "col")
    part = lax.all_to_all(outgoing, axes, 0, 0, axis_index_groups=planes, tiled=True)
    part = pl.pallas_call(
        middle_kernel,
        out_shape=shape((16, 32, width), BF),
        in_specs=smem(1) + vmem(1),
        out_specs=pl.BlockSpec(memory_space=pltpu.VMEM),
        compiler_params=LIMIT,
        name="middle",
    )(device, part)

    part, first, second = lax.optimization_barrier((part, first, second))
    scattered = lax.all_to_all(part, axes, 0, 0, axis_index_groups=lines, tiled=True)
    first = lax.ppermute(first, ("row", "col"), odd_pairs)
    second = lax.ppermute(second, ("row", "col"), pairs)
    scattered, first, second = lax.optimization_barrier((scattered, first, second))
    part = pl.pallas_call(
        spread_kernel,
        out_shape=shape((32, 24, width), BF),
        in_specs=vmem(1),
        out_specs=pl.BlockSpec(memory_space=pltpu.VMEM),
        compiler_params=LIMIT,
        name="spread",
    )(scattered)
    part = lax.all_to_all(part, axes, 0, 0, axis_index_groups=planes, tiled=True)
    band_grad = pl.pallas_call(
        band_kernel,
        out_shape=shape((keys, cols * block, width), BF),
        in_specs=smem(1) + vmem(3),
        out_specs=pl.BlockSpec(memory_space=pltpu.VMEM),
        compiler_params=LIMIT,
        name="band",
    )(device, tiles.reshape(entries, width), scattered, sent)
    band_grad = jnp.transpose(band_grad, (1, 0, 2))
    atoms_grad = pl.pallas_call(
        finish_kernel,
        out_shape=shape(atoms.shape, BF),
        in_specs=smem(1) + vmem(6),
        out_specs=pl.BlockSpec(memory_space=pltpu.VMEM),
        compiler_params=LIMIT,
        name="finish",
    )(device, atoms, cotangent, own_grad, first, second, sent)
    part, atoms_grad, band_grad = lax.optimization_barrier((part, atoms_grad, band_grad))
    project_grad, combine_grad, weight_grad, scale_grad, gain_grad = pl.pallas_call(
        last_kernel,
        out_shape=(
            shape(project.shape, BF),
            shape(combine.shape, BF),
            shape(weights.shape, BF),
            shape((1, width), F32),
            shape((1, width), F32),
        ),
        in_specs=vmem(3),
        out_specs=tuple(vmem(5)),
        compiler_params=LIMIT,
        name="last",
    )(part, project, sent)
    return (
        atoms_grad,
        project_grad,
        combine_grad,
        scale_grad.reshape(width),
        band_grad,
        weight_grad.T,
        gain_grad.reshape(width),
    )


def solution(mesh):
    in_specs = (
        P(None, ("row", "col"), None),
        P(None, ("row", "col"), None),
        P(),
        P(),
        P(),
        P("row", "col", None),
        P(),
        P(),
        P(("row", "col")),
        P(("row", "col"), None),
    )
    out_specs = (P(None, ("row", "col"), None), P(), P(), P(), P("row", "col", None), P(), P())
    return jax.shard_map(shards, mesh=mesh, in_specs=in_specs, out_specs=out_specs, check_vma=False)
```

```python
import math

import jax
import jax.numpy as jnp
from jax import lax
from jax.experimental import pallas as pl
from jax.experimental.pallas import tpu as pltpu
from jax.sharding import PartitionSpec as P

QW = 32
KW = 128
RIM = 48
EPSILON = 1e-05
NEG_FILL = -1e30
F32 = jnp.float32
BF = jnp.bfloat16


LIMIT = pltpu.CompilerParams(vmem_limit_bytes=16 * 1024 * 1024)


def nn(a, b):
    return lax.dot_general(a, b, (((1,), (0,)), ((), ())), preferred_element_type=F32)


def nt(a, b):
    return lax.dot_general(a, b, (((1,), (1,)), ((), ())), preferred_element_type=F32)


def tn(a, b):
    return lax.dot_general(a, b, (((0,), (0,)), ((), ())), preferred_element_type=F32)


def split2(x):
    high = x.astype(BF)
    return high, (x - high.astype(F32)).astype(BF)


def norm(v):
    mean = jnp.mean(v, axis=-1, keepdims=True)
    centred = v - mean
    inv = lax.rsqrt(jnp.mean(centred * centred, axis=-1, keepdims=True) + EPSILON)
    return centred * inv, inv


def norm_back(g, hat, inv):
    first = jnp.mean(g, axis=-1, keepdims=True)
    second = jnp.mean(g * hat, axis=-1, keepdims=True)
    return inv * (g - first - hat * second)


def iota(shape, dim):
    return lax.broadcasted_iota(jnp.int32, shape, dim)


def fetch(pairs, sems):
    copies = [pltpu.make_async_copy(src, dst, sems.at[n]) for n, (src, dst) in enumerate(pairs)]
    for copy in copies:
        copy.start()
    return copies


def split3(x):
    high = x.astype(BF).astype(F32)
    middle = (x - high).astype(BF).astype(F32)
    return [high, middle, x - high - middle]


def small(sent):
    block = sent[sent.shape[0] - 1].astype(F32)
    atom_gain = block[20:21] + block[21:22] + block[22:23]
    pair_gain = block[23:24] + block[24:25] + block[25:26]
    return block[:1], block[16:20], atom_gain, pair_gain


def start_kernel(
    device,
    band,
    atoms,
    tokens,
    weights_hbm,
    atom_gain_hbm,
    pair_gain_hbm,
    tiles,
    first,
    second,
    line,
    weights,
    atom_gain,
    pair_gain,
    sems,
):
    samples, count, width = atoms.shape
    odd = (device[0] + 1) & 1
    low = pl.multiple_of((1 - odd) * (count - RIM), 16)
    high = pl.multiple_of(odd * (count - RIM), 16)
    copies = fetch(
        [
            (tokens, line),
            (weights_hbm, weights),
            (atom_gain_hbm, atom_gain),
            (pair_gain_hbm, pair_gain),
        ]
        + [(band.at[k], tiles.at[:, k]) for k in range(band.shape[0])]
        + [
            (atoms.at[:, pl.ds(low, RIM)], first.at[:samples]),
            (atoms.at[:, pl.ds(high, RIM)], second.at[:samples]),
        ],
        sems,
    )
    for copy in copies[:4]:
        copy.wait()
    local = jnp.broadcast_to((line[...] - device[0] * 16).astype(F32), (16, width))
    rows = [local, weights[...].astype(F32)] + split3(atom_gain[...]) + split3(pair_gain[...])
    block = jnp.concatenate(rows + [jnp.zeros((RIM - 26, width), F32)], axis=0).astype(BF)
    first[samples] = block
    second[samples] = block
    for copy in copies[4:]:
        copy.wait()


def weight_lines(rows):
    return jnp.concatenate([rows, jnp.zeros((16 - rows.shape[0], rows.shape[1]), F32)], axis=0)


def weight_spread(rows):
    rows = [jnp.broadcast_to(rows[h : h + 1], (16, rows.shape[1])) for h in range(4)]
    return jnp.concatenate(rows * 2, axis=0).astype(BF)


def spread_slots(entries):
    hit = (iota((entries, KW), 0) >> 4) == iota((entries, KW), 1)
    return jnp.where(hit, 1.0, 0.0).astype(BF)


def entry_grads(table_grad, entries):
    grad = nn(spread_slots(entries), table_grad)
    column = iota((entries, KW), 1)
    shown = ((iota((entries, KW), 0) & 15) == (column & 15)) & (column < 64)
    return jnp.where(shown, grad, 0.0).astype(BF)


def pair_kernel(band, sent, table, pair_norm):
    heads = 4
    entries = band.shape[0]
    _, weights, _, gain = small(sent)
    hat, _ = norm(band[...].astype(F32))
    normed = (hat * gain).astype(BF)
    pair_norm[...] = normed
    bias_rows = nt(weight_lines(weights).astype(BF), normed)
    stacked = jnp.concatenate(
        [jnp.broadcast_to(bias_rows[h : h + 1], (16, entries)) for h in range(heads)], axis=0
    )
    own_token = (iota((64, entries), 0) & 15) == (iota((64, entries), 1) & 15)
    high, low = split2(jnp.where(own_token, stacked, 0.0))
    both = jnp.concatenate([high, low], axis=0)
    table[...] = nn(both, spread_slots(entries)).astype(BF)


def middle_kernel(device, scattered, outgoing):
    width = scattered.shape[2]
    total = scattered[0].astype(F32)
    for p in range(1, scattered.shape[0]):
        total = total + scattered[p].astype(F32)
    first = ((device[0] >> 7) & 3) * 8 + ((device[0] >> 4) & 1) * 4
    blocks = [scattered[first + x].astype(F32)[24:32] for x in range(4)]
    turned = [pltpu.roll(b, 64, 1) for b in blocks]
    left = iota((8, width), 1) < 64
    for z_lo in range(4):
        rows = slice(3 * (z_lo // 2), 3 * (z_lo // 2) + 3)
        lows, highs = (blocks, turned) if z_lo % 2 == 0 else (turned, blocks)
        pairs = [jnp.where(left, lows[x], highs[x + 1])[rows] for x in (0, 2)]
        tables = pairs + [jnp.zeros((2, width), F32)]
        result = jnp.concatenate([total[:24]] + tables, axis=0).astype(BF)
        for z_hi in range(4):
            outgoing[z_hi * 4 + z_lo] = result


def band_kernel(device, band, scattered, sent, band_grad):
    entries = band.shape[0]
    width = band.shape[1]
    z_hi = (device[0] >> 5) & 3
    rows = []
    for z_lo in range(4):
        block = scattered[z_hi * 4 + z_lo].astype(F32)[24:32]
        turned = pltpu.roll(block, 64, 1)
        rows = rows + [block[:3], turned[:3], block[3:6], turned[3:6]]
    rows = jnp.concatenate(rows + [jnp.zeros((KW - 48, width), F32)], axis=0).astype(BF)
    hat, inv = norm(band[...].astype(F32))
    _, weights, _, pair_gain = small(sent)
    norm_grad = nn(entry_grads(rows, entries), weight_spread(weights)).astype(BF).astype(F32)
    result = norm_back(norm_grad * pair_gain, hat, inv).astype(BF)
    slots = band_grad.shape[0]
    for n in range(entries // 16):
        block, slot = divmod(n, slots)
        band_grad[slot, 16 * block : 16 * block + 16, :] = result[16 * n : 16 * n + 16]


def head_tokens(own, w):
    lane = iota((8, KW), 1)
    row = pltpu.roll(own, (-w % 4) * QW, 1)
    for h in range(1, 4):
        row = jnp.where((lane >> 5) == h, pltpu.roll(own, ((h - w) % 4) * QW, 1), row)
    return row.astype(jnp.int32)[:1]


def query_hot(own, w):
    lane = iota((KW, KW), 1)
    line = iota((KW, KW), 0)
    hit = ((line & 15) == head_tokens(own, w)) & (((line >> 4) & 3) == (lane >> 5))
    return jnp.where(hit, 1.0, 0.0).astype(BF)


def prepare_kernel(
    table, sent, atoms, cotangent, project, combine, rows, normed, projected, gates, gated_grad
):
    samples, count, width = atoms.shape
    tokens, _, gain, _ = small(sent)
    own = jnp.broadcast_to(tokens, (8, KW))
    for w in range(count // QW):
        high, low = split2(tn(table[...], query_hot(own, w)))
        rows[w] = jnp.concatenate([high, low], axis=0)
    for s in range(samples):
        x_hat, _ = norm(atoms[s].astype(F32))
        x = (x_hat * gain).astype(BF)
        normed[s] = x
        columns = nn(x, project[...]).astype(BF)
        projected[s] = columns
        gates[s] = jax.nn.sigmoid(columns[:, 3 * width :].astype(F32))
        gated_grad[s] = nt(cotangent[s], combine[...]).astype(BF)


def attention_kernel(
    key_range,
    device,
    cotangent,
    project,
    sent,
    first,
    second,
    rows,
    normed_own,
    projected_own,
    gates,
    gated_grads,
    pair_norm,
    outgoing,
    to_first,
    to_second,
    own_grad,
    bias,
):
    samples, count, width = cotangent.shape
    heads = 4
    windows = count // QW
    entries = pair_norm.shape[0]
    scale = 1.0 / math.sqrt(width // heads)
    lane = iota((KW, KW), 1)
    line = iota((KW, KW), 0)

    tokens, _, gain, _ = small(sent)
    own = jnp.broadcast_to(tokens, (8, KW))
    odd = (device[0] & 1) == 0

    def sides(x, y):
        return jnp.where(odd, x, y), jnp.where(odd, y, x)

    left, right = sides(first[samples].astype(F32), second[samples].astype(F32))
    left = left[:8] - 16.0
    right = right[:8] + 16.0
    row_lane = iota((8, KW), 1)

    def key_row(w):
        shift = RIM - w * QW
        one, two = (left, own) if shift > 0 else (own, right)
        shift = shift % KW
        row = jnp.where(row_lane < shift, pltpu.roll(one, shift, 1), pltpu.roll(two, shift, 1))
        return row.astype(jnp.int32)[:1] + 16

    def key_hot(w):
        return jnp.where(line == key_row(w), 1.0, 0.0).astype(BF)

    for w in range(windows):
        hot = key_hot(w)
        values = tn(jnp.concatenate([hot, hot], axis=0), rows[w])
        begin = device[0] * count - RIM + w * QW
        allowed = (line >= key_range[w, 0] - begin) & (line < key_range[w, 1] - begin)
        bias[w] = jnp.where(allowed, values, NEG_FILL)
    diag = jnp.where((line >> 5) == (lane >> 5), 1.0, 0.0).astype(BF)
    head_of = iota((QW, width), 1) >> 5

    def spread_heads(x):
        return jnp.concatenate([x] * heads, axis=0) * diag

    def gather_heads(x):
        total = x[:QW]
        for h in range(1, heads):
            total = jnp.where(head_of == h, x[h * QW : (h + 1) * QW], total)
        return total

    def overlap(parts):
        sums = []
        for m in range(windows + KW // QW - 1):
            total = None
            for w in range(windows):
                if 0 <= m - w < KW // QW:
                    term = parts[w][(m - w) * QW : (m - w + 1) * QW]
                    total = term if total is None else total + term
            sums.append(total)
        return jnp.concatenate(sums, axis=0).astype(BF)

    def sample(s, carry):
        project_sum, combine_sum, bias_sums = carry
        before, after = sides(first[s].astype(F32), second[s].astype(F32))
        x_hat, _ = norm(jnp.concatenate([before, after], axis=0))
        rims = (x_hat * gain).astype(BF)
        columns = nn(rims, project[:, width : 3 * width]).astype(BF)
        own_columns = projected_own[s]
        normed = jnp.concatenate([rims[:RIM], normed_own[s], rims[RIM:]], axis=0)
        query = own_columns[:, :width]
        key, value = [
            jnp.concatenate(
                [
                    columns[:RIM, n * width : (n + 1) * width],
                    own_columns[:, (n + 1) * width : (n + 2) * width],
                    columns[RIM:, n * width : (n + 1) * width],
                ],
                axis=0,
            )
            for n in range(2)
        ]
        out = cotangent[s]
        sigmoid = gates[s]
        gated_grad = gated_grads[s].astype(F32)
        mixture_grad = (gated_grad * sigmoid).astype(BF)
        span = range(windows)
        q = [spread_heads(query[w * QW : (w + 1) * QW]) for w in span]
        g = [spread_heads(mixture_grad[w * QW : (w + 1) * QW]) for w in span]
        k = [key[w * QW : w * QW + KW] for w in span]
        v = [value[w * QW : w * QW + KW] for w in span]
        scores = [nt(k[w], q[w]) * scale + bias[w] for w in span]
        weights_grad = [nt(v[w], g[w]).astype(BF).astype(F32) for w in span]
        scores = [jnp.exp(x - jnp.max(x, axis=0, keepdims=True)) for x in scores]
        weights = [x * (1.0 / jnp.sum(x, axis=0, keepdims=True)) for x in scores]
        low = [x.astype(BF) for x in weights]
        mixture = jnp.concatenate([gather_heads(tn(low[w], v[w])) for w in span], axis=0)
        row_dot = [jnp.sum(weights[w] * weights_grad[w], axis=0, keepdims=True) for w in span]
        score_grad = [weights[w] * (weights_grad[w] - row_dot[w]) for w in span]
        bias_sums = tuple(bias_sums[w] + score_grad[w] for w in span)
        score_low = [(x * scale).astype(BF) for x in score_grad]
        query_grads = [gather_heads(tn(score_low[w], k[w])).astype(BF) for w in span]
        key_grad = overlap([nn(score_low[w], q[w]) for w in span])
        value_grad = overlap([nn(low[w], g[w]) for w in span])
        gated = (mixture * sigmoid).astype(BF)
        combine_sum = combine_sum + tn(gated, out)
        gate_grad = (gated_grad * mixture * sigmoid * (1.0 - sigmoid)).astype(BF)
        rim = jnp.zeros((RIM, width), BF)
        query_cols = jnp.concatenate([rim] + query_grads + [rim], axis=0)
        gate_cols = jnp.concatenate([rim, gate_grad, rim], axis=0)
        grad = jnp.concatenate([query_cols, key_grad, value_grad, gate_cols], axis=1)
        project_sum = project_sum + tn(normed, grad)
        normed_grad = nt(grad, project[...])
        before, after = sides(normed_grad[:RIM], normed_grad[RIM + count :])
        to_first[s] = before.astype(BF)
        to_second[s] = after.astype(BF)
        own_grad[s] = normed_grad[RIM : RIM + count]
        return project_sum, combine_sum, bias_sums

    start = (
        jnp.zeros((width, 4 * width), F32),
        jnp.zeros((width, width), F32),
        tuple(jnp.zeros((KW, KW), F32) for _ in range(windows)),
    )
    project_sum, combine_sum, bias_sums = lax.fori_loop(0, samples, sample, start, unroll=True)

    table_grad = jnp.zeros((KW, KW), F32)
    for w in range(windows):
        high, low = split2(bias_sums[w])
        hot = key_hot(w)
        by_slot = nn(hot, high) + nn(hot, low)
        high, low = split2(by_slot)
        queries = query_hot(own, w)
        table_grad = table_grad + nt(high, queries) + nt(low, queries)
    spread = iota((KW, entries), 0) == (iota((KW, entries), 1) >> 4)
    spread = jnp.where(spread, 1.0, 0.0).astype(BF)
    entry_grad = tn(table_grad.astype(BF), spread)
    shown = (iota((KW, entries), 0) & 15) == (iota((KW, entries), 1) & 15)
    entry_grad = jnp.where(shown, entry_grad, 0.0).astype(BF)
    weight_part = nn(entry_grad, pair_norm[...])
    left = iota((3, width), 1) < 64
    tables = []
    for x in range(4):
        by_z = [table_grad[3 * (4 * z + x) : 3 * (4 * z + x) + 3] for z in range(4)]
        pairs = [jnp.where(left, by_z[z], by_z[z + 1]) for z in (0, 2)]
        tables.append(jnp.concatenate(pairs + [jnp.zeros((2, width), F32)], axis=0))
    peers = outgoing.shape[0]
    for p in range(peers):
        part, row = divmod(16 * p, width)
        weight_row = jnp.zeros((1, width), F32)
        if p < heads:
            weight_row = jnp.sum(weight_part[p * 16 : (p + 1) * 16], axis=0, keepdims=True)
        parts = [
            project_sum[row : row + 16, part * width : (part + 1) * width],
            combine_sum[4 * p : 4 * p + 4],
            weight_row,
            jnp.zeros((3, width), F32),
            tables[p % 4],
        ]
        outgoing[p] = jnp.concatenate(parts, axis=0).astype(BF)


def last_kernel(
    parts,
    project,
    sent,
    project_grad,
    combine_grad,
    weight_grad,
    scale_grad,
    gain_grad,
):
    _, weights, atom_gain, pair_gain = small(sent)
    chunks = [parts[p].astype(F32) for p in range(parts.shape[0])]
    rows = jnp.concatenate([x[:16] for x in chunks], axis=0)
    width = rows.shape[1]
    dots = jnp.zeros((width, 1), F32)
    for part in range(4):
        columns = slice(part * width, (part + 1) * width)
        block = rows[part * width : (part + 1) * width]
        project_grad[:, columns] = block.astype(BF)
        dots = dots + jnp.sum(block * project[:, columns].astype(F32), axis=1, keepdims=True)
    combine_grad[...] = jnp.concatenate([x[16:20] for x in chunks], axis=0).astype(BF)
    dots = jnp.transpose(jnp.broadcast_to(dots, (width, width)))[:1]
    scale_grad[...] = dots / atom_gain
    tail = jnp.concatenate([x[20:21] for x in chunks[:4]], axis=0)
    weight_grad[...] = tail.astype(BF)
    dots = jnp.sum(tail * weights, axis=0, keepdims=True)
    gain_grad[...] = dots / pair_gain


def finish_kernel(device, atoms, cotangent, own_grad, first, second, sent, result):
    samples, count, width = atoms.shape
    odd = (device[0] & 1) == 0
    _, _, gain, _ = small(sent)
    for s in range(samples):
        x_hat, inv = norm(atoms[s].astype(F32))
        rim = jnp.zeros((count - RIM, width), F32)
        one, two = first[s].astype(F32), second[s].astype(F32)
        total = own_grad[s] + jnp.concatenate([jnp.where(odd, one, two), rim], axis=0)
        total = total + jnp.concatenate([rim, jnp.where(odd, two, one)], axis=0)
        g = total.astype(BF).astype(F32) * gain
        result[s] = (cotangent[s].astype(F32) + norm_back(g, x_hat, inv)).astype(BF)


def vmem(n):
    return [pl.BlockSpec(memory_space=pltpu.VMEM)] * n


def smem(n):
    return [pl.BlockSpec(memory_space=pltpu.SMEM)] * n


def anywhere(n):
    return [pl.BlockSpec(memory_space=pl.ANY)] * n


def shards(
    atoms,
    cotangent,
    project,
    combine,
    atom_gain,
    pair_band,
    pair_gain,
    pair_weight,
    atom_token,
    key_range,
):
    samples, count, width = atoms.shape
    cols = lax.axis_size("col")
    peers = lax.axis_size("row") * cols
    device = lax.axis_index(("row", "col"))
    windows = count // QW
    block = pair_band.shape[0] // cols
    keys = pair_band.shape[1]
    pairs = [(i + j, i + 1 - j) for i in range(1, peers - 1, 2) for j in range(2)]
    odd_pairs = [(i, i ^ 1) for i in range(peers)]

    shape = jax.ShapeDtypeStruct

    shape = jax.ShapeDtypeStruct
    device = device.astype(jnp.int32).reshape(1)
    tokens = atom_token.reshape(1, count)
    weights = pair_weight.T
    gain = atom_gain.reshape(1, width)
    band_gain = pair_gain.reshape(1, width)

    entries = cols * keys * block
    tiles, first, sent = pl.pallas_call(
        start_kernel,
        out_shape=(
            shape((cols, keys, block, width), BF),
            shape((samples + 1, RIM, width), BF),
            shape((samples + 1, RIM, width), BF),
        ),
        in_specs=smem(1) + anywhere(6),
        out_specs=tuple(vmem(3)),
        scratch_shapes=[
            pltpu.VMEM((1, count), jnp.int32),
            pltpu.VMEM(weights.shape, BF),
            pltpu.VMEM(gain.shape, F32),
            pltpu.VMEM(band_gain.shape, F32),
            pltpu.SemaphoreType.DMA((6 + keys,)),
        ],
        compiler_params=pltpu.CompilerParams(vmem_limit_bytes=60 * 1024 * 1024),
        name="start",
    )(
        device,
        jnp.transpose(pair_band, (1, 0, 2)).reshape(keys, cols, block, width),
        atoms,
        tokens,
        weights,
        gain,
        band_gain,
    )
    band = lax.all_to_all(tiles, "col", 0, 0, tiled=True).reshape(entries, width)

    first = lax.ppermute(first, ("row", "col"), pairs)
    second = lax.ppermute(sent, ("row", "col"), odd_pairs)

    table, pair_norm = pl.pallas_call(
        pair_kernel,
        out_shape=(shape((KW, KW), BF), shape((entries, width), BF)),
        in_specs=vmem(2),
        out_specs=tuple(vmem(2)),
        cost_estimate=pl.CostEstimate(flops=10**9, bytes_accessed=10**7, transcendentals=0),
        compiler_params=LIMIT,
        name="pair",
    )(band, sent)
    rows, normed, projected, gates, gated_grads = pl.pallas_call(
        prepare_kernel,
        out_shape=(
            shape((windows, 2 * KW, KW), BF),
            shape((samples, count, width), BF),
            shape((samples, count, 4 * width), BF),
            shape((samples, count, width), F32),
            shape((samples, count, width), BF),
        ),
        in_specs=vmem(6),
        out_specs=tuple(vmem(5)),
        cost_estimate=pl.CostEstimate(flops=10**9, bytes_accessed=10**7, transcendentals=0),
        compiler_params=LIMIT,
        name="prepare",
    )(table, sent, atoms, cotangent, project, combine)
    outgoing, first, second, own_grad = pl.pallas_call(
        attention_kernel,
        out_shape=(
            shape((32, 32, width), BF),
            shape((samples, RIM, width), BF),
            shape((samples, RIM, width), BF),
            shape((samples, count, width), F32),
        ),
        in_specs=smem(2) + vmem(11),
        out_specs=tuple(vmem(4)),
        scratch_shapes=[
            pltpu.VMEM((windows, KW, KW), F32),
        ],
        compiler_params=LIMIT,
        name="attention",
    )(
        key_range,
        device,
        cotangent,
        project,
        sent,
        first,
        second,
        rows,
        normed,
        projected,
        gates,
        gated_grads,
        pair_norm,
    )

    def place(y, z_hi, core, z_lo, x):
        return ((y * 4 + z_hi) * 2 + core) * 16 + z_lo * 4 + x

    four = range(4)
    planes = [
        [place(y, z_hi, core, z_lo, x) for y in four for core in range(2) for x in four]
        for z_hi in four
        for z_lo in four
    ]
    lines = [
        [place(y, z_hi, core, z_lo, x) for z_hi in four for z_lo in four]
        for y in four
        for core in range(2)
        for x in four
    ]
    axes = ("row", "col")
    part = lax.all_to_all(outgoing, axes, 0, 0, axis_index_groups=planes, tiled=True)
    part = pl.pallas_call(
        middle_kernel,
        out_shape=shape((16, 32, width), BF),
        in_specs=smem(1) + vmem(1),
        out_specs=pl.BlockSpec(memory_space=pltpu.VMEM),
        compiler_params=LIMIT,
        name="middle",
    )(device, part)

    part, first, second = lax.optimization_barrier((part, first, second))
    scattered = lax.all_to_all(part, axes, 0, 0, axis_index_groups=lines, tiled=True)
    first = lax.ppermute(first, ("row", "col"), pairs)
    second = lax.ppermute(second, ("row", "col"), odd_pairs)
    part = jnp.sum(scattered[:, :24].astype(F32), axis=0).astype(BF)
    part, first, second = lax.optimization_barrier((part, first, second))
    part = jnp.broadcast_to(part, (32,) + part.shape)
    part = lax.all_to_all(part, axes, 0, 0, axis_index_groups=planes, tiled=True)
    band_grad = pl.pallas_call(
        band_kernel,
        out_shape=shape((keys, cols * block, width), BF),
        in_specs=smem(1) + vmem(3),
        out_specs=pl.BlockSpec(memory_space=pltpu.VMEM),
        compiler_params=LIMIT,
        name="band",
    )(device, tiles.reshape(entries, width), scattered, sent)
    band_grad = jnp.transpose(band_grad, (1, 0, 2))
    atoms_grad = pl.pallas_call(
        finish_kernel,
        out_shape=shape(atoms.shape, BF),
        in_specs=smem(1) + vmem(6),
        out_specs=pl.BlockSpec(memory_space=pltpu.VMEM),
        compiler_params=LIMIT,
        name="finish",
    )(device, atoms, cotangent, own_grad, first, second, sent)
    part, atoms_grad, band_grad = lax.optimization_barrier((part, atoms_grad, band_grad))
    project_grad, combine_grad, weight_grad, scale_grad, gain_grad = pl.pallas_call(
        last_kernel,
        out_shape=(
            shape(project.shape, BF),
            shape(combine.shape, BF),
            shape(weights.shape, BF),
            shape((1, width), F32),
            shape((1, width), F32),
        ),
        in_specs=vmem(3),
        out_specs=tuple(vmem(5)),
        compiler_params=LIMIT,
        name="last",
    )(part, project, sent)
    return (
        atoms_grad,
        project_grad,
        combine_grad,
        scale_grad.reshape(width),
        band_grad,
        weight_grad.T,
        gain_grad.reshape(width),
    )


def solution(mesh):
    in_specs = (
        P(None, ("row", "col"), None),
        P(None, ("row", "col"), None),
        P(),
        P(),
        P(),
        P("row", "col", None),
        P(),
        P(),
        P(("row", "col")),
        P(("row", "col"), None),
    )
    out_specs = (P(None, ("row", "col"), None), P(), P(), P(), P("row", "col", None), P(), P())
    return jax.shard_map(shards, mesh=mesh, in_specs=in_specs, out_specs=out_specs, check_vma=False)
```
